512 devices in a mesh: psg: 64 (over z, y), pb: 4 (over x), rep: 2 (over core).
Axes of the slice: x: 4, y: 8, z: 8, core: 2. Of those that a mesh axis runs over, the one named last changes fastest.
Arguments:
- queries: bfloat16 [512, 2048], P(None, ('pb', 'rep'))
- prefixes: bfloat16 [2048, 32, 2048], P('psg', None, ('pb', 'rep')), may hold values from -6 to 6
- owner: int32 [2048], P('psg'), may hold values from 0 to 16, as said below
- key_weight: bfloat16 [2048, 2048], P(None, ('pb', 'rep')), may hold values from -0.125 to 0.125
- value_weight: bfloat16 [2048, 2048], P(None, ('pb', 'rep')), may hold values from -0.125 to 0.125
- cotangent: bfloat16 [512, 2048], P(None, ('pb', 'rep')), may hold values from -6 to 6
Outputs:
- attended: bfloat16 [512, 2048], P(None, ('pb', 'rep'))
- query_grad: bfloat16 [512, 2048], P(None, ('pb', 'rep'))
The draws below stay inside these ranges and needn't reach their ends.
Inputs may be any that keep to these rules, and one draw needn't show every extreme that they name: owner[j] is the question of slot j; the value 16 marks an empty slot. Slots 0 to 15 hold every question once, the last slot is empty, and the other slots follow a skewed law over the questions.
All inputs are finite; a program needn't handle non-finite values.
Results may differ from the reference program's by a relative error of at most 0.025.
The reference program's roundings to bfloat16 on the way count: a program that leaves them out, or rounds other values in their place, can miss the bound.
Values may be sent and summed in bfloat16 or wider, within the bound.
No kernel may reach another device: no remote copies, remote signals or barrier semaphores. Data moves between devices by JAX's collectives and lax.ppermute only.
A program may use at most 64 MiB of HBM per device.

```python
import jax
import jax.numpy as jnp
from jax import lax

D = 2048
HEADS = 32
HDIM = 64
PL = 32
TGT = 32
QUESTIONS = 16
ROWS = 512
SLOTS = 2048


def draw_queries(key, part):
    key = jax.random.fold_in(key, 11)
    first_key = jax.random.fold_in(key, 0)
    base = jax.random.normal(first_key, (ROWS, D), jnp.float32) * 0.2
    return base.astype(jnp.bfloat16)


def draw_owner(key, part):
    key = jax.random.fold_in(key, 23)
    first_key, second_key, third_key, fourth_key = jax.random.split(key, 4)
    choice_span = QUESTIONS + QUESTIONS // 4 + 1
    first_pick = jax.random.randint(first_key, (SLOTS,), 0, choice_span)
    second_pick = jax.random.randint(second_key, (SLOTS,), 0, choice_span)
    ranking = jnp.minimum(first_pick, second_pick)
    question_order = jax.random.permutation(third_key, QUESTIONS)
    picked = jnp.where(ranking < QUESTIONS, jnp.take(question_order, jnp.minimum(ranking, QUESTIONS - 1)), QUESTIONS)
    picked = picked.at[:QUESTIONS].set(jax.random.permutation(fourth_key, QUESTIONS))
    picked = picked.at[SLOTS - 1].set(QUESTIONS)
    return picked.astype(jnp.int32)


def levels(own_key, extent, pieces, low, top_value):
    def one(position, parts):
        draws = jax.random.uniform(jax.random.fold_in(jax.random.fold_in(own_key, 6), position), (parts,), jnp.float32, low / len(pieces), top_value / len(pieces))
        return jnp.repeat(jnp.exp(draws), extent[position] // parts).reshape((-1,) + (1,) * (len(extent) - position - 1))

    loudness = one(*pieces[0])
    for cut in pieces[1:]:
        loudness = loudness * one(*cut)
    return loudness


def bell_draw(own_key, dims, deviation, reach, pieces=(), held_as=jnp.bfloat16):
    loudness = levels(own_key, dims, pieces, -0.22, 0.18) if pieces else 1.0
    array = jax.random.normal(own_key, dims, jnp.float32) * deviation * loudness
    return jnp.minimum(jnp.maximum(array, -reach), reach).astype(held_as)


def setup_inputs(seed: int = 0) -> dict:
    keys = jax.random.split(jax.random.key(seed), 7)
    queries = draw_queries(jax.random.fold_in(keys[6], 71), 0)
    prefixes = bell_draw(keys[1], (SLOTS, PL, D), 1.0, 6.0, ((0, 64), (2, 8)))
    owner = draw_owner(jax.random.fold_in(keys[6], 71), 0)
    key_weight = bell_draw(keys[3], (D, D), D ** -0.5, 0.125, ((1, 8),))
    value_weight = bell_draw(keys[4], (D, D), D ** -0.5, 0.125, ((1, 8),))
    cotangent = bell_draw(keys[5], (ROWS, D), 1.0, 6.0, ((1, 8),))
    return {"queries": queries, "prefixes": prefixes, "owner": owner, "key_weight": key_weight, "value_weight": value_weight, "cotangent": cotangent}


masked_value = -1.0e30


def reference(queries, prefixes, owner, key_weight, value_weight, cotangent):
    passage_rows = prefixes.reshape(SLOTS * PL, D)
    key_rows = jnp.dot(passage_rows, key_weight, preferred_element_type=jnp.float32).astype(jnp.bfloat16)
    value_rows = jnp.dot(passage_rows, value_weight, preferred_element_type=jnp.float32).astype(jnp.bfloat16)
    key_owner = jnp.repeat(owner, PL)
    row_owner = jnp.arange(QUESTIONS * TGT, dtype=jnp.int32) // TGT
    counted = row_owner[:, None] == key_owner[None, :]

    def one_head(head_index):
        offset = head_index * HDIM
        query_head = lax.dynamic_slice_in_dim(queries, offset, HDIM, 1)
        key_head = lax.dynamic_slice_in_dim(key_rows, offset, HDIM, 1)
        value_head = lax.dynamic_slice_in_dim(value_rows, offset, HDIM, 1)
        grad_head = lax.dynamic_slice_in_dim(cotangent, offset, HDIM, 1)
        scores = jnp.dot(query_head, key_head.T, preferred_element_type=jnp.float32)
        scores = jnp.where(counted, scores, masked_value)
        row_max = jnp.max(scores, axis=1, keepdims=True)
        exponent = jnp.where(counted, jnp.exp(scores - row_max), jnp.float32(0.0))
        totals = jnp.sum(exponent, axis=1, keepdims=True)
        summed = jnp.dot(exponent.astype(jnp.bfloat16), value_head, preferred_element_type=jnp.float32)
        attended = (summed / totals).astype(jnp.bfloat16)
        correction = jnp.sum(grad_head.astype(jnp.float32) * attended.astype(jnp.float32), axis=1, keepdims=True)
        product = jnp.dot(grad_head, value_head.T, preferred_element_type=jnp.float32)
        grad_scores = (exponent / totals * (product - correction)).astype(jnp.bfloat16)
        query_grad = jnp.dot(grad_scores, key_head, preferred_element_type=jnp.float32).astype(jnp.bfloat16)
        return attended, query_grad

    head_ids = jnp.arange(HEADS, dtype=jnp.int32)
    attended, query_grad = lax.map(one_head, head_ids)
    attended = jnp.transpose(attended, (1, 0, 2)).reshape(QUESTIONS * TGT, D)
    query_grad = jnp.transpose(query_grad, (1, 0, 2)).reshape(QUESTIONS * TGT, D)
    return attended, query_grad
```

```python
import jax
import jax.numpy as jnp
from jax import lax
from jax.experimental import pallas as pl
from jax.experimental.pallas import tpu as pltpu
from jax.sharding import PartitionSpec as P

HDIM = 64
TGT = 32
PL = 32
QUESTIONS = 16
PARTS = 3

masked_value = -1e30

f32 = jnp.float32
bf16 = jnp.bfloat16
NT = (((1,), (1,)), ((), ()))


def split_parts(x):
    first = x.astype(bf16)
    rest = x - first.astype(f32)
    second = rest.astype(bf16)
    third = (rest - second.astype(f32)).astype(bf16)
    return first.astype(f32), second.astype(f32), third.astype(f32)


def per_head(x, width, reduce, fill):
    lane_head = lax.broadcasted_iota(jnp.int32, x.shape, x.ndim - 1) // width
    out = jnp.zeros_like(x)
    for head in range(x.shape[-1] // width):
        one = reduce(jnp.where(lane_head == head, x, fill), axis=-1, keepdims=True)
        out = jnp.where(lane_head == head, one, out)
    return out


def local_kernel(pieces, *refs):
    block_ref, owner_ref = refs[:2]
    x_refs = refs[2 : 2 + pieces]
    (wk_ref, wv_ref, q_ref, c_ref, out_ref, kblk, vblk, score, product, top, total, dots, corr, acc_v, acc_k) = refs[
        2 + pieces :
    ]
    slots = owner_ref.shape[0]
    half = slots // 2
    heads = q_ref.shape[1] // HDIM
    keys = heads * PL

    top[...] = jnp.full_like(top, masked_value)
    total[...] = jnp.zeros_like(total)
    dots[...] = jnp.zeros_like(dots)
    acc_v[...] = jnp.zeros_like(acc_v)
    acc_k[...] = jnp.zeros_like(acc_k)

    blocks = 8
    wide = wk_ref.shape[0] // blocks

    def weight(ref):
        rows = [ref[pl.ds(pl.multiple_of(block_ref[j] * wide, wide), wide), :] for j in range(blocks)]
        return jnp.concatenate(rows, axis=0)

    on_diagonal = (
        lax.broadcasted_iota(jnp.int32, (keys, heads * HDIM), 0) // PL
        == lax.broadcasted_iota(jnp.int32, (keys, heads * HDIM), 1) // HDIM
    ).astype(f32).astype(bf16)

    group = 8
    for start in range(0, slots, group):
        side = 0 if start < half else 1
        low = (start - side * half) * PL
        rows = jnp.concatenate([x_refs[j * 2 + side][low : low + group * PL, :] for j in range(blocks)], axis=1)
        key_rows = jnp.dot(rows, weight(wk_ref), preferred_element_type=f32).astype(bf16)
        value_rows = jnp.dot(rows, weight(wv_ref), preferred_element_type=f32).astype(bf16)
        for i in range(group):
            slot = start + i
            kb = jnp.concatenate([key_rows[i * PL : (i + 1) * PL]] * heads, axis=0) * on_diagonal
            vb = jnp.concatenate([value_rows[i * PL : (i + 1) * PL]] * heads, axis=0) * on_diagonal
            kblk[slot] = kb
            vblk[slot] = vb
            o = owner_ref[slot]
            at = pl.ds(pl.multiple_of(jnp.minimum(o, QUESTIONS - 1) * TGT, TGT), TGT)
            s = lax.dot_general(q_ref[at, :], kb, NT, preferred_element_type=f32)
            score[slot] = s
            product[slot] = lax.dot_general(c_ref[at, :], vb, NT, preferred_element_type=f32)
            top[o] = jnp.maximum(top[o], s)

    for q in range(QUESTIONS):
        top[q] = per_head(top[q], PL, jnp.max, masked_value)

    for slot in range(slots):
        o = owner_ref[slot]
        e = jnp.exp(score[slot] - top[o])
        score[slot] = e
        total[o] = total[o] + e
        dots[o] = dots[o] + e * product[slot]

    for q in range(QUESTIONS):
        t = per_head(total[q], PL, jnp.sum, 0.0)
        d = per_head(dots[q], PL, jnp.sum, 0.0)
        total[q] = t
        corr[q] = jnp.where(t > 0.0, d / jnp.where(t > 0.0, t, 1.0), 0.0)
    corr[QUESTIONS] = jnp.zeros_like(corr[QUESTIONS])

    for slot in range(slots):
        o = owner_ref[slot]
        e = score[slot]
        g = e * (product[slot] - corr[o])
        both = jnp.concatenate([e, g], axis=0).astype(bf16)
        acc_v[o] = acc_v[o] + jnp.dot(both[:TGT], vblk[slot], preferred_element_type=f32)
        acc_k[o] = acc_k[o] + jnp.dot(both, kblk[slot], preferred_element_type=f32)

    cols = heads * HDIM
    part = lax.broadcasted_iota(jnp.int32, (TGT, keys), 1) % PL
    for q in range(QUESTIONS):
        at = slice(q * TGT, (q + 1) * TGT)
        out_ref[at, 0:cols] = acc_v[q].astype(bf16)
        out_ref[at, cols : 2 * cols] = acc_k[q, TGT:, :].astype(bf16)
        out_ref[at, 2 * cols : 3 * cols] = acc_k[q, :TGT, :].astype(bf16)
        extra = jnp.zeros((TGT, keys), f32)
        pieces_of = split_parts(top[q]) + split_parts(total[q]) + split_parts(corr[q])
        for n, piece in enumerate(pieces_of):
            extra = jnp.where(part == n, piece, extra)
        out_ref[at, 3 * cols :] = extra.astype(bf16)


def final_kernel(r_ref, c_ref, out_ref):
    rows, cols = c_ref.shape
    heads = cols // HDIM
    keys = heads * PL
    devices = r_ref.shape[0] // rows
    lane = lax.broadcasted_iota(jnp.int32, (keys, 3 * cols), 0)
    spot = lax.broadcasted_iota(jnp.int32, (keys, 3 * cols), 1)
    pick = (lane // PL == (spot % cols) // HDIM) & ((lane % PL) // PARTS == spot // cols)
    pick = pick.astype(f32).astype(bf16)
    wide = jnp.dot(r_ref[:, 3 * cols :], pick, preferred_element_type=f32).reshape(devices, rows, 3 * cols)
    top = wide[:, :, 0:cols]
    weight = jnp.exp(top - jnp.max(top, axis=0, keepdims=True))
    total = jnp.sum(weight * wide[:, :, cols : 2 * cols], axis=0)

    def read(n):
        return r_ref[:, n * cols : (n + 1) * cols].astype(f32).reshape(devices, rows, cols)

    summed = jnp.sum(weight * read(0), axis=0)
    attended = (summed / total).astype(bf16).astype(f32)
    corr = per_head(c_ref[...] * attended, HDIM, jnp.sum, 0.0)
    shift = wide[:, :, 2 * cols :] - corr[None]
    grad = jnp.sum(weight * (read(1) + shift * read(2)), axis=0) / total
    both = jnp.concatenate([attended, grad], axis=1)
    two = jnp.concatenate([both, both], axis=0).astype(bf16)
    for n in range(devices // 2):
        out_ref[2 * rows * n : 2 * rows * (n + 1), :] = two


def gather(x):
    n = lax.axis_size("pb")
    right = [(i, (i + 1) % n) for i in range(n)]
    left = [(i, (i - 1) % n) for i in range(n)]
    swap = [(0, 1), (1, 0)]
    half = x.shape[0] // 2
    a, b = x[:half], x[half:]
    left_a = lax.ppermute(a, "pb", right)
    right_b = lax.ppermute(b, "pb", left)
    left_b = lax.ppermute(b, "pb", right)
    right_a = lax.ppermute(a, "pb", left)
    far_a = lax.ppermute(left_a, "pb", right)
    far_b = lax.ppermute(right_b, "pb", left)
    pb, rep = lax.axis_index("pb"), lax.axis_index("rep")
    out = []
    for shift, first, second in ((0, a, b), (n - 1, left_a, left_b), (1, right_a, right_b), (2, far_a, far_b)):
        place = (pb + shift) % n
        out.append((place * 2 + rep, first, second))
        out.append((place * 2 + 1 - rep, lax.ppermute(first, "rep", swap), lax.ppermute(second, "rep", swap)))
    return out


def body(queries, prefixes, owner, key_weight, value_weight, cotangent):
    slots, vectors, features = prefixes.shape
    rows, cols = queries.shape
    heads = cols // HDIM
    keys = heads * PL
    devices = lax.axis_size("psg")
    own = rows // devices

    parts = gather(prefixes.reshape(slots * vectors, features))
    block = jnp.stack([p[0] for p in parts]).astype(jnp.int32)
    pieces = [p for part in parts for p in part[1:]]
    smem = pl.BlockSpec(memory_space=pltpu.SMEM)
    vmem = pl.BlockSpec(memory_space=pltpu.VMEM)
    payload = pl.pallas_call(
        lambda *refs: local_kernel(len(pieces), *refs),
        out_shape=jax.ShapeDtypeStruct((rows, 3 * cols + keys), bf16),
        in_specs=[smem, smem] + [vmem] * (len(pieces) + 4),
        out_specs=vmem,
        scratch_shapes=[
            pltpu.VMEM((slots, keys, cols), bf16),
            pltpu.VMEM((slots, keys, cols), bf16),
            pltpu.VMEM((slots, TGT, keys), f32),
            pltpu.VMEM((slots, TGT, keys), f32),
            pltpu.VMEM((QUESTIONS + 1, TGT, keys), f32),
            pltpu.VMEM((QUESTIONS + 1, TGT, keys), f32),
            pltpu.VMEM((QUESTIONS + 1, TGT, keys), f32),
            pltpu.VMEM((QUESTIONS + 1, TGT, keys), f32),
            pltpu.VMEM((QUESTIONS + 1, TGT, cols), f32),
            pltpu.VMEM((QUESTIONS + 1, 2 * TGT, cols), f32),
        ],
        compiler_params=pltpu.CompilerParams(vmem_limit_bytes=48 * 1024 * 1024),
        name="local_sums",
    )(block, owner, *pieces, key_weight, value_weight, queries, cotangent)

    received = lax.all_to_all(payload, "psg", 0, 0, tiled=True)
    own_cotangent = lax.dynamic_slice_in_dim(cotangent, lax.axis_index("psg") * own, own, 0).astype(f32)
    finished = pl.pallas_call(
        final_kernel,
        out_shape=jax.ShapeDtypeStruct((rows, 2 * cols), bf16),
        in_specs=[vmem, vmem],
        out_specs=vmem,
        compiler_params=pltpu.CompilerParams(vmem_limit_bytes=48 * 1024 * 1024),
        name="final_sums",
    )(received, own_cotangent)
    outputs = lax.all_to_all(finished, "psg", 0, 0, tiled=True)
    return outputs[:, :cols], outputs[:, cols:]


def solution(mesh):
    placed = (
        P(None, ("pb", "rep")),
        P("psg", None, ("pb", "rep")),
        P("psg"),
        P(None, ("pb", "rep")),
        P(None, ("pb", "rep")),
        P(None, ("pb", "rep")),
    )
    return jax.shard_map(
        body,
        mesh=mesh,
        in_specs=placed,
        out_specs=(P(None, ("pb", "rep")), P(None, ("pb", "rep"))),
        check_vma=False,
    )
```

```python
import jax
import jax.numpy as jnp
from jax import lax
from jax.experimental import pallas as pl
from jax.experimental.pallas import tpu as pltpu
from jax.sharding import PartitionSpec as P

HDIM = 64
TGT = 32
PL = 32
QUESTIONS = 16
PARTS = 3

masked_value = -1e30

f32 = jnp.float32
bf16 = jnp.bfloat16
NT = (((1,), (1,)), ((), ()))


def split_parts(x):
    first = x.astype(bf16)
    rest = x - first.astype(f32)
    second = rest.astype(bf16)
    third = (rest - second.astype(f32)).astype(bf16)
    return first.astype(f32), second.astype(f32), third.astype(f32)


def per_head(x, width, reduce, fill):
    lane_head = lax.broadcasted_iota(jnp.int32, x.shape, x.ndim - 1) // width
    out = jnp.zeros_like(x)
    for head in range(x.shape[-1] // width):
        one = reduce(jnp.where(lane_head == head, x, fill), axis=-1, keepdims=True)
        out = jnp.where(lane_head == head, one, out)
    return out


def own_kernel(block_ref, x_ref, wk_ref, wv_ref, acc_ref, rest_ref):
    wide = x_ref.shape[1]
    cols = wk_ref.shape[1]
    for n in range(wk_ref.shape[0] // wide):
        at = pl.ds(pl.multiple_of(block_ref[n] * wide, wide), wide)
        for side, ref in enumerate((wk_ref, wv_ref)):
            columns = slice(side * cols, (side + 1) * cols)
            if n == 0:
                acc_ref[:, columns] = jnp.dot(x_ref[...], ref[at, :], preferred_element_type=f32)
            else:
                rest_ref[(n - 1) * wide : n * wide, columns] = ref[at, :]


def near_kernel(acc_ref, rest_ref, *refs):
    x_refs, out_ref = refs[:-1], refs[-1]
    weight = rest_ref[0 : len(x_refs) * x_refs[0].shape[1], :]
    chunk = 512
    for low in range(0, acc_ref.shape[0], chunk):
        rows = jnp.concatenate([x[low : low + chunk, :] for x in x_refs], axis=1)
        out_ref[low : low + chunk, :] = acc_ref[low : low + chunk, :] + jnp.dot(
            rows, weight, preferred_element_type=f32
        )


def local_kernel(owner_ref, acc_ref, *refs):
    (far_ref, rest_ref, q_ref, c_ref, out_ref, kblk, vblk, score, product, top, total, dots, corr, acc_v, acc_k) = refs
    slots = owner_ref.shape[0]
    half = slots // 2
    cols = q_ref.shape[1]
    heads = cols // HDIM
    keys = heads * PL

    top[...] = jnp.full_like(top, masked_value)
    total[...] = jnp.zeros_like(total)
    dots[...] = jnp.zeros_like(dots)
    acc_v[...] = jnp.zeros_like(acc_v)
    acc_k[...] = jnp.zeros_like(acc_k)

    on_diagonal = (
        lax.broadcasted_iota(jnp.int32, (keys, cols), 0) // PL
        == lax.broadcasted_iota(jnp.int32, (keys, cols), 1) // HDIM
    ).astype(f32).astype(bf16)

    for side in range(2):
        low = side * half * PL
        rows = far_ref[low : low + half * PL, :]
        projected = acc_ref[low : low + half * PL, :] + jnp.dot(
            rows, rest_ref[-rows.shape[1] :, :], preferred_element_type=f32
        )
        projected = projected.astype(bf16)
        for i in range(half):
            slot = side * half + i
            own = projected[i * PL : (i + 1) * PL]
            kb = jnp.concatenate([own[:, :cols]] * heads, axis=0) * on_diagonal
            vb = jnp.concatenate([own[:, cols:]] * heads, axis=0) * on_diagonal
            kblk[slot] = kb
            vblk[slot] = vb
            o = owner_ref[slot]
            at = pl.ds(pl.multiple_of(jnp.minimum(o, QUESTIONS - 1) * TGT, TGT), TGT)
            s = lax.dot_general(q_ref[at, :], kb, NT, preferred_element_type=f32)
            score[slot] = s
            product[slot] = lax.dot_general(c_ref[at, :], vb, NT, preferred_element_type=f32)
            top[o] = jnp.maximum(top[o], s)

    for q in range(QUESTIONS):
        top[q] = per_head(top[q], PL, jnp.max, masked_value)

    for slot in range(slots):
        o = owner_ref[slot]
        e = jnp.exp(score[slot] - top[o])
        score[slot] = e
        total[o] = total[o] + e
        dots[o] = dots[o] + e * product[slot]

    for q in range(QUESTIONS):
        t = per_head(total[q], PL, jnp.sum, 0.0)
        d = per_head(dots[q], PL, jnp.sum, 0.0)
        total[q] = t
        corr[q] = jnp.where(t > 0.0, d / jnp.where(t > 0.0, t, 1.0), 0.0)
    corr[QUESTIONS] = jnp.zeros_like(corr[QUESTIONS])

    for slot in range(slots):
        o = owner_ref[slot]
        e = score[slot]
        g = e * (product[slot] - corr[o])
        both = jnp.concatenate([e, g], axis=0).astype(bf16)
        acc_v[o] = acc_v[o] + jnp.dot(both[:TGT], vblk[slot], preferred_element_type=f32)
        acc_k[o] = acc_k[o] + jnp.dot(both, kblk[slot], preferred_element_type=f32)

    part = lax.broadcasted_iota(jnp.int32, (TGT, keys), 1) % PL
    for q in range(QUESTIONS):
        at = slice(q * TGT, (q + 1) * TGT)
        out_ref[at, 0:cols] = acc_v[q].astype(bf16)
        out_ref[at, cols : 2 * cols] = acc_k[q, TGT:, :].astype(bf16)
        out_ref[at, 2 * cols : 3 * cols] = acc_k[q, :TGT, :].astype(bf16)
        extra = jnp.zeros((TGT, keys), f32)
        pieces_of = split_parts(top[q]) + split_parts(total[q]) + split_parts(corr[q])
        for n, piece in enumerate(pieces_of):
            extra = jnp.where(part == n, piece, extra)
        out_ref[at, 3 * cols :] = extra.astype(bf16)


def final_kernel(r_ref, c_ref, out_ref):
    rows, cols = c_ref.shape
    heads = cols // HDIM
    keys = heads * PL
    devices = r_ref.shape[0] // rows
    lane = lax.broadcasted_iota(jnp.int32, (keys, 3 * cols), 0)
    spot = lax.broadcasted_iota(jnp.int32, (keys, 3 * cols), 1)
    pick = (lane // PL == (spot % cols) // HDIM) & ((lane % PL) // PARTS == spot // cols)
    pick = pick.astype(f32).astype(bf16)
    wide = jnp.dot(r_ref[:, 3 * cols :], pick, preferred_element_type=f32).reshape(devices, rows, 3 * cols)
    top = wide[:, :, 0:cols]
    weight = jnp.exp(top - jnp.max(top, axis=0, keepdims=True))
    total = jnp.sum(weight * wide[:, :, cols : 2 * cols], axis=0)

    def read(n):
        return r_ref[:, n * cols : (n + 1) * cols].astype(f32).reshape(devices, rows, cols)

    summed = jnp.sum(weight * read(0), axis=0)
    attended = (summed / total).astype(bf16).astype(f32)
    corr = per_head(c_ref[...] * attended, HDIM, jnp.sum, 0.0)
    shift = wide[:, :, 2 * cols :] - corr[None]
    grad = jnp.sum(weight * (read(1) + shift * read(2)), axis=0) / total
    both = jnp.concatenate([attended, grad], axis=1)
    two = jnp.concatenate([both, both], axis=0).astype(bf16)
    for n in range(devices // 2):
        out_ref[2 * rows * n : 2 * rows * (n + 1), :] = two


def swap(block):
    return lax.ppermute(block, "rep", [(0, 1), (1, 0)])


def block_numbers():
    n = lax.axis_size("pb")
    pb, rep = lax.axis_index("pb"), lax.axis_index("rep")
    places = [(pb + shift) % n for shift in (0, n - 1, 1, 2)]
    numbers = [number for place in places for number in (place * 2 + rep, place * 2 + 1 - rep)]
    return jnp.stack(numbers).astype(jnp.int32)


def body(queries, prefixes, owner, key_weight, value_weight, cotangent):
    slots, vectors, features = prefixes.shape
    rows, cols = queries.shape
    heads = cols // HDIM
    keys = heads * PL
    devices = lax.axis_size("psg")
    own = rows // devices

    passages = prefixes.reshape(slots * vectors, features)
    n = lax.axis_size("pb")
    left, right, far = (
        lax.ppermute(passages, "pb", [(i, (i + shift) % n) for i in range(n)]) for shift in (1, n - 1, 2)
    )
    other = swap(passages)
    smem = pl.BlockSpec(memory_space=pltpu.SMEM)
    vmem = pl.BlockSpec(memory_space=pltpu.VMEM)
    sums = jax.ShapeDtypeStruct((slots * vectors, 2 * cols), f32)
    projected, rest = pl.pallas_call(
        own_kernel,
        out_shape=(sums, jax.ShapeDtypeStruct((key_weight.shape[0] - features, 2 * cols), bf16)),
        in_specs=[smem] + [vmem] * 3,
        out_specs=(vmem, vmem),
        compiler_params=pltpu.CompilerParams(vmem_limit_bytes=16 * 1024 * 1024),
        name="own_projection",
    )(block_numbers(), passages, key_weight, value_weight)
    left, projected, rest = lax.optimization_barrier((left, projected, rest))
    near = [other, left, swap(left), right, swap(right), far]
    far = swap(far)
    projected = pl.pallas_call(
        near_kernel,
        out_shape=sums,
        in_specs=[vmem] * (2 + len(near)),
        out_specs=vmem,
        compiler_params=pltpu.CompilerParams(vmem_limit_bytes=16 * 1024 * 1024),
        name="near_projection",
    )(projected, rest, *near)
    payload = pl.pallas_call(
        local_kernel,
        out_shape=jax.ShapeDtypeStruct((rows, 3 * cols + keys), bf16),
        in_specs=[smem] + [vmem] * 5,
        out_specs=vmem,
        scratch_shapes=[
            pltpu.VMEM((slots, keys, cols), bf16),
            pltpu.VMEM((slots, keys, cols), bf16),
            pltpu.VMEM((slots, TGT, keys), f32),
            pltpu.VMEM((slots, TGT, keys), f32),
            pltpu.VMEM((QUESTIONS + 1, TGT, keys), f32),
            pltpu.VMEM((QUESTIONS + 1, TGT, keys), f32),
            pltpu.VMEM((QUESTIONS + 1, TGT, keys), f32),
            pltpu.VMEM((QUESTIONS + 1, TGT, keys), f32),
            pltpu.VMEM((QUESTIONS + 1, TGT, cols), f32),
            pltpu.VMEM((QUESTIONS + 1, 2 * TGT, cols), f32),
        ],
        compiler_params=pltpu.CompilerParams(vmem_limit_bytes=24 * 1024 * 1024),
        name="local_sums",
    )(owner, projected, far, rest, queries, cotangent)

    received = lax.all_to_all(payload, "psg", 0, 0, tiled=True)
    own_cotangent = lax.dynamic_slice_in_dim(cotangent, lax.axis_index("psg") * own, own, 0).astype(f32)
    finished = pl.pallas_call(
        final_kernel,
        out_shape=jax.ShapeDtypeStruct((rows, 2 * cols), bf16),
        in_specs=[vmem, vmem],
        out_specs=vmem,
        compiler_params=pltpu.CompilerParams(vmem_limit_bytes=24 * 1024 * 1024),
        name="final_sums",
    )(received, own_cotangent)
    outputs = lax.all_to_all(finished, "psg", 0, 0, tiled=True)
    return outputs[:, :cols], outputs[:, cols:]


def solution(mesh):
    placed = (
        P(None, ("pb", "rep")),
        P("psg", None, ("pb", "rep")),
        P("psg"),
        P(None, ("pb", "rep")),
        P(None, ("pb", "rep")),
        P(None, ("pb", "rep")),
    )
    return jax.shard_map(
        body,
        mesh=mesh,
        in_specs=placed,
        out_specs=(P(None, ("pb", "rep")), P(None, ("pb", "rep"))),
        check_vma=False,
    )
```

```python
import jax
import jax.numpy as jnp
import numpy as np
from jax import lax
from jax.experimental import pallas as pl
from jax.experimental.pallas import tpu as pltpu
from jax.sharding import PartitionSpec as P

HDIM = 64
TGT = 32
PL = 32
QUESTIONS = 16
PARTS = 3
SIDE = 8

masked_value = -1e30

f32 = jnp.float32
bf16 = jnp.bfloat16
NT = (((1,), (1,)), ((), ()))


def split_parts(x):
    first = x.astype(bf16)
    rest = x - first.astype(f32)
    second = rest.astype(bf16)
    third = (rest - second.astype(f32)).astype(bf16)
    return first.astype(f32), second.astype(f32), third.astype(f32)


def per_head(x, width, reduce, fill):
    lane_head = lax.broadcasted_iota(jnp.int32, x.shape, x.ndim - 1) // width
    out = jnp.zeros_like(x)
    for head in range(x.shape[-1] // width):
        one = reduce(jnp.where(lane_head == head, x, fill), axis=-1, keepdims=True)
        out = jnp.where(lane_head == head, one, out)
    return out


def own_kernel(block_ref, x_ref, wk_ref, wv_ref, acc_ref, rest_ref):
    wide = x_ref.shape[1]
    cols = wk_ref.shape[1]
    for n in range(wk_ref.shape[0] // wide):
        at = pl.ds(pl.multiple_of(block_ref[n] * wide, wide), wide)
        for side, ref in enumerate((wk_ref, wv_ref)):
            columns = slice(side * cols, (side + 1) * cols)
            if n == 0:
                acc_ref[:, columns] = jnp.dot(x_ref[...], ref[at, :], preferred_element_type=f32)
            else:
                rest_ref[(n - 1) * wide : n * wide, columns] = ref[at, :]


def near_kernel(acc_ref, rest_ref, *refs):
    x_refs, out_ref = refs[:-1], refs[-1]
    weight = rest_ref[0 : len(x_refs) * x_refs[0].shape[1], :]
    chunk = 512
    for low in range(0, acc_ref.shape[0], chunk):
        rows = jnp.concatenate([x[low : low + chunk, :] for x in x_refs], axis=1)
        out_ref[low : low + chunk, :] = acc_ref[low : low + chunk, :] + jnp.dot(
            rows, weight, preferred_element_type=f32
        )


def local_kernel(owner_ref, acc_ref, *refs):
    (far_ref, rest_ref, q_ref, c_ref, out_ref, kblk, vblk, score, product, top, total, dots, corr, acc_v, acc_k) = refs
    slots = owner_ref.shape[0]
    half = slots // 2
    cols = q_ref.shape[1]
    heads = cols // HDIM
    keys = heads * PL

    top[...] = jnp.full_like(top, masked_value)
    total[...] = jnp.zeros_like(total)
    dots[...] = jnp.zeros_like(dots)
    acc_v[...] = jnp.zeros_like(acc_v)
    acc_k[...] = jnp.zeros_like(acc_k)

    on_diagonal = (
        lax.broadcasted_iota(jnp.int32, (keys, cols), 0) // PL
        == lax.broadcasted_iota(jnp.int32, (keys, cols), 1) // HDIM
    ).astype(f32).astype(bf16)

    for side in range(2):
        low = side * half * PL
        rows = far_ref[low : low + half * PL, :]
        projected = acc_ref[low : low + half * PL, :] + jnp.dot(
            rows, rest_ref[-rows.shape[1] :, :], preferred_element_type=f32
        )
        projected = projected.astype(bf16)
        for i in range(half):
            slot = side * half + i
            own = projected[i * PL : (i + 1) * PL]
            kb = jnp.concatenate([own[:, :cols]] * heads, axis=0) * on_diagonal
            vb = jnp.concatenate([own[:, cols:]] * heads, axis=0) * on_diagonal
            kblk[slot] = kb
            vblk[slot] = vb
            o = owner_ref[slot]
            at = pl.ds(pl.multiple_of(jnp.minimum(o, QUESTIONS - 1) * TGT, TGT), TGT)
            s = lax.dot_general(q_ref[at, :], kb, NT, preferred_element_type=f32)
            score[slot] = s
            product[slot] = lax.dot_general(c_ref[at, :], vb, NT, preferred_element_type=f32)
            top[o] = jnp.maximum(top[o], s)

    for q in range(QUESTIONS):
        top[q] = per_head(top[q], PL, jnp.max, masked_value)

    for slot in range(slots):
        o = owner_ref[slot]
        e = jnp.exp(score[slot] - top[o])
        score[slot] = e
        total[o] = total[o] + e
        dots[o] = dots[o] + e * product[slot]

    for q in range(QUESTIONS):
        t = per_head(total[q], PL, jnp.sum, 0.0)
        d = per_head(dots[q], PL, jnp.sum, 0.0)
        total[q] = t
        corr[q] = jnp.where(t > 0.0, d / jnp.where(t > 0.0, t, 1.0), 0.0)
    corr[QUESTIONS] = jnp.zeros_like(corr[QUESTIONS])

    for slot in range(slots):
        o = owner_ref[slot]
        e = score[slot]
        g = e * (product[slot] - corr[o])
        both = jnp.concatenate([e, g], axis=0).astype(bf16)
        acc_v[o] = acc_v[o] + jnp.dot(both[:TGT], vblk[slot], preferred_element_type=f32)
        acc_k[o] = acc_k[o] + jnp.dot(both, kblk[slot], preferred_element_type=f32)

    for q in range(QUESTIONS):
        at = slice(q * TGT, (q + 1) * TGT)
        out_ref[at, 0:cols] = acc_v[q].astype(bf16)
        out_ref[at, cols : 2 * cols] = acc_k[q, TGT:, :].astype(bf16)
        out_ref[at, 2 * cols : 3 * cols] = acc_k[q, :TGT, :].astype(bf16)
        out_ref[at, 3 * cols :] = pack((top[q], total[q], corr[q]))


def spread(extra, cols):
    keys = extra.shape[1]
    heads = keys // PL
    lane = lax.broadcasted_iota(jnp.int32, (keys, 3 * cols), 0)
    spot = lax.broadcasted_iota(jnp.int32, (keys, 3 * cols), 1)
    pick = (lane // PL == (spot % cols) // (cols // heads)) & ((lane % PL) // PARTS == spot // cols)
    wide = jnp.dot(extra, pick.astype(f32).astype(bf16), preferred_element_type=f32)
    return [wide[:, n * cols : (n + 1) * cols] for n in range(3)]


def pack(values):
    part = lax.broadcasted_iota(jnp.int32, values[0].shape, 1) % PL
    out = jnp.zeros_like(values[0])
    for n, piece in enumerate([piece for value in values for piece in split_parts(value)]):
        out = jnp.where(part == n, piece, out)
    return out.astype(bf16)


def merge(extra, cols, rows):
    top, total, corr = [x.reshape(-1, rows, cols) for x in spread(extra, cols)]
    high = jnp.max(top, axis=0)
    scale = jnp.exp(top - high[None])
    sums = jnp.sum(scale * total, axis=0)
    dots = jnp.sum(scale * total * corr, axis=0)
    mean = jnp.where(sums > 0.0, dots / jnp.where(sums > 0.0, sums, 1.0), 0.0)
    return scale, corr, high, sums, mean


def merge_kernel(r_ref, out_ref):
    rows = out_ref.shape[0]
    keys = r_ref.shape[1] % 256
    cols = (r_ref.shape[1] - keys) // 3
    extra = r_ref[:, 3 * cols :]

    def read(n):
        return r_ref[:, n * cols : (n + 1) * cols].astype(f32).reshape(-1, rows, cols)

    scale, corr, _, _, mean = merge(extra, cols, rows)
    out_ref[:, 0:cols] = jnp.sum(scale * read(0), axis=0).astype(bf16)
    low = scale * read(2)
    grad = jnp.sum(scale * read(1) + (corr - mean[None]) * low, axis=0)
    out_ref[:, cols : 2 * cols] = grad.astype(bf16)
    out_ref[:, 2 * cols : 3 * cols] = jnp.sum(low, axis=0).astype(bf16)
    out_ref[:, 3 * cols :] = pack(merge(extra, keys, rows)[2:])


def final_kernel(r_ref, c_ref, out_ref):
    rows, cols = c_ref.shape
    scale, own, _, total, _ = merge(r_ref[:, 3 * cols :], cols, rows)

    def read(n):
        return r_ref[:, n * cols : (n + 1) * cols].astype(f32).reshape(-1, rows, cols)

    summed = jnp.sum(scale * read(0), axis=0)
    attended = (summed / total).astype(bf16).astype(f32)
    corr = per_head(c_ref[...] * attended, HDIM, jnp.sum, 0.0)
    grad = jnp.sum(scale * (read(1) + (own - corr[None]) * read(2)), axis=0) / total
    both = jnp.concatenate([attended, grad], axis=1)
    two = jnp.concatenate([both, both], axis=0).astype(bf16)
    for n in range(out_ref.shape[0] // (2 * rows)):
        out_ref[2 * rows * n : 2 * rows * (n + 1), :] = two


def swap(block):
    return lax.ppermute(block, "rep", [(0, 1), (1, 0)])


def block_numbers():
    n = lax.axis_size("pb")
    pb, rep = lax.axis_index("pb"), lax.axis_index("rep")
    places = [(pb + shift) % n for shift in (0, n - 1, 1, 2)]
    numbers = [number for place in places for number in (place * 2 + rep, place * 2 + 1 - rep)]
    return jnp.stack(numbers).astype(jnp.int32)


AXES = ("psg", "pb", "rep")


def line_groups(mesh_shape, turn):
    side = SIDE
    assert side * side == mesh_shape[0]
    ids = np.arange(np.prod(mesh_shape)).reshape((side, side) + tuple(mesh_shape[1:]))
    groups = []
    for core in range(mesh_shape[2]):
        along = (core + turn + 1) % 2
        lines = np.moveaxis(ids[:, :, :, core], along, -1)
        groups += lines.reshape(-1, side).tolist()
    return groups


def exchange(x, groups):
    return lax.all_to_all(x, AXES, 0, 0, axis_index_groups=groups, tiled=True)


def body(queries, prefixes, owner, key_weight, value_weight, cotangent):
    slots, vectors, features = prefixes.shape
    rows, cols = queries.shape
    heads = cols // HDIM
    keys = heads * PL

    passages = prefixes.reshape(slots * vectors, features)
    n = lax.axis_size("pb")
    left, right, far = (
        lax.ppermute(passages, "pb", [(i, (i + shift) % n) for i in range(n)]) for shift in (1, n - 1, 2)
    )
    other = swap(passages)
    smem = pl.BlockSpec(memory_space=pltpu.SMEM)
    vmem = pl.BlockSpec(memory_space=pltpu.VMEM)
    sums = jax.ShapeDtypeStruct((slots * vectors, 2 * cols), f32)
    projected, rest = pl.pallas_call(
        own_kernel,
        out_shape=(sums, jax.ShapeDtypeStruct((key_weight.shape[0] - features, 2 * cols), bf16)),
        in_specs=[smem] + [vmem] * 3,
        out_specs=(vmem, vmem),
        compiler_params=pltpu.CompilerParams(vmem_limit_bytes=16 * 1024 * 1024),
        name="own_projection",
    )(block_numbers(), passages, key_weight, value_weight)
    left, projected, rest = lax.optimization_barrier((left, projected, rest))
    near = [other, left, swap(left), right, swap(right), far]
    far = swap(far)
    projected = pl.pallas_call(
        near_kernel,
        out_shape=sums,
        in_specs=[vmem] * (2 + len(near)),
        out_specs=vmem,
        compiler_params=pltpu.CompilerParams(vmem_limit_bytes=16 * 1024 * 1024),
        name="near_projection",
    )(projected, rest, *near)
    payload = pl.pallas_call(
        local_kernel,
        out_shape=jax.ShapeDtypeStruct((rows, 3 * cols + keys), bf16),
        in_specs=[smem] + [vmem] * 5,
        out_specs=vmem,
        scratch_shapes=[
            pltpu.VMEM((slots, keys, cols), bf16),
            pltpu.VMEM((slots, keys, cols), bf16),
            pltpu.VMEM((slots, TGT, keys), f32),
            pltpu.VMEM((slots, TGT, keys), f32),
            pltpu.VMEM((QUESTIONS + 1, TGT, keys), f32),
            pltpu.VMEM((QUESTIONS + 1, TGT, keys), f32),
            pltpu.VMEM((QUESTIONS + 1, TGT, keys), f32),
            pltpu.VMEM((QUESTIONS + 1, TGT, keys), f32),
            pltpu.VMEM((QUESTIONS + 1, TGT, cols), f32),
            pltpu.VMEM((QUESTIONS + 1, 2 * TGT, cols), f32),
        ],
        compiler_params=pltpu.CompilerParams(vmem_limit_bytes=24 * 1024 * 1024),
        name="local_sums",
    )(owner, projected, far, rest, queries, cotangent)

    shape = tuple(lax.axis_size(name) for name in AXES)
    first_lines, second_lines = line_groups(shape, 0), line_groups(shape, 1)
    block_rows = rows // SIDE
    merged = pl.pallas_call(
        merge_kernel,
        out_shape=jax.ShapeDtypeStruct((block_rows, payload.shape[1]), bf16),
        in_specs=[vmem],
        out_specs=vmem,
        compiler_params=pltpu.CompilerParams(vmem_limit_bytes=24 * 1024 * 1024),
        name="line_sums",
    )(exchange(payload, first_lines))
    received = exchange(merged, second_lines)

    own = block_rows // SIDE
    place = lax.axis_index("psg")
    z, y = place // SIDE, place % SIDE
    core = lax.axis_index("rep")
    start = jnp.where(core == 0, y, z) * block_rows + jnp.where(core == 0, z, y) * own
    own_cotangent = lax.dynamic_slice_in_dim(cotangent, start, own, 0).astype(f32)
    finished = pl.pallas_call(
        final_kernel,
        out_shape=jax.ShapeDtypeStruct((block_rows, 2 * cols), bf16),
        in_specs=[vmem, vmem],
        out_specs=vmem,
        compiler_params=pltpu.CompilerParams(vmem_limit_bytes=24 * 1024 * 1024),
        name="final_sums",
    )(received, own_cotangent)
    block_out = exchange(finished, second_lines)
    copies = jnp.broadcast_to(block_out[None], (SIDE,) + block_out.shape).reshape(rows, 2 * cols)
    outputs = exchange(copies, first_lines)
    return outputs[:, :cols], outputs[:, cols:]


def solution(mesh):
    placed = (
        P(None, ("pb", "rep")),
        P("psg", None, ("pb", "rep")),
        P("psg"),
        P(None, ("pb", "rep")),
        P(None, ("pb", "rep")),
        P(None, ("pb", "rep")),
    )
    return jax.shard_map(
        body,
        mesh=mesh,
        in_specs=placed,
        out_specs=(P(None, ("pb", "rep")), P(None, ("pb", "rep"))),
        check_vma=False,
    )
```

```python
import jax
import jax.numpy as jnp
from jax import lax
from jax.experimental import pallas as pl
from jax.experimental.pallas import tpu as pltpu
from jax.sharding import PartitionSpec as P

HDIM = 64
TGT = 32
PL = 32
QUESTIONS = 16
PARTS = 3

masked_value = -1e30

f32 = jnp.float32
bf16 = jnp.bfloat16
NT = (((1,), (1,)), ((), ()))


def split_parts(x):
    first = x.astype(bf16)
    rest = x - first.astype(f32)
    second = rest.astype(bf16)
    third = (rest - second.astype(f32)).astype(bf16)
    return first.astype(f32), second.astype(f32), third.astype(f32)


def per_head(x, width, reduce, fill):
    lane_head = lax.broadcasted_iota(jnp.int32, x.shape, x.ndim - 1) // width
    out = jnp.zeros_like(x)
    for head in range(x.shape[-1] // width):
        one = reduce(jnp.where(lane_head == head, x, fill), axis=-1, keepdims=True)
        out = jnp.where(lane_head == head, one, out)
    return out


def own_kernel(block_ref, x_ref, wk_ref, wv_ref, acc_ref, rest_ref):
    wide = x_ref.shape[1]
    cols = wk_ref.shape[1]
    for n in range(wk_ref.shape[0] // wide):
        at = pl.ds(pl.multiple_of(block_ref[n] * wide, wide), wide)
        for side, ref in enumerate((wk_ref, wv_ref)):
            columns = slice(side * cols, (side + 1) * cols)
            if n == 0:
                acc_ref[:, columns] = jnp.dot(x_ref[...], ref[at, :], preferred_element_type=f32)
            else:
                rest_ref[(n - 1) * wide : n * wide, columns] = ref[at, :]


def near_kernel(acc_ref, rest_ref, *refs):
    x_refs, out_ref = refs[:-1], refs[-1]
    weight = rest_ref[0 : len(x_refs) * x_refs[0].shape[1], :]
    chunk = 512
    for low in range(0, acc_ref.shape[0], chunk):
        rows = jnp.concatenate([x[low : low + chunk, :] for x in x_refs], axis=1)
        out_ref[low : low + chunk, :] = acc_ref[low : low + chunk, :] + jnp.dot(
            rows, weight, preferred_element_type=f32
        )


def local_kernel(owner_ref, acc_ref, *refs):
    (far_ref, rest_ref, q_ref, c_ref, out_ref, kblk, vblk, score, product, top, total, dots, corr, acc_v, acc_k) = refs
    slots = owner_ref.shape[0]
    half = slots // 2
    cols = q_ref.shape[1]
    heads = cols // HDIM
    keys = heads * PL

    top[...] = jnp.full_like(top, masked_value)
    total[...] = jnp.zeros_like(total)
    dots[...] = jnp.zeros_like(dots)
    acc_v[...] = jnp.zeros_like(acc_v)
    acc_k[...] = jnp.zeros_like(acc_k)

    on_diagonal = (
        lax.broadcasted_iota(jnp.int32, (keys, cols), 0) // PL
        == lax.broadcasted_iota(jnp.int32, (keys, cols), 1) // HDIM
    ).astype(f32).astype(bf16)

    for side in range(2):
        low = side * half * PL
        rows = far_ref[low : low + half * PL, :]
        projected = acc_ref[low : low + half * PL, :] + jnp.dot(
            rows, rest_ref[-rows.shape[1] :, :], preferred_element_type=f32
        )
        projected = projected.astype(bf16)
        for i in range(half):
            slot = side * half + i
            own = projected[i * PL : (i + 1) * PL]
            kb = jnp.concatenate([own[:, :cols]] * heads, axis=0) * on_diagonal
            vb = jnp.concatenate([own[:, cols:]] * heads, axis=0) * on_diagonal
            kblk[slot] = kb
            vblk[slot] = vb
            o = owner_ref[slot]
            at = pl.ds(pl.multiple_of(jnp.minimum(o, QUESTIONS - 1) * TGT, TGT), TGT)
            s = lax.dot_general(q_ref[at, :], kb, NT, preferred_element_type=f32)
            score[slot] = s
            product[slot] = lax.dot_general(c_ref[at, :], vb, NT, preferred_element_type=f32)
            top[o] = jnp.maximum(top[o], s)

    for q in range(QUESTIONS):
        top[q] = per_head(top[q], PL, jnp.max, masked_value)

    for slot in range(slots):
        o = owner_ref[slot]
        e = jnp.exp(score[slot] - top[o])
        score[slot] = e
        total[o] = total[o] + e
        dots[o] = dots[o] + e * product[slot]

    for q in range(QUESTIONS):
        t = per_head(total[q], PL, jnp.sum, 0.0)
        d = per_head(dots[q], PL, jnp.sum, 0.0)
        total[q] = t
        corr[q] = jnp.where(t > 0.0, d / jnp.where(t > 0.0, t, 1.0), 0.0)
    corr[QUESTIONS] = jnp.zeros_like(corr[QUESTIONS])

    for slot in range(slots):
        o = owner_ref[slot]
        e = score[slot]
        g = e * (product[slot] - corr[o])
        both = jnp.concatenate([e, g], axis=0).astype(bf16)
        acc_v[o] = acc_v[o] + jnp.dot(both[:TGT], vblk[slot], preferred_element_type=f32)
        acc_k[o] = acc_k[o] + jnp.dot(both, kblk[slot], preferred_element_type=f32)

    part = lax.broadcasted_iota(jnp.int32, (TGT, keys), 1) % PL
    for q in range(QUESTIONS):
        at = slice(q * TGT, (q + 1) * TGT)
        out_ref[at, 0:cols] = acc_v[q].astype(bf16)
        out_ref[at, cols : 2 * cols] = acc_k[q, TGT:, :].astype(bf16)
        out_ref[at, 2 * cols : 3 * cols] = acc_k[q, :TGT, :].astype(bf16)
        extra = jnp.zeros((TGT, keys), f32)
        pieces_of = split_parts(top[q]) + split_parts(total[q]) + split_parts(corr[q])
        for n, piece in enumerate(pieces_of):
            extra = jnp.where(part == n, piece, extra)
        out_ref[at, 3 * cols :] = extra.astype(bf16)


def final_kernel(r_ref, c_ref, out_ref):
    rows, cols = c_ref.shape
    heads = cols // HDIM
    keys = heads * PL
    devices = r_ref.shape[0] // rows
    lane = lax.broadcasted_iota(jnp.int32, (keys, 3 * cols), 0)
    spot = lax.broadcasted_iota(jnp.int32, (keys, 3 * cols), 1)
    pick = (lane // PL == (spot % cols) // HDIM) & ((lane % PL) // PARTS == spot // cols)
    pick = pick.astype(f32).astype(bf16)
    wide = jnp.dot(r_ref[:, 3 * cols :], pick, preferred_element_type=f32).reshape(devices, rows, 3 * cols)
    top = wide[:, :, 0:cols]
    weight = jnp.exp(top - jnp.max(top, axis=0, keepdims=True))
    total = jnp.sum(weight * wide[:, :, cols : 2 * cols], axis=0)

    def read(n):
        return r_ref[:, n * cols : (n + 1) * cols].astype(f32).reshape(devices, rows, cols)

    summed = jnp.sum(weight * read(0), axis=0)
    attended = (summed / total).astype(bf16).astype(f32)
    corr = per_head(c_ref[...] * attended, HDIM, jnp.sum, 0.0)
    shift = wide[:, :, 2 * cols :] - corr[None]
    grad = jnp.sum(weight * (read(1) + shift * read(2)), axis=0) / total
    both = jnp.concatenate([attended, grad], axis=1)
    two = jnp.concatenate([both, both], axis=0).astype(bf16)
    for n in range(devices // 2):
        out_ref[2 * rows * n : 2 * rows * (n + 1), :] = two


def swap(block):
    return lax.ppermute(block, "rep", [(0, 1), (1, 0)])


def block_numbers():
    n = lax.axis_size("pb")
    pb, rep = lax.axis_index("pb"), lax.axis_index("rep")
    places = [(pb + shift) % n for shift in (0, n - 1, 1, 2)]
    numbers = [number for place in places for number in (place * 2 + rep, place * 2 + 1 - rep)]
    return jnp.stack(numbers).astype(jnp.int32)


def body(queries, prefixes, owner, key_weight, value_weight, cotangent):
    slots, vectors, features = prefixes.shape
    rows, cols = queries.shape
    heads = cols // HDIM
    keys = heads * PL
    devices = lax.axis_size("psg")
    own = rows // devices

    passages = prefixes.reshape(slots * vectors, features)
    n = lax.axis_size("pb")
    to_right = [(i, (i + 1) % n) for i in range(n)]
    left = lax.ppermute(passages, "pb", to_right)
    right = lax.ppermute(passages, "pb", [(i, (i - 1) % n) for i in range(n)])
    other = swap(passages)
    smem = pl.BlockSpec(memory_space=pltpu.SMEM)
    vmem = pl.BlockSpec(memory_space=pltpu.VMEM)
    sums = jax.ShapeDtypeStruct((slots * vectors, 2 * cols), f32)
    projected, rest = pl.pallas_call(
        own_kernel,
        out_shape=(sums, jax.ShapeDtypeStruct((key_weight.shape[0] - features, 2 * cols), bf16)),
        in_specs=[smem] + [vmem] * 3,
        out_specs=(vmem, vmem),
        compiler_params=pltpu.CompilerParams(vmem_limit_bytes=16 * 1024 * 1024),
        name="own_projection",
    )(block_numbers(), passages, key_weight, value_weight)
    left, projected, rest = lax.optimization_barrier((left, projected, rest))
    far = lax.ppermute(left, "pb", to_right)
    near = [other, left, swap(left), right, swap(right), far]
    far = swap(far)
    projected = pl.pallas_call(
        near_kernel,
        out_shape=sums,
        in_specs=[vmem] * (2 + len(near)),
        out_specs=vmem,
        compiler_params=pltpu.CompilerParams(vmem_limit_bytes=16 * 1024 * 1024),
        name="near_projection",
    )(projected, rest, *near)
    payload = pl.pallas_call(
        local_kernel,
        out_shape=jax.ShapeDtypeStruct((rows, 3 * cols + keys), bf16),
        in_specs=[smem] + [vmem] * 5,
        out_specs=vmem,
        scratch_shapes=[
            pltpu.VMEM((slots, keys, cols), bf16),
            pltpu.VMEM((slots, keys, cols), bf16),
            pltpu.VMEM((slots, TGT, keys), f32),
            pltpu.VMEM((slots, TGT, keys), f32),
            pltpu.VMEM((QUESTIONS + 1, TGT, keys), f32),
            pltpu.VMEM((QUESTIONS + 1, TGT, keys), f32),
            pltpu.VMEM((QUESTIONS + 1, TGT, keys), f32),
            pltpu.VMEM((QUESTIONS + 1, TGT, keys), f32),
            pltpu.VMEM((QUESTIONS + 1, TGT, cols), f32),
            pltpu.VMEM((QUESTIONS + 1, 2 * TGT, cols), f32),
        ],
        compiler_params=pltpu.CompilerParams(vmem_limit_bytes=24 * 1024 * 1024),
        name="local_sums",
    )(owner, projected, far, rest, queries, cotangent)

    received = lax.all_to_all(payload, "psg", 0, 0, tiled=True)
    own_cotangent = lax.dynamic_slice_in_dim(cotangent, lax.axis_index("psg") * own, own, 0).astype(f32)
    finished = pl.pallas_call(
        final_kernel,
        out_shape=jax.ShapeDtypeStruct((rows, 2 * cols), bf16),
        in_specs=[vmem, vmem],
        out_specs=vmem,
        compiler_params=pltpu.CompilerParams(vmem_limit_bytes=24 * 1024 * 1024),
        name="final_sums",
    )(received, own_cotangent)
    outputs = lax.all_to_all(finished, "psg", 0, 0, tiled=True)
    return outputs[:, :cols], outputs[:, cols:]


def solution(mesh):
    placed = (
        P(None, ("pb", "rep")),
        P("psg", None, ("pb", "rep")),
        P("psg"),
        P(None, ("pb", "rep")),
        P(None, ("pb", "rep")),
        P(None, ("pb", "rep")),
    )
    return jax.shard_map(
        body,
        mesh=mesh,
        in_specs=placed,
        out_specs=(P(None, ("pb", "rep")), P(None, ("pb", "rep"))),
        check_vma=False,
    )
```

```python
import jax
import jax.numpy as jnp
from jax import lax
from jax.experimental import pallas as pl
from jax.experimental.pallas import tpu as pltpu
from jax.sharding import PartitionSpec as P

HDIM = 64
TGT = 32
PL = 32
QUESTIONS = 16
PARTS = 3

masked_value = -1e30

f32 = jnp.float32
bf16 = jnp.bfloat16
NT = (((1,), (1,)), ((), ()))


def split_parts(x):
    first = x.astype(bf16)
    rest = x - first.astype(f32)
    second = rest.astype(bf16)
    third = (rest - second.astype(f32)).astype(bf16)
    return first.astype(f32), second.astype(f32), third.astype(f32)


def per_head(x, width, reduce, fill):
    lane_head = lax.broadcasted_iota(jnp.int32, x.shape, x.ndim - 1) // width
    out = jnp.zeros_like(x)
    for head in range(x.shape[-1] // width):
        one = reduce(jnp.where(lane_head == head, x, fill), axis=-1, keepdims=True)
        out = jnp.where(lane_head == head, one, out)
    return out


def own_kernel(block_ref, x_ref, wk_ref, wv_ref, acc_ref, rest_ref):
    wide = x_ref.shape[1]
    cols = wk_ref.shape[1]
    for n in range(wk_ref.shape[0] // wide):
        at = pl.ds(pl.multiple_of(block_ref[n] * wide, wide), wide)
        for side, ref in enumerate((wk_ref, wv_ref)):
            columns = slice(side * cols, (side + 1) * cols)
            if n == 0:
                acc_ref[:, columns] = jnp.dot(x_ref[...], ref[at, :], preferred_element_type=f32)
            else:
                rest_ref[(n - 1) * wide : n * wide, columns] = ref[at, :]


def near_kernel(acc_ref, rest_ref, *refs):
    x_refs, out_ref = refs[:-1], refs[-1]
    weight = rest_ref[0 : len(x_refs) * x_refs[0].shape[1], :]
    chunk = 512
    for low in range(0, acc_ref.shape[0], chunk):
        rows = jnp.concatenate([x[low : low + chunk, :] for x in x_refs], axis=1)
        out_ref[low : low + chunk, :] = acc_ref[low : low + chunk, :] + jnp.dot(
            rows, weight, preferred_element_type=f32
        )


def local_kernel(owner_ref, acc_ref, *refs):
    (far_ref, rest_ref, q_ref, c_ref, out_ref, kblk, vblk, score, product, top, total, dots, corr, acc_v, acc_k) = refs
    slots = owner_ref.shape[0]
    half = slots // 2
    cols = q_ref.shape[1]
    heads = cols // HDIM
    keys = heads * PL

    top[...] = jnp.full_like(top, masked_value)
    total[...] = jnp.zeros_like(total)
    dots[...] = jnp.zeros_like(dots)
    acc_v[...] = jnp.zeros_like(acc_v)
    acc_k[...] = jnp.zeros_like(acc_k)

    on_diagonal = (
        lax.broadcasted_iota(jnp.int32, (keys, cols), 0) // PL
        == lax.broadcasted_iota(jnp.int32, (keys, cols), 1) // HDIM
    ).astype(f32).astype(bf16)

    for side in range(2):
        low = side * half * PL
        rows = far_ref[low : low + half * PL, :]
        projected = acc_ref[low : low + half * PL, :] + jnp.dot(
            rows, rest_ref[-rows.shape[1] :, :], preferred_element_type=f32
        )
        projected = projected.astype(bf16)
        for i in range(half):
            slot = side * half + i
            own = projected[i * PL : (i + 1) * PL]
            kb = jnp.concatenate([own[:, :cols]] * heads, axis=0) * on_diagonal
            vb = jnp.concatenate([own[:, cols:]] * heads, axis=0) * on_diagonal
            kblk[slot] = kb
            vblk[slot] = vb
            o = owner_ref[slot]
            at = pl.ds(pl.multiple_of(jnp.minimum(o, QUESTIONS - 1) * TGT, TGT), TGT)
            s = lax.dot_general(q_ref[at, :], kb, NT, preferred_element_type=f32)
            score[slot] = s
            product[slot] = lax.dot_general(c_ref[at, :], vb, NT, preferred_element_type=f32)
            top[o] = jnp.maximum(top[o], s)

    for q in range(QUESTIONS):
        top[q] = per_head(top[q], PL, jnp.max, masked_value)

    for slot in range(slots):
        o = owner_ref[slot]
        e = jnp.exp(score[slot] - top[o])
        score[slot] = e
        total[o] = total[o] + e
        dots[o] = dots[o] + e * product[slot]

    for q in range(QUESTIONS):
        t = per_head(total[q], PL, jnp.sum, 0.0)
        d = per_head(dots[q], PL, jnp.sum, 0.0)
        total[q] = t
        corr[q] = jnp.where(t > 0.0, d / jnp.where(t > 0.0, t, 1.0), 0.0)
    corr[QUESTIONS] = jnp.zeros_like(corr[QUESTIONS])

    for slot in range(slots):
        o = owner_ref[slot]
        e = score[slot]
        g = e * (product[slot] - corr[o])
        both = jnp.concatenate([e, g], axis=0).astype(bf16)
        acc_v[o] = acc_v[o] + jnp.dot(both[:TGT], vblk[slot], preferred_element_type=f32)
        acc_k[o] = acc_k[o] + jnp.dot(both, kblk[slot], preferred_element_type=f32)

    part = lax.broadcasted_iota(jnp.int32, (TGT, keys), 1) % PL
    for q in range(QUESTIONS):
        at = slice(q * TGT, (q + 1) * TGT)
        out_ref[at, 0:cols] = acc_v[q].astype(bf16)
        out_ref[at, cols : 2 * cols] = acc_k[q, TGT:, :].astype(bf16)
        out_ref[at, 2 * cols : 3 * cols] = acc_k[q, :TGT, :].astype(bf16)
        extra = jnp.zeros((TGT, keys), f32)
        pieces_of = split_parts(top[q]) + split_parts(total[q]) + split_parts(corr[q])
        for n, piece in enumerate(pieces_of):
            extra = jnp.where(part == n, piece, extra)
        out_ref[at, 3 * cols :] = extra.astype(bf16)


def final_kernel(r_ref, c_ref, out_ref):
    rows, cols = c_ref.shape
    heads = cols // HDIM
    keys = heads * PL
    devices = r_ref.shape[0] // rows
    lane = lax.broadcasted_iota(jnp.int32, (keys, 3 * cols), 0)
    spot = lax.broadcasted_iota(jnp.int32, (keys, 3 * cols), 1)
    pick = (lane // PL == (spot % cols) // HDIM) & ((lane % PL) // PARTS == spot // cols)
    pick = pick.astype(f32).astype(bf16)
    wide = jnp.dot(r_ref[:, 3 * cols :], pick, preferred_element_type=f32).reshape(devices, rows, 3 * cols)
    top = wide[:, :, 0:cols]
    weight = jnp.exp(top - jnp.max(top, axis=0, keepdims=True))
    total = jnp.sum(weight * wide[:, :, cols : 2 * cols], axis=0)

    def read(n):
        return r_ref[:, n * cols : (n + 1) * cols].astype(f32).reshape(devices, rows, cols)

    summed = jnp.sum(weight * read(0), axis=0)
    attended = (summed / total).astype(bf16).astype(f32)
    corr = per_head(c_ref[...] * attended, HDIM, jnp.sum, 0.0)
    shift = wide[:, :, 2 * cols :] - corr[None]
    grad = jnp.sum(weight * (read(1) + shift * read(2)), axis=0) / total
    both = jnp.concatenate([attended, grad], axis=1)
    two = jnp.concatenate([both, both], axis=0).astype(bf16)
    for n in range(devices // 2):
        out_ref[2 * rows * n : 2 * rows * (n + 1), :] = two


def swap(block):
    return lax.ppermute(block, "rep", [(0, 1), (1, 0)])


def block_numbers():
    n = lax.axis_size("pb")
    pb, rep = lax.axis_index("pb"), lax.axis_index("rep")
    step = 1 - 2 * rep
    own = [(pb + shift) % n for shift in (0, n - step, n + step, 2)]
    other = [(pb + shift) % n for shift in (0, n + step, n - step, 2)]
    numbers = [number for pair in zip(own, other) for number in (pair[0] * 2 + rep, pair[1] * 2 + 1 - rep)]
    return jnp.stack(numbers).astype(jnp.int32)


def along(block, way):
    n = lax.axis_size("pb")
    pairs = []
    for chip in range(n):
        pairs.append((chip * 2, (chip + way) % n * 2))
        pairs.append((chip * 2 + 1, (chip - way) % n * 2 + 1))
    return lax.ppermute(block, ("pb", "rep"), pairs)


def body(queries, prefixes, owner, key_weight, value_weight, cotangent):
    slots, vectors, features = prefixes.shape
    rows, cols = queries.shape
    heads = cols // HDIM
    keys = heads * PL
    devices = lax.axis_size("psg")
    own = rows // devices

    passages = prefixes.reshape(slots * vectors, features)
    ahead, behind = along(passages, 1), along(passages, -1)
    other = swap(passages)
    smem = pl.BlockSpec(memory_space=pltpu.SMEM)
    vmem = pl.BlockSpec(memory_space=pltpu.VMEM)
    sums = jax.ShapeDtypeStruct((slots * vectors, 2 * cols), f32)
    projected, rest = pl.pallas_call(
        own_kernel,
        out_shape=(sums, jax.ShapeDtypeStruct((key_weight.shape[0] - features, 2 * cols), bf16)),
        in_specs=[smem] + [vmem] * 3,
        out_specs=(vmem, vmem),
        compiler_params=pltpu.CompilerParams(vmem_limit_bytes=16 * 1024 * 1024),
        name="own_projection",
    )(block_numbers(), passages, key_weight, value_weight)
    ahead, projected, rest = lax.optimization_barrier((ahead, projected, rest))
    far = along(ahead, 1)
    near = [other, ahead, swap(ahead), behind, swap(behind), far]
    far = swap(far)
    projected = pl.pallas_call(
        near_kernel,
        out_shape=sums,
        in_specs=[vmem] * (2 + len(near)),
        out_specs=vmem,
        compiler_params=pltpu.CompilerParams(vmem_limit_bytes=16 * 1024 * 1024),
        name="near_projection",
    )(projected, rest, *near)
    payload = pl.pallas_call(
        local_kernel,
        out_shape=jax.ShapeDtypeStruct((rows, 3 * cols + keys), bf16),
        in_specs=[smem] + [vmem] * 5,
        out_specs=vmem,
        scratch_shapes=[
            pltpu.VMEM((slots, keys, cols), bf16),
            pltpu.VMEM((slots, keys, cols), bf16),
            pltpu.VMEM((slots, TGT, keys), f32),
            pltpu.VMEM((slots, TGT, keys), f32),
            pltpu.VMEM((QUESTIONS + 1, TGT, keys), f32),
            pltpu.VMEM((QUESTIONS + 1, TGT, keys), f32),
            pltpu.VMEM((QUESTIONS + 1, TGT, keys), f32),
            pltpu.VMEM((QUESTIONS + 1, TGT, keys), f32),
            pltpu.VMEM((QUESTIONS + 1, TGT, cols), f32),
            pltpu.VMEM((QUESTIONS + 1, 2 * TGT, cols), f32),
        ],
        compiler_params=pltpu.CompilerParams(vmem_limit_bytes=24 * 1024 * 1024),
        name="local_sums",
    )(owner, projected, far, rest, queries, cotangent)

    received = lax.all_to_all(payload, "psg", 0, 0, tiled=True)
    own_cotangent = lax.dynamic_slice_in_dim(cotangent, lax.axis_index("psg") * own, own, 0).astype(f32)
    finished = pl.pallas_call(
        final_kernel,
        out_shape=jax.ShapeDtypeStruct((rows, 2 * cols), bf16),
        in_specs=[vmem, vmem],
        out_specs=vmem,
        compiler_params=pltpu.CompilerParams(vmem_limit_bytes=24 * 1024 * 1024),
        name="final_sums",
    )(received, own_cotangent)
    outputs = lax.all_to_all(finished, "psg", 0, 0, tiled=True)
    return outputs[:, :cols], outputs[:, cols:]


def solution(mesh):
    placed = (
        P(None, ("pb", "rep")),
        P("psg", None, ("pb", "rep")),
        P("psg"),
        P(None, ("pb", "rep")),
        P(None, ("pb", "rep")),
        P(None, ("pb", "rep")),
    )
    return jax.shard_map(
        body,
        mesh=mesh,
        in_specs=placed,
        out_specs=(P(None, ("pb", "rep")), P(None, ("pb", "rep"))),
        check_vma=False,
    )
```

```python
import jax
import jax.numpy as jnp
from jax import lax
from jax.experimental import pallas as pl
from jax.experimental.pallas import tpu as pltpu
from jax.sharding import PartitionSpec as P

HDIM = 64
TGT = 32
PL = 32
QUESTIONS = 16
PARTS = 3

masked_value = -1e30

f32 = jnp.float32
bf16 = jnp.bfloat16
NT = (((1,), (1,)), ((), ()))


def split_parts(x):
    first = x.astype(bf16)
    rest = x - first.astype(f32)
    second = rest.astype(bf16)
    third = (rest - second.astype(f32)).astype(bf16)
    return first.astype(f32), second.astype(f32), third.astype(f32)


def per_head(x, width, reduce, fill):
    lane_head = lax.broadcasted_iota(jnp.int32, x.shape, x.ndim - 1) // width
    out = jnp.zeros_like(x)
    for head in range(x.shape[-1] // width):
        one = reduce(jnp.where(lane_head == head, x, fill), axis=-1, keepdims=True)
        out = jnp.where(lane_head == head, one, out)
    return out


def own_kernel(block_ref, x_ref, wk_ref, wv_ref, acc_ref, rest_ref):
    wide = x_ref.shape[1]
    cols = wk_ref.shape[1]
    for n in range(wk_ref.shape[0] // wide):
        at = pl.ds(pl.multiple_of(block_ref[n] * wide, wide), wide)
        for side, ref in enumerate((wk_ref, wv_ref)):
            columns = slice(side * cols, (side + 1) * cols)
            if n == 0:
                acc_ref[:, columns] = jnp.dot(x_ref[...], ref[at, :], preferred_element_type=f32)
            else:
                rest_ref[(n - 1) * wide : n * wide, columns] = ref[at, :]


def near_kernel(acc_ref, rest_ref, *refs):
    x_refs, out_ref = refs[:-1], refs[-1]
    weight = rest_ref[0 : len(x_refs) * x_refs[0].shape[1], :]
    chunk = 512
    for low in range(0, acc_ref.shape[0], chunk):
        rows = jnp.concatenate([x[low : low + chunk, :] for x in x_refs], axis=1)
        out_ref[low : low + chunk, :] = acc_ref[low : low + chunk, :] + jnp.dot(
            rows, weight, preferred_element_type=f32
        )


def local_kernel(owner_ref, acc_ref, *refs):
    (far_ref, rest_ref, q_ref, c_ref, out_ref, kblk, vblk, score, product, top, total, dots, corr, acc_v, acc_k) = refs
    slots = owner_ref.shape[0]
    half = slots // 2
    cols = q_ref.shape[1]
    heads = cols // HDIM
    keys = heads * PL

    top[...] = jnp.full_like(top, masked_value)
    total[...] = jnp.zeros_like(total)
    dots[...] = jnp.zeros_like(dots)
    acc_v[...] = jnp.zeros_like(acc_v)
    acc_k[...] = jnp.zeros_like(acc_k)

    on_diagonal = (
        lax.broadcasted_iota(jnp.int32, (keys, cols), 0) // PL
        == lax.broadcasted_iota(jnp.int32, (keys, cols), 1) // HDIM
    ).astype(f32).astype(bf16)

    for side in range(2):
        low = side * half * PL
        rows = far_ref[low : low + half * PL, :]
        projected = acc_ref[low : low + half * PL, :] + jnp.dot(
            rows, rest_ref[-rows.shape[1] :, :], preferred_element_type=f32
        )
        projected = projected.astype(bf16)
        for i in range(half):
            slot = side * half + i
            own = projected[i * PL : (i + 1) * PL]
            kb = jnp.concatenate([own[:, :cols]] * heads, axis=0) * on_diagonal
            vb = jnp.concatenate([own[:, cols:]] * heads, axis=0) * on_diagonal
            kblk[slot] = kb
            vblk[slot] = vb
            o = owner_ref[slot]
            at = pl.ds(pl.multiple_of(jnp.minimum(o, QUESTIONS - 1) * TGT, TGT), TGT)
            s = lax.dot_general(q_ref[at, :], kb, NT, preferred_element_type=f32)
            score[slot] = s
            product[slot] = lax.dot_general(c_ref[at, :], vb, NT, preferred_element_type=f32)
            top[o] = jnp.maximum(top[o], s)

    for q in range(QUESTIONS):
        top[q] = per_head(top[q], PL, jnp.max, masked_value)

    for slot in range(slots):
        o = owner_ref[slot]
        e = jnp.exp(score[slot] - top[o])
        score[slot] = e
        total[o] = total[o] + e
        dots[o] = dots[o] + e * product[slot]

    for q in range(QUESTIONS):
        t = per_head(total[q], PL, jnp.sum, 0.0)
        d = per_head(dots[q], PL, jnp.sum, 0.0)
        total[q] = t
        corr[q] = jnp.where(t > 0.0, d / jnp.where(t > 0.0, t, 1.0), 0.0)
    corr[QUESTIONS] = jnp.zeros_like(corr[QUESTIONS])

    for slot in range(slots):
        o = owner_ref[slot]
        e = score[slot]
        g = e * (product[slot] - corr[o])
        both = jnp.concatenate([e, g], axis=0).astype(bf16)
        acc_v[o] = acc_v[o] + jnp.dot(both[:TGT], vblk[slot], preferred_element_type=f32)
        acc_k[o] = acc_k[o] + jnp.dot(both, kblk[slot], preferred_element_type=f32)

    part = lax.broadcasted_iota(jnp.int32, (TGT, keys), 1) % PL
    for q in range(QUESTIONS):
        at = slice(q * TGT, (q + 1) * TGT)
        out_ref[at, 0:cols] = acc_v[q].astype(bf16)
        out_ref[at, cols : 2 * cols] = acc_k[q, TGT:, :].astype(bf16)
        out_ref[at, 2 * cols : 3 * cols] = acc_k[q, :TGT, :].astype(bf16)
        extra = jnp.zeros((TGT, keys), f32)
        pieces_of = split_parts(top[q]) + split_parts(total[q]) + split_parts(corr[q])
        for n, piece in enumerate(pieces_of):
            extra = jnp.where(part == n, piece, extra)
        out_ref[at, 3 * cols :] = extra.astype(bf16)


def final_kernel(r_ref, c_ref, out_ref):
    rows, cols = c_ref.shape
    heads = cols // HDIM
    keys = heads * PL
    devices = r_ref.shape[0] // rows
    lane = lax.broadcasted_iota(jnp.int32, (keys, 3 * cols), 0)
    spot = lax.broadcasted_iota(jnp.int32, (keys, 3 * cols), 1)
    pick = (lane // PL == (spot % cols) // HDIM) & ((lane % PL) // PARTS == spot // cols)
    pick = pick.astype(f32).astype(bf16)
    wide = jnp.dot(r_ref[:, 3 * cols :], pick, preferred_element_type=f32).reshape(devices, rows, 3 * cols)
    top = wide[:, :, 0:cols]
    weight = jnp.exp(top - jnp.max(top, axis=0, keepdims=True))
    total = jnp.sum(weight * wide[:, :, cols : 2 * cols], axis=0)

    def read(n):
        return r_ref[:, n * cols : (n + 1) * cols].astype(f32).reshape(devices, rows, cols)

    summed = jnp.sum(weight * read(0), axis=0)
    attended = (summed / total).astype(bf16).astype(f32)
    corr = per_head(c_ref[...] * attended, HDIM, jnp.sum, 0.0)
    shift = wide[:, :, 2 * cols :] - corr[None]
    grad = jnp.sum(weight * (read(1) + shift * read(2)), axis=0) / total
    both = jnp.concatenate([attended, grad], axis=1)
    two = jnp.concatenate([both, both], axis=0).astype(bf16)
    for n in range(devices // 2):
        out_ref[2 * rows * n : 2 * rows * (n + 1), :] = two


def swap(block):
    return lax.ppermute(block, "rep", [(0, 1), (1, 0)])


def block_numbers():
    n = lax.axis_size("pb")
    pb, rep = lax.axis_index("pb"), lax.axis_index("rep")
    step = 1 - 2 * rep
    own = [(pb + shift) % n for shift in (0, n - step, n + step, 2)]
    other = [(pb + shift) % n for shift in (0, n + step, n - step, 2)]
    numbers = [number for pair in zip(own, other) for number in (pair[0] * 2 + rep, pair[1] * 2 + 1 - rep)]
    return jnp.stack(numbers).astype(jnp.int32)


def along(block, way):
    n = lax.axis_size("pb")
    pairs = []
    for chip in range(n):
        pairs.append((chip * 2, (chip + way) % n * 2))
        pairs.append((chip * 2 + 1, (chip - way) % n * 2 + 1))
    return lax.ppermute(block, ("pb", "rep"), pairs)


def body(queries, prefixes, owner, key_weight, value_weight, cotangent):
    slots, vectors, features = prefixes.shape
    rows, cols = queries.shape
    heads = cols // HDIM
    keys = heads * PL
    devices = lax.axis_size("psg")
    own = rows // devices

    passages = prefixes.reshape(slots * vectors, features)
    ahead = along(passages, 1)
    smem = pl.BlockSpec(memory_space=pltpu.SMEM)
    vmem = pl.BlockSpec(memory_space=pltpu.VMEM)
    sums = jax.ShapeDtypeStruct((slots * vectors, 2 * cols), f32)
    projected, rest = pl.pallas_call(
        own_kernel,
        out_shape=(sums, jax.ShapeDtypeStruct((key_weight.shape[0] - features, 2 * cols), bf16)),
        in_specs=[smem] + [vmem] * 3,
        out_specs=(vmem, vmem),
        compiler_params=pltpu.CompilerParams(vmem_limit_bytes=16 * 1024 * 1024),
        name="own_projection",
    )(block_numbers(), passages, key_weight, value_weight)
    held, projected, rest = lax.optimization_barrier((passages, projected, rest))
    behind, other = along(held, -1), swap(held)
    far = along(ahead, 1)
    near = [other, ahead, swap(ahead), behind, swap(behind), far]
    far = swap(far)
    projected = pl.pallas_call(
        near_kernel,
        out_shape=sums,
        in_specs=[vmem] * (2 + len(near)),
        out_specs=vmem,
        compiler_params=pltpu.CompilerParams(vmem_limit_bytes=16 * 1024 * 1024),
        name="near_projection",
    )(projected, rest, *near)
    payload = pl.pallas_call(
        local_kernel,
        out_shape=jax.ShapeDtypeStruct((rows, 3 * cols + keys), bf16),
        in_specs=[smem] + [vmem] * 5,
        out_specs=vmem,
        scratch_shapes=[
            pltpu.VMEM((slots, keys, cols), bf16),
            pltpu.VMEM((slots, keys, cols), bf16),
            pltpu.VMEM((slots, TGT, keys), f32),
            pltpu.VMEM((slots, TGT, keys), f32),
            pltpu.VMEM((QUESTIONS + 1, TGT, keys), f32),
            pltpu.VMEM((QUESTIONS + 1, TGT, keys), f32),
            pltpu.VMEM((QUESTIONS + 1, TGT, keys), f32),
            pltpu.VMEM((QUESTIONS + 1, TGT, keys), f32),
            pltpu.VMEM((QUESTIONS + 1, TGT, cols), f32),
            pltpu.VMEM((QUESTIONS + 1, 2 * TGT, cols), f32),
        ],
        compiler_params=pltpu.CompilerParams(vmem_limit_bytes=24 * 1024 * 1024),
        name="local_sums",
    )(owner, projected, far, rest, queries, cotangent)

    received = lax.all_to_all(payload, "psg", 0, 0, tiled=True)
    own_cotangent = lax.dynamic_slice_in_dim(cotangent, lax.axis_index("psg") * own, own, 0).astype(f32)
    finished = pl.pallas_call(
        final_kernel,
        out_shape=jax.ShapeDtypeStruct((rows, 2 * cols), bf16),
        in_specs=[vmem, vmem],
        out_specs=vmem,
        compiler_params=pltpu.CompilerParams(vmem_limit_bytes=24 * 1024 * 1024),
        name="final_sums",
    )(received, own_cotangent)
    outputs = lax.all_to_all(finished, "psg", 0, 0, tiled=True)
    return outputs[:, :cols], outputs[:, cols:]


def solution(mesh):
    placed = (
        P(None, ("pb", "rep")),
        P("psg", None, ("pb", "rep")),
        P("psg"),
        P(None, ("pb", "rep")),
        P(None, ("pb", "rep")),
        P(None, ("pb", "rep")),
    )
    return jax.shard_map(
        body,
        mesh=mesh,
        in_specs=placed,
        out_specs=(P(None, ("pb", "rep")), P(None, ("pb", "rep"))),
        check_vma=False,
    )
```

```python
import jax
import jax.numpy as jnp
from jax import lax
from jax.experimental import pallas as pl
from jax.experimental.pallas import tpu as pltpu
from jax.sharding import PartitionSpec as P

HDIM = 64
TGT = 32
PL = 32
QUESTIONS = 16
PARTS = 3

masked_value = -1e30

f32 = jnp.float32
bf16 = jnp.bfloat16
NT = (((1,), (1,)), ((), ()))


def split_parts(x):
    first = x.astype(bf16)
    rest = x - first.astype(f32)
    second = rest.astype(bf16)
    third = (rest - second.astype(f32)).astype(bf16)
    return first.astype(f32), second.astype(f32), third.astype(f32)


def per_head(x, width, reduce, fill):
    lane_head = lax.broadcasted_iota(jnp.int32, x.shape, x.ndim - 1) // width
    out = jnp.zeros_like(x)
    for head in range(x.shape[-1] // width):
        one = reduce(jnp.where(lane_head == head, x, fill), axis=-1, keepdims=True)
        out = jnp.where(lane_head == head, one, out)
    return out


def own_kernel(block_ref, x_ref, wk_ref, wv_ref, acc_ref, rest_ref):
    wide = x_ref.shape[1]
    cols = wk_ref.shape[1]
    for n in range(wk_ref.shape[0] // wide):
        at = pl.ds(pl.multiple_of(block_ref[n] * wide, wide), wide)
        for side, ref in enumerate((wk_ref, wv_ref)):
            columns = slice(side * cols, (side + 1) * cols)
            if n == 0:
                acc_ref[:, columns] = jnp.dot(x_ref[...], ref[at, :], preferred_element_type=f32)
            else:
                rest_ref[(n - 1) * wide : n * wide, columns] = ref[at, :]


def near_kernel(acc_ref, rest_ref, *refs):
    x_refs, out_ref = refs[:-1], refs[-1]
    weight = rest_ref[0 : len(x_refs) * x_refs[0].shape[1], :]
    chunk = 512
    for low in range(0, acc_ref.shape[0], chunk):
        rows = jnp.concatenate([x[low : low + chunk, :] for x in x_refs], axis=1)
        out_ref[low : low + chunk, :] = acc_ref[low : low + chunk, :] + jnp.dot(
            rows, weight, preferred_element_type=f32
        )


def local_kernel(owner_ref, acc_ref, *refs):
    (far_ref, rest_ref, q_ref, c_ref, out_ref, kblk, vblk, score, product, top, total, dots, corr, acc_v, acc_k) = refs
    slots = owner_ref.shape[0]
    half = slots // 2
    cols = q_ref.shape[1]
    heads = cols // HDIM
    keys = heads * PL

    top[...] = jnp.full_like(top, masked_value)
    total[...] = jnp.zeros_like(total)
    dots[...] = jnp.zeros_like(dots)
    acc_v[...] = jnp.zeros_like(acc_v)
    acc_k[...] = jnp.zeros_like(acc_k)

    on_diagonal = (
        lax.broadcasted_iota(jnp.int32, (keys, cols), 0) // PL
        == lax.broadcasted_iota(jnp.int32, (keys, cols), 1) // HDIM
    ).astype(f32).astype(bf16)

    for side in range(2):
        low = side * half * PL
        rows = far_ref[low : low + half * PL, :]
        projected = acc_ref[low : low + half * PL, :] + jnp.dot(
            rows, rest_ref[-rows.shape[1] :, :], preferred_element_type=f32
        )
        projected = projected.astype(bf16)
        for i in range(half):
            slot = side * half + i
            own = projected[i * PL : (i + 1) * PL]
            kb = jnp.concatenate([own[:, :cols]] * heads, axis=0) * on_diagonal
            vb = jnp.concatenate([own[:, cols:]] * heads, axis=0) * on_diagonal
            kblk[slot] = kb
            vblk[slot] = vb
            o = owner_ref[slot]
            at = pl.ds(pl.multiple_of(jnp.minimum(o, QUESTIONS - 1) * TGT, TGT), TGT)
            s = lax.dot_general(q_ref[at, :], kb, NT, preferred_element_type=f32)
            score[slot] = s
            product[slot] = lax.dot_general(c_ref[at, :], vb, NT, preferred_element_type=f32)
            top[o] = jnp.maximum(top[o], s)

    for q in range(QUESTIONS):
        top[q] = per_head(top[q], PL, jnp.max, masked_value)

    for slot in range(slots):
        o = owner_ref[slot]
        e = jnp.exp(score[slot] - top[o])
        score[slot] = e
        total[o] = total[o] + e
        dots[o] = dots[o] + e * product[slot]

    for q in range(QUESTIONS):
        t = per_head(total[q], PL, jnp.sum, 0.0)
        d = per_head(dots[q], PL, jnp.sum, 0.0)
        total[q] = t
        corr[q] = jnp.where(t > 0.0, d / jnp.where(t > 0.0, t, 1.0), 0.0)
    corr[QUESTIONS] = jnp.zeros_like(corr[QUESTIONS])

    for slot in range(slots):
        o = owner_ref[slot]
        e = score[slot]
        g = e * (product[slot] - corr[o])
        both = jnp.concatenate([e, g], axis=0).astype(bf16)
        acc_v[o] = acc_v[o] + jnp.dot(both[:TGT], vblk[slot], preferred_element_type=f32)
        acc_k[o] = acc_k[o] + jnp.dot(both, kblk[slot], preferred_element_type=f32)

    part = lax.broadcasted_iota(jnp.int32, (TGT, keys), 1) % PL
    for q in range(QUESTIONS):
        at = slice(q * TGT, (q + 1) * TGT)
        out_ref[at, 0:cols] = acc_v[q].astype(bf16)
        out_ref[at, cols : 2 * cols] = acc_k[q, TGT:, :].astype(bf16)
        out_ref[at, 2 * cols : 3 * cols] = acc_k[q, :TGT, :].astype(bf16)
        extra = jnp.zeros((TGT, keys), f32)
        pieces_of = split_parts(top[q]) + split_parts(total[q]) + split_parts(corr[q])
        for n, piece in enumerate(pieces_of):
            extra = jnp.where(part == n, piece, extra)
        out_ref[at, 3 * cols :] = extra.astype(bf16)


def final_kernel(r_ref, c_ref, out_ref):
    rows, cols = c_ref.shape
    heads = cols // HDIM
    keys = heads * PL
    devices = r_ref.shape[0] // rows
    lane = lax.broadcasted_iota(jnp.int32, (keys, 3 * cols), 0)
    spot = lax.broadcasted_iota(jnp.int32, (keys, 3 * cols), 1)
    pick = (lane // PL == (spot % cols) // HDIM) & ((lane % PL) // PARTS == spot // cols)
    pick = pick.astype(f32).astype(bf16)
    wide = jnp.dot(r_ref[:, 3 * cols :], pick, preferred_element_type=f32).reshape(devices, rows, 3 * cols)
    top = wide[:, :, 0:cols]
    weight = jnp.exp(top - jnp.max(top, axis=0, keepdims=True))
    total = jnp.sum(weight * wide[:, :, cols : 2 * cols], axis=0)

    def read(n):
        return r_ref[:, n * cols : (n + 1) * cols].astype(f32).reshape(devices, rows, cols)

    summed = jnp.sum(weight * read(0), axis=0)
    attended = (summed / total).astype(bf16).astype(f32)
    corr = per_head(c_ref[...] * attended, HDIM, jnp.sum, 0.0)
    shift = wide[:, :, 2 * cols :] - corr[None]
    grad = jnp.sum(weight * (read(1) + shift * read(2)), axis=0) / total
    both = jnp.concatenate([attended, grad], axis=1)
    two = jnp.concatenate([both, both], axis=0).astype(bf16)
    for n in range(devices // 2):
        out_ref[2 * rows * n : 2 * rows * (n + 1), :] = two


def swap(block):
    return lax.ppermute(block, "rep", [(0, 1), (1, 0)])


def block_numbers():
    n = lax.axis_size("pb")
    pb, rep = lax.axis_index("pb"), lax.axis_index("rep")
    step = 1 - 2 * rep
    own = [(pb + shift) % n for shift in (0, n - step, n + step, 2)]
    other = [(pb + shift) % n for shift in (0, n + step, n - step, 2)]
    numbers = [number for pair in zip(own, other) for number in (pair[0] * 2 + rep, pair[1] * 2 + 1 - rep)]
    return jnp.stack(numbers).astype(jnp.int32)


def along(block, way):
    n = lax.axis_size("pb")
    pairs = []
    for chip in range(n):
        pairs.append((chip * 2, (chip + way) % n * 2))
        pairs.append((chip * 2 + 1, (chip - way) % n * 2 + 1))
    return lax.ppermute(block, ("pb", "rep"), pairs)


def body(queries, prefixes, owner, key_weight, value_weight, cotangent):
    slots, vectors, features = prefixes.shape
    rows, cols = queries.shape
    heads = cols // HDIM
    keys = heads * PL
    devices = lax.axis_size("psg")
    own = rows // devices

    passages = prefixes.reshape(slots * vectors, features)
    ahead = along(passages, 1)
    smem = pl.BlockSpec(memory_space=pltpu.SMEM)
    vmem = pl.BlockSpec(memory_space=pltpu.VMEM)
    sums = jax.ShapeDtypeStruct((slots * vectors, 2 * cols), f32)
    projected, rest = pl.pallas_call(
        own_kernel,
        out_shape=(sums, jax.ShapeDtypeStruct((key_weight.shape[0] - features, 2 * cols), bf16)),
        in_specs=[smem] + [vmem] * 3,
        out_specs=(vmem, vmem),
        compiler_params=pltpu.CompilerParams(vmem_limit_bytes=16 * 1024 * 1024),
        name="own_projection",
    )(block_numbers(), passages, key_weight, value_weight)
    held, projected, rest = lax.optimization_barrier((passages, projected, rest))
    behind, other = along(held, -1), swap(held)
    far = along(ahead, 1)
    ahead_other = swap(ahead)
    far, ahead_other = lax.optimization_barrier((far, ahead_other))
    near = [other, ahead, ahead_other, behind, swap(behind), far]
    far = swap(far)
    projected = pl.pallas_call(
        near_kernel,
        out_shape=sums,
        in_specs=[vmem] * (2 + len(near)),
        out_specs=vmem,
        compiler_params=pltpu.CompilerParams(vmem_limit_bytes=16 * 1024 * 1024),
        name="near_projection",
    )(projected, rest, *near)
    payload = pl.pallas_call(
        local_kernel,
        out_shape=jax.ShapeDtypeStruct((rows, 3 * cols + keys), bf16),
        in_specs=[smem] + [vmem] * 5,
        out_specs=vmem,
        scratch_shapes=[
            pltpu.VMEM((slots, keys, cols), bf16),
            pltpu.VMEM((slots, keys, cols), bf16),
            pltpu.VMEM((slots, TGT, keys), f32),
            pltpu.VMEM((slots, TGT, keys), f32),
            pltpu.VMEM((QUESTIONS + 1, TGT, keys), f32),
            pltpu.VMEM((QUESTIONS + 1, TGT, keys), f32),
            pltpu.VMEM((QUESTIONS + 1, TGT, keys), f32),
            pltpu.VMEM((QUESTIONS + 1, TGT, keys), f32),
            pltpu.VMEM((QUESTIONS + 1, TGT, cols), f32),
            pltpu.VMEM((QUESTIONS + 1, 2 * TGT, cols), f32),
        ],
        compiler_params=pltpu.CompilerParams(vmem_limit_bytes=24 * 1024 * 1024),
        name="local_sums",
    )(owner, projected, far, rest, queries, cotangent)

    received = lax.all_to_all(payload, "psg", 0, 0, tiled=True)
    own_cotangent = lax.dynamic_slice_in_dim(cotangent, lax.axis_index("psg") * own, own, 0).astype(f32)
    finished = pl.pallas_call(
        final_kernel,
        out_shape=jax.ShapeDtypeStruct((rows, 2 * cols), bf16),
        in_specs=[vmem, vmem],
        out_specs=vmem,
        compiler_params=pltpu.CompilerParams(vmem_limit_bytes=24 * 1024 * 1024),
        name="final_sums",
    )(received, own_cotangent)
    outputs = lax.all_to_all(finished, "psg", 0, 0, tiled=True)
    return outputs[:, :cols], outputs[:, cols:]


def solution(mesh):
    placed = (
        P(None, ("pb", "rep")),
        P("psg", None, ("pb", "rep")),
        P("psg"),
        P(None, ("pb", "rep")),
        P(None, ("pb", "rep")),
        P(None, ("pb", "rep")),
    )
    return jax.shard_map(
        body,
        mesh=mesh,
        in_specs=placed,
        out_specs=(P(None, ("pb", "rep")), P(None, ("pb", "rep"))),
        check_vma=False,
    )
```

```python
import jax
import jax.numpy as jnp
from jax import lax
from jax.experimental import pallas as pl
from jax.experimental.pallas import tpu as pltpu
from jax.sharding import PartitionSpec as P

HDIM = 64
TGT = 32
PL = 32
QUESTIONS = 16
PARTS = 3

masked_value = -1e30

f32 = jnp.float32
bf16 = jnp.bfloat16
NT = (((1,), (1,)), ((), ()))


def split_parts(x):
    first = x.astype(bf16)
    rest = x - first.astype(f32)
    second = rest.astype(bf16)
    third = (rest - second.astype(f32)).astype(bf16)
    return first.astype(f32), second.astype(f32), third.astype(f32)


def per_head(x, width, reduce, fill):
    lane_head = lax.broadcasted_iota(jnp.int32, x.shape, x.ndim - 1) // width
    out = jnp.zeros_like(x)
    for head in range(x.shape[-1] // width):
        one = reduce(jnp.where(lane_head == head, x, fill), axis=-1, keepdims=True)
        out = jnp.where(lane_head == head, one, out)
    return out


def hold_kernel(x_ref, out_ref):
    out_ref[...] = x_ref[...]


def own_kernel(block_ref, x_ref, wk_ref, wv_ref, acc_ref, rest_ref):
    wide = x_ref.shape[1]
    cols = wk_ref.shape[1]
    for n in range(wk_ref.shape[0] // wide):
        at = pl.ds(pl.multiple_of(block_ref[n] * wide, wide), wide)
        for side, ref in enumerate((wk_ref, wv_ref)):
            columns = slice(side * cols, (side + 1) * cols)
            if n == 0:
                acc_ref[:, columns] = jnp.dot(x_ref[...], ref[at, :], preferred_element_type=f32)
            else:
                rest_ref[(n - 1) * wide : n * wide, columns] = ref[at, :]


def near_kernel(acc_ref, rest_ref, *refs):
    x_refs, out_ref = refs[:-1], refs[-1]
    weight = rest_ref[0 : len(x_refs) * x_refs[0].shape[1], :]
    chunk = 512
    for low in range(0, acc_ref.shape[0], chunk):
        rows = jnp.concatenate([x[low : low + chunk, :] for x in x_refs], axis=1)
        out_ref[low : low + chunk, :] = acc_ref[low : low + chunk, :] + jnp.dot(
            rows, weight, preferred_element_type=f32
        )


def local_kernel(owner_ref, acc_ref, *refs):
    (far_ref, rest_ref, q_ref, c_ref, out_ref, kblk, vblk, score, product, top, total, dots, corr, acc_v, acc_k) = refs
    slots = owner_ref.shape[0]
    half = slots // 2
    cols = q_ref.shape[1]
    heads = cols // HDIM
    keys = heads * PL

    top[...] = jnp.full_like(top, masked_value)
    total[...] = jnp.zeros_like(total)
    dots[...] = jnp.zeros_like(dots)
    acc_v[...] = jnp.zeros_like(acc_v)
    acc_k[...] = jnp.zeros_like(acc_k)

    on_diagonal = (
        lax.broadcasted_iota(jnp.int32, (keys, cols), 0) // PL
        == lax.broadcasted_iota(jnp.int32, (keys, cols), 1) // HDIM
    ).astype(f32).astype(bf16)

    for side in range(2):
        low = side * half * PL
        rows = far_ref[low : low + half * PL, :]
        projected = acc_ref[low : low + half * PL, :] + jnp.dot(
            rows, rest_ref[-rows.shape[1] :, :], preferred_element_type=f32
        )
        projected = projected.astype(bf16)
        for i in range(half):
            slot = side * half + i
            own = projected[i * PL : (i + 1) * PL]
            kb = jnp.concatenate([own[:, :cols]] * heads, axis=0) * on_diagonal
            vb = jnp.concatenate([own[:, cols:]] * heads, axis=0) * on_diagonal
            kblk[slot] = kb
            vblk[slot] = vb
            o = owner_ref[slot]
            at = pl.ds(pl.multiple_of(jnp.minimum(o, QUESTIONS - 1) * TGT, TGT), TGT)
            s = lax.dot_general(q_ref[at, :], kb, NT, preferred_element_type=f32)
            score[slot] = s
            product[slot] = lax.dot_general(c_ref[at, :], vb, NT, preferred_element_type=f32)
            top[o] = jnp.maximum(top[o], s)

    for q in range(QUESTIONS):
        top[q] = per_head(top[q], PL, jnp.max, masked_value)

    for slot in range(slots):
        o = owner_ref[slot]
        e = jnp.exp(score[slot] - top[o])
        score[slot] = e
        total[o] = total[o] + e
        dots[o] = dots[o] + e * product[slot]

    for q in range(QUESTIONS):
        t = per_head(total[q], PL, jnp.sum, 0.0)
        d = per_head(dots[q], PL, jnp.sum, 0.0)
        total[q] = t
        corr[q] = jnp.where(t > 0.0, d / jnp.where(t > 0.0, t, 1.0), 0.0)
    corr[QUESTIONS] = jnp.zeros_like(corr[QUESTIONS])

    for slot in range(slots):
        o = owner_ref[slot]
        e = score[slot]
        g = e * (product[slot] - corr[o])
        both = jnp.concatenate([e, g], axis=0).astype(bf16)
        acc_v[o] = acc_v[o] + jnp.dot(both[:TGT], vblk[slot], preferred_element_type=f32)
        acc_k[o] = acc_k[o] + jnp.dot(both, kblk[slot], preferred_element_type=f32)

    part = lax.broadcasted_iota(jnp.int32, (TGT, keys), 1) % PL
    for q in range(QUESTIONS):
        at = slice(q * TGT, (q + 1) * TGT)
        out_ref[at, 0:cols] = acc_v[q].astype(bf16)
        out_ref[at, cols : 2 * cols] = acc_k[q, TGT:, :].astype(bf16)
        out_ref[at, 2 * cols : 3 * cols] = acc_k[q, :TGT, :].astype(bf16)
        extra = jnp.zeros((TGT, keys), f32)
        pieces_of = split_parts(top[q]) + split_parts(total[q]) + split_parts(corr[q])
        for n, piece in enumerate(pieces_of):
            extra = jnp.where(part == n, piece, extra)
        out_ref[at, 3 * cols :] = extra.astype(bf16)


def final_kernel(r_ref, c_ref, out_ref):
    rows, cols = c_ref.shape
    heads = cols // HDIM
    keys = heads * PL
    devices = r_ref.shape[0] // rows
    lane = lax.broadcasted_iota(jnp.int32, (keys, 3 * cols), 0)
    spot = lax.broadcasted_iota(jnp.int32, (keys, 3 * cols), 1)
    pick = (lane // PL == (spot % cols) // HDIM) & ((lane % PL) // PARTS == spot // cols)
    pick = pick.astype(f32).astype(bf16)
    wide = jnp.dot(r_ref[:, 3 * cols :], pick, preferred_element_type=f32).reshape(devices, rows, 3 * cols)
    top = wide[:, :, 0:cols]
    weight = jnp.exp(top - jnp.max(top, axis=0, keepdims=True))
    total = jnp.sum(weight * wide[:, :, cols : 2 * cols], axis=0)

    def read(n):
        return r_ref[:, n * cols : (n + 1) * cols].astype(f32).reshape(devices, rows, cols)

    summed = jnp.sum(weight * read(0), axis=0)
    attended = (summed / total).astype(bf16).astype(f32)
    corr = per_head(c_ref[...] * attended, HDIM, jnp.sum, 0.0)
    shift = wide[:, :, 2 * cols :] - corr[None]
    grad = jnp.sum(weight * (read(1) + shift * read(2)), axis=0) / total
    both = jnp.concatenate([attended, grad], axis=1)
    two = jnp.concatenate([both, both], axis=0).astype(bf16)
    for n in range(devices // 2):
        out_ref[2 * rows * n : 2 * rows * (n + 1), :] = two


def swap(block):
    return lax.ppermute(block, "rep", [(0, 1), (1, 0)])


def block_numbers():
    n = lax.axis_size("pb")
    pb, rep = lax.axis_index("pb"), lax.axis_index("rep")
    step = 1 - 2 * rep
    own = [(pb + shift) % n for shift in (0, n - step, n + step, 2)]
    other = [(pb + shift) % n for shift in (0, n + step, n - step, 2)]
    numbers = [number for pair in zip(own, other) for number in (pair[0] * 2 + rep, pair[1] * 2 + 1 - rep)]
    return jnp.stack(numbers).astype(jnp.int32)


def along(block, way):
    n = lax.axis_size("pb")
    pairs = []
    for chip in range(n):
        pairs.append((chip * 2, (chip + way) % n * 2))
        pairs.append((chip * 2 + 1, (chip - way) % n * 2 + 1))
    return lax.ppermute(block, ("pb", "rep"), pairs)


def body(queries, prefixes, owner, key_weight, value_weight, cotangent):
    slots, vectors, features = prefixes.shape
    rows, cols = queries.shape
    heads = cols // HDIM
    keys = heads * PL
    devices = lax.axis_size("psg")
    own = rows // devices

    passages = prefixes.reshape(slots * vectors, features)
    ahead = along(passages, 1)
    smem = pl.BlockSpec(memory_space=pltpu.SMEM)
    vmem = pl.BlockSpec(memory_space=pltpu.VMEM)
    small = pltpu.CompilerParams(vmem_limit_bytes=16 * 1024 * 1024)
    held = pl.pallas_call(
        hold_kernel,
        out_shape=jax.ShapeDtypeStruct(passages.shape, bf16),
        in_specs=[vmem],
        out_specs=vmem,
        compiler_params=small,
        name="hold",
    )(passages)
    behind, other = along(held, -1), swap(held)
    far = along(ahead, 1)
    sums = jax.ShapeDtypeStruct((slots * vectors, 2 * cols), f32)
    projected, rest = pl.pallas_call(
        own_kernel,
        out_shape=(sums, jax.ShapeDtypeStruct((key_weight.shape[0] - features, 2 * cols), bf16)),
        in_specs=[smem] + [vmem] * 3,
        out_specs=(vmem, vmem),
        compiler_params=small,
        name="own_projection",
    )(block_numbers(), held, key_weight, value_weight)
    ahead_other = swap(ahead)
    far, ahead_other, projected, rest = lax.optimization_barrier((far, ahead_other, projected, rest))
    near = [other, ahead, ahead_other, behind, swap(behind), far]
    far = swap(far)
    projected = pl.pallas_call(
        near_kernel,
        out_shape=sums,
        in_specs=[vmem] * (2 + len(near)),
        out_specs=vmem,
        compiler_params=small,
        name="near_projection",
    )(projected, rest, *near)
    payload = pl.pallas_call(
        local_kernel,
        out_shape=jax.ShapeDtypeStruct((rows, 3 * cols + keys), bf16),
        in_specs=[smem] + [vmem] * 5,
        out_specs=vmem,
        scratch_shapes=[
            pltpu.VMEM((slots, keys, cols), bf16),
            pltpu.VMEM((slots, keys, cols), bf16),
            pltpu.VMEM((slots, TGT, keys), f32),
            pltpu.VMEM((slots, TGT, keys), f32),
            pltpu.VMEM((QUESTIONS + 1, TGT, keys), f32),
            pltpu.VMEM((QUESTIONS + 1, TGT, keys), f32),
            pltpu.VMEM((QUESTIONS + 1, TGT, keys), f32),
            pltpu.VMEM((QUESTIONS + 1, TGT, keys), f32),
            pltpu.VMEM((QUESTIONS + 1, TGT, cols), f32),
            pltpu.VMEM((QUESTIONS + 1, 2 * TGT, cols), f32),
        ],
        compiler_params=pltpu.CompilerParams(vmem_limit_bytes=24 * 1024 * 1024),
        name="local_sums",
    )(owner, projected, far, rest, queries, cotangent)

    received = lax.all_to_all(payload, "psg", 0, 0, tiled=True)
    own_cotangent = lax.dynamic_slice_in_dim(cotangent, lax.axis_index("psg") * own, own, 0).astype(f32)
    finished = pl.pallas_call(
        final_kernel,
        out_shape=jax.ShapeDtypeStruct((rows, 2 * cols), bf16),
        in_specs=[vmem, vmem],
        out_specs=vmem,
        compiler_params=pltpu.CompilerParams(vmem_limit_bytes=24 * 1024 * 1024),
        name="final_sums",
    )(received, own_cotangent)
    outputs = lax.all_to_all(finished, "psg", 0, 0, tiled=True)
    return outputs[:, :cols], outputs[:, cols:]


def solution(mesh):
    placed = (
        P(None, ("pb", "rep")),
        P("psg", None, ("pb", "rep")),
        P("psg"),
        P(None, ("pb", "rep")),
        P(None, ("pb", "rep")),
        P(None, ("pb", "rep")),
    )
    return jax.shard_map(
        body,
        mesh=mesh,
        in_specs=placed,
        out_specs=(P(None, ("pb", "rep")), P(None, ("pb", "rep"))),
        check_vma=False,
    )
```

```python
import jax
import jax.numpy as jnp
from jax import lax
from jax.experimental import pallas as pl
from jax.experimental.pallas import tpu as pltpu
from jax.sharding import PartitionSpec as P

HDIM = 64
TGT = 32
PL = 32
QUESTIONS = 16
PARTS = 3

masked_value = -1e30

f32 = jnp.float32
bf16 = jnp.bfloat16
NT = (((1,), (1,)), ((), ()))


def split_parts(x):
    first = x.astype(bf16)
    rest = x - first.astype(f32)
    second = rest.astype(bf16)
    third = (rest - second.astype(f32)).astype(bf16)
    return first.astype(f32), second.astype(f32), third.astype(f32)


def per_head(x, width, reduce, fill):
    lane_head = lax.broadcasted_iota(jnp.int32, x.shape, x.ndim - 1) // width
    out = jnp.zeros_like(x)
    for head in range(x.shape[-1] // width):
        one = reduce(jnp.where(lane_head == head, x, fill), axis=-1, keepdims=True)
        out = jnp.where(lane_head == head, one, out)
    return out


def block_rows(block_ref, n, wide):
    return pl.ds(pl.multiple_of(block_ref[n] * wide, wide), wide)


def reorder(block_ref, w_ref, rest_ref, wide):
    for n in range(1, w_ref.shape[0] // wide):
        rest_ref[(n - 1) * wide : n * wide, :] = w_ref[block_rows(block_ref, n, wide), :]


def own_kernel(block_ref, x_ref, wk_ref, keys_ref, rest_ref):
    wide = x_ref.shape[1]
    weight = wk_ref[block_rows(block_ref, 0, wide), :]
    keys_ref[...] = jnp.dot(x_ref[...], weight, preferred_element_type=f32)
    reorder(block_ref, wk_ref, rest_ref, wide)


def early_kernel(block_ref, keys_ref, rest_key_ref, x_ref, wv_ref, *refs):
    x_refs, out_ref, rest_ref = refs[:-2], refs[-2], refs[-1]
    wide = x_ref.shape[1]
    cols = wv_ref.shape[1]
    depth = len(x_refs) * wide
    reorder(block_ref, wv_ref, rest_ref, wide)
    chunk = 512
    for low in range(0, x_ref.shape[0], chunk):
        at = slice(low, low + chunk)
        rows = jnp.concatenate([x[at, :] for x in x_refs], axis=1)
        out_ref[at, :cols] = keys_ref[at, :] + jnp.dot(rows, rest_key_ref[:depth, :], preferred_element_type=f32)
        rows = jnp.concatenate([rows, x_ref[at, :]], axis=1)
        weight = jnp.concatenate([rest_ref[:depth, :], wv_ref[block_rows(block_ref, 0, wide), :]], axis=0)
        out_ref[at, cols:] = jnp.dot(rows, weight, preferred_element_type=f32)


def late_kernel(first, acc_ref, rest_key_ref, rest_value_ref, *refs):
    x_refs, out_ref = refs[:-1], refs[-1]
    at = slice(first, first + len(x_refs) * x_refs[0].shape[1])
    weight = jnp.concatenate([rest_key_ref[at, :], rest_value_ref[at, :]], axis=1)
    chunk = 512
    for low in range(0, acc_ref.shape[0], chunk):
        rows = jnp.concatenate([x[low : low + chunk, :] for x in x_refs], axis=1)
        out_ref[low : low + chunk, :] = acc_ref[low : low + chunk, :] + jnp.dot(
            rows, weight, preferred_element_type=f32
        )


def local_kernel(owner_ref, acc_ref, *refs):
    (far_ref, rest_key_ref, rest_value_ref, q_ref, c_ref, out_ref, kblk, vblk, score, product, top, total, dots, corr, acc_v, acc_k) = refs
    slots = owner_ref.shape[0]
    half = slots // 2
    cols = q_ref.shape[1]
    heads = cols // HDIM
    keys = heads * PL

    top[...] = jnp.full_like(top, masked_value)
    total[...] = jnp.zeros_like(total)
    dots[...] = jnp.zeros_like(dots)
    acc_v[...] = jnp.zeros_like(acc_v)
    acc_k[...] = jnp.zeros_like(acc_k)

    on_diagonal = (
        lax.broadcasted_iota(jnp.int32, (keys, cols), 0) // PL
        == lax.broadcasted_iota(jnp.int32, (keys, cols), 1) // HDIM
    ).astype(f32).astype(bf16)

    weight = jnp.concatenate([ref[-far_ref.shape[1] :, :] for ref in (rest_key_ref, rest_value_ref)], axis=1)
    for side in range(2):
        low = side * half * PL
        rows = far_ref[low : low + half * PL, :]
        projected = acc_ref[low : low + half * PL, :] + jnp.dot(rows, weight, preferred_element_type=f32)
        projected = projected.astype(bf16)
        for i in range(half):
            slot = side * half + i
            own = projected[i * PL : (i + 1) * PL]
            kb = jnp.concatenate([own[:, :cols]] * heads, axis=0) * on_diagonal
            vb = jnp.concatenate([own[:, cols:]] * heads, axis=0) * on_diagonal
            kblk[slot] = kb
            vblk[slot] = vb
            o = owner_ref[slot]
            at = pl.ds(pl.multiple_of(jnp.minimum(o, QUESTIONS - 1) * TGT, TGT), TGT)
            s = lax.dot_general(q_ref[at, :], kb, NT, preferred_element_type=f32)
            score[slot] = s
            product[slot] = lax.dot_general(c_ref[at, :], vb, NT, preferred_element_type=f32)
            top[o] = jnp.maximum(top[o], s)

    for q in range(QUESTIONS):
        top[q] = per_head(top[q], PL, jnp.max, masked_value)

    for slot in range(slots):
        o = owner_ref[slot]
        e = jnp.exp(score[slot] - top[o])
        score[slot] = e
        total[o] = total[o] + e
        dots[o] = dots[o] + e * product[slot]

    for q in range(QUESTIONS):
        t = per_head(total[q], PL, jnp.sum, 0.0)
        d = per_head(dots[q], PL, jnp.sum, 0.0)
        total[q] = t
        corr[q] = jnp.where(t > 0.0, d / jnp.where(t > 0.0, t, 1.0), 0.0)
    corr[QUESTIONS] = jnp.zeros_like(corr[QUESTIONS])

    for slot in range(slots):
        o = owner_ref[slot]
        e = score[slot]
        g = e * (product[slot] - corr[o])
        both = jnp.concatenate([e, g], axis=0).astype(bf16)
        acc_v[o] = acc_v[o] + jnp.dot(both[:TGT], vblk[slot], preferred_element_type=f32)
        acc_k[o] = acc_k[o] + jnp.dot(both, kblk[slot], preferred_element_type=f32)

    part = lax.broadcasted_iota(jnp.int32, (TGT, keys), 1) % PL
    for q in range(QUESTIONS):
        at = slice(q * TGT, (q + 1) * TGT)
        out_ref[at, 0:cols] = acc_v[q].astype(bf16)
        out_ref[at, cols : 2 * cols] = acc_k[q, TGT:, :].astype(bf16)
        out_ref[at, 2 * cols : 3 * cols] = acc_k[q, :TGT, :].astype(bf16)
        extra = jnp.zeros((TGT, keys), f32)
        pieces_of = split_parts(top[q]) + split_parts(total[q]) + split_parts(corr[q])
        for n, piece in enumerate(pieces_of):
            extra = jnp.where(part == n, piece, extra)
        out_ref[at, 3 * cols :] = extra.astype(bf16)


def final_kernel(r_ref, c_ref, out_ref):
    rows, cols = c_ref.shape
    heads = cols // HDIM
    keys = heads * PL
    devices = r_ref.shape[0] // rows
    lane = lax.broadcasted_iota(jnp.int32, (keys, 3 * cols), 0)
    spot = lax.broadcasted_iota(jnp.int32, (keys, 3 * cols), 1)
    pick = (lane // PL == (spot % cols) // HDIM) & ((lane % PL) // PARTS == spot // cols)
    pick = pick.astype(f32).astype(bf16)
    wide = jnp.dot(r_ref[:, 3 * cols :], pick, preferred_element_type=f32).reshape(devices, rows, 3 * cols)
    top = wide[:, :, 0:cols]
    weight = jnp.exp(top - jnp.max(top, axis=0, keepdims=True))
    total = jnp.sum(weight * wide[:, :, cols : 2 * cols], axis=0)

    def read(n):
        return r_ref[:, n * cols : (n + 1) * cols].astype(f32).reshape(devices, rows, cols)

    summed = jnp.sum(weight * read(0), axis=0)
    attended = (summed / total).astype(bf16).astype(f32)
    corr = per_head(c_ref[...] * attended, HDIM, jnp.sum, 0.0)
    shift = wide[:, :, 2 * cols :] - corr[None]
    grad = jnp.sum(weight * (read(1) + shift * read(2)), axis=0) / total
    both = jnp.concatenate([attended, grad], axis=1)
    two = jnp.concatenate([both, both], axis=0).astype(bf16)
    for n in range(devices // 2):
        out_ref[2 * rows * n : 2 * rows * (n + 1), :] = two


def swap(block):
    return lax.ppermute(block, "rep", [(0, 1), (1, 0)])


def block_numbers():
    n = lax.axis_size("pb")
    pb, rep = lax.axis_index("pb"), lax.axis_index("rep")
    step = 1 - 2 * rep
    own = [(pb + shift) % n for shift in (0, n - step, n + step, 2)]
    other = [(pb + shift) % n for shift in (0, n + step, n - step, 2)]
    numbers = [number for pair in zip(own, other) for number in (pair[0] * 2 + rep, pair[1] * 2 + 1 - rep)]
    return jnp.stack(numbers).astype(jnp.int32)


def along(block, way):
    n = lax.axis_size("pb")
    pairs = []
    for chip in range(n):
        pairs.append((chip * 2, (chip + way) % n * 2))
        pairs.append((chip * 2 + 1, (chip - way) % n * 2 + 1))
    return lax.ppermute(block, ("pb", "rep"), pairs)


def body(queries, prefixes, owner, key_weight, value_weight, cotangent):
    slots, vectors, features = prefixes.shape
    rows, cols = queries.shape
    heads = cols // HDIM
    keys = heads * PL
    devices = lax.axis_size("psg")
    own = rows // devices

    passages = prefixes.reshape(slots * vectors, features)
    smem = pl.BlockSpec(memory_space=pltpu.SMEM)
    vmem = pl.BlockSpec(memory_space=pltpu.VMEM)
    small = pltpu.CompilerParams(vmem_limit_bytes=16 * 1024 * 1024)
    count = slots * vectors
    sums = jax.ShapeDtypeStruct((count, 2 * cols), f32)
    rest_rows = jax.ShapeDtypeStruct((key_weight.shape[0] - features, cols), bf16)
    block = block_numbers()

    ahead = along(passages, 1)
    keys_sum, rest_key = pl.pallas_call(
        own_kernel,
        out_shape=(jax.ShapeDtypeStruct((count, cols), f32), rest_rows),
        in_specs=[smem] + [vmem] * 2,
        out_specs=(vmem, vmem),
        compiler_params=small,
        name="own_keys",
    )(block, passages, key_weight)
    held, keys_sum, rest_key = lax.optimization_barrier((passages, keys_sum, rest_key))
    behind, other = along(held, -1), swap(held)
    far = along(ahead, 1)
    ahead_other = swap(ahead)
    early = [other, ahead]
    projected, rest_value = pl.pallas_call(
        early_kernel,
        out_shape=(sums, rest_rows),
        in_specs=[smem] + [vmem] * (4 + len(early)),
        out_specs=(vmem, vmem),
        compiler_params=small,
        name="early_blocks",
    )(block, keys_sum, rest_key, held, value_weight, *early)
    far, ahead_other, projected, rest_value = lax.optimization_barrier((far, ahead_other, projected, rest_value))
    late = [ahead_other, behind, swap(behind), far]
    far = swap(far)
    projected = pl.pallas_call(
        lambda *refs: late_kernel(len(early) * features, *refs),
        out_shape=sums,
        in_specs=[vmem] * (3 + len(late)),
        out_specs=vmem,
        compiler_params=small,
        name="late_blocks",
    )(projected, rest_key, rest_value, *late)
    payload = pl.pallas_call(
        local_kernel,
        out_shape=jax.ShapeDtypeStruct((rows, 3 * cols + keys), bf16),
        in_specs=[smem] + [vmem] * 6,
        out_specs=vmem,
        scratch_shapes=[
            pltpu.VMEM((slots, keys, cols), bf16),
            pltpu.VMEM((slots, keys, cols), bf16),
            pltpu.VMEM((slots, TGT, keys), f32),
            pltpu.VMEM((slots, TGT, keys), f32),
            pltpu.VMEM((QUESTIONS + 1, TGT, keys), f32),
            pltpu.VMEM((QUESTIONS + 1, TGT, keys), f32),
            pltpu.VMEM((QUESTIONS + 1, TGT, keys), f32),
            pltpu.VMEM((QUESTIONS + 1, TGT, keys), f32),
            pltpu.VMEM((QUESTIONS + 1, TGT, cols), f32),
            pltpu.VMEM((QUESTIONS + 1, 2 * TGT, cols), f32),
        ],
        compiler_params=pltpu.CompilerParams(vmem_limit_bytes=24 * 1024 * 1024),
        name="local_sums",
    )(owner, projected, far, rest_key, rest_value, queries, cotangent)

    received = lax.all_to_all(payload, "psg", 0, 0, tiled=True)
    own_cotangent = lax.dynamic_slice_in_dim(cotangent, lax.axis_index("psg") * own, own, 0).astype(f32)
    finished = pl.pallas_call(
        final_kernel,
        out_shape=jax.ShapeDtypeStruct((rows, 2 * cols), bf16),
        in_specs=[vmem, vmem],
        out_specs=vmem,
        compiler_params=pltpu.CompilerParams(vmem_limit_bytes=24 * 1024 * 1024),
        name="final_sums",
    )(received, own_cotangent)
    outputs = lax.all_to_all(finished, "psg", 0, 0, tiled=True)
    return outputs[:, :cols], outputs[:, cols:]


def solution(mesh):
    placed = (
        P(None, ("pb", "rep")),
        P("psg", None, ("pb", "rep")),
        P("psg"),
        P(None, ("pb", "rep")),
        P(None, ("pb", "rep")),
        P(None, ("pb", "rep")),
    )
    return jax.shard_map(
        body,
        mesh=mesh,
        in_specs=placed,
        out_specs=(P(None, ("pb", "rep")), P(None, ("pb", "rep"))),
        check_vma=False,
    )
```

```python
import jax
import jax.numpy as jnp
from jax import lax
from jax.experimental import pallas as pl
from jax.experimental.pallas import tpu as pltpu
from jax.sharding import PartitionSpec as P

HDIM = 64
TGT = 32
PL = 32
QUESTIONS = 16
PARTS = 3
ROWS_EACH = 8

masked_value = -1e30

f32 = jnp.float32
bf16 = jnp.bfloat16
NT = (((1,), (1,)), ((), ()))


def split_parts(x):
    first = x.astype(bf16)
    rest = x - first.astype(f32)
    second = rest.astype(bf16)
    third = (rest - second.astype(f32)).astype(bf16)
    return first.astype(f32), second.astype(f32), third.astype(f32)


def per_head(x, width, reduce, fill):
    lane_head = lax.broadcasted_iota(jnp.int32, x.shape, x.ndim - 1) // width
    out = jnp.zeros_like(x)
    for head in range(x.shape[-1] // width):
        one = reduce(jnp.where(lane_head == head, x, fill), axis=-1, keepdims=True)
        out = jnp.where(lane_head == head, one, out)
    return out


def block_rows(block_ref, n, wide):
    return pl.ds(pl.multiple_of(block_ref[n] * wide, wide), wide)


def reorder(block_ref, w_ref, rest_ref, wide):
    for n in range(1, w_ref.shape[0] // wide):
        rest_ref[(n - 1) * wide : n * wide, :] = w_ref[block_rows(block_ref, n, wide), :]


def own_kernel(block_ref, x_ref, wk_ref, keys_ref, rest_ref):
    wide = x_ref.shape[1]
    weight = wk_ref[block_rows(block_ref, 0, wide), :]
    keys_ref[...] = jnp.dot(x_ref[...], weight, preferred_element_type=f32)
    reorder(block_ref, wk_ref, rest_ref, wide)


def early_kernel(block_ref, keys_ref, rest_key_ref, x_ref, wv_ref, *refs):
    x_refs, out_ref, rest_ref = refs[:-2], refs[-2], refs[-1]
    wide = x_ref.shape[1]
    cols = wv_ref.shape[1]
    depth = len(x_refs) * wide
    reorder(block_ref, wv_ref, rest_ref, wide)
    chunk = 512
    for low in range(0, x_ref.shape[0], chunk):
        at = slice(low, low + chunk)
        rows = jnp.concatenate([x[at, :] for x in x_refs], axis=1)
        out_ref[at, :cols] = keys_ref[at, :] + jnp.dot(rows, rest_key_ref[:depth, :], preferred_element_type=f32)
        rows = jnp.concatenate([rows, x_ref[at, :]], axis=1)
        weight = jnp.concatenate([rest_ref[:depth, :], wv_ref[block_rows(block_ref, 0, wide), :]], axis=0)
        out_ref[at, cols:] = jnp.dot(rows, weight, preferred_element_type=f32)


def late_kernel(first, acc_ref, rest_key_ref, rest_value_ref, *refs):
    x_refs, out_ref = refs[:-1], refs[-1]
    at = slice(first, first + len(x_refs) * x_refs[0].shape[1])
    weight = jnp.concatenate([rest_key_ref[at, :], rest_value_ref[at, :]], axis=1)
    chunk = 512
    for low in range(0, acc_ref.shape[0], chunk):
        rows = jnp.concatenate([x[low : low + chunk, :] for x in x_refs], axis=1)
        out_ref[low : low + chunk, :] = acc_ref[low : low + chunk, :] + jnp.dot(
            rows, weight, preferred_element_type=f32
        )


def local_kernel(owner_ref, acc_ref, *refs):
    (far_ref, rest_key_ref, rest_value_ref, q_ref, c_ref, out_ref, kblk, vblk, score, product, top, total, dots, corr, acc_v, acc_k) = refs
    slots = owner_ref.shape[0]
    half = slots // 2
    cols = q_ref.shape[1]
    heads = cols // HDIM
    keys = heads * PL

    top[...] = jnp.full_like(top, masked_value)
    total[...] = jnp.zeros_like(total)
    dots[...] = jnp.zeros_like(dots)
    acc_v[...] = jnp.zeros_like(acc_v)
    acc_k[...] = jnp.zeros_like(acc_k)

    on_diagonal = (
        lax.broadcasted_iota(jnp.int32, (keys, cols), 0) // PL
        == lax.broadcasted_iota(jnp.int32, (keys, cols), 1) // HDIM
    ).astype(f32).astype(bf16)

    weight = jnp.concatenate([ref[-far_ref.shape[1] :, :] for ref in (rest_key_ref, rest_value_ref)], axis=1)
    for side in range(2):
        low = side * half * PL
        rows = far_ref[low : low + half * PL, :]
        projected = acc_ref[low : low + half * PL, :] + jnp.dot(rows, weight, preferred_element_type=f32)
        projected = projected.astype(bf16)
        for i in range(half):
            slot = side * half + i
            own = projected[i * PL : (i + 1) * PL]
            kb = jnp.concatenate([own[:, :cols]] * heads, axis=0) * on_diagonal
            vb = jnp.concatenate([own[:, cols:]] * heads, axis=0) * on_diagonal
            kblk[slot] = kb
            vblk[slot] = vb
            o = owner_ref[slot]
            at = pl.ds(pl.multiple_of(jnp.minimum(o, QUESTIONS - 1) * TGT, TGT), TGT)
            s = lax.dot_general(q_ref[at, :], kb, NT, preferred_element_type=f32)
            score[slot] = s
            product[slot] = lax.dot_general(c_ref[at, :], vb, NT, preferred_element_type=f32)
            top[o] = jnp.maximum(top[o], s)

    for q in range(QUESTIONS):
        top[q] = per_head(top[q], PL, jnp.max, masked_value)

    for slot in range(slots):
        o = owner_ref[slot]
        e = jnp.exp(score[slot] - top[o])
        score[slot] = e
        total[o] = total[o] + e
        dots[o] = dots[o] + e * product[slot]

    for q in range(QUESTIONS):
        t = per_head(total[q], PL, jnp.sum, 0.0)
        d = per_head(dots[q], PL, jnp.sum, 0.0)
        total[q] = t
        corr[q] = jnp.where(t > 0.0, d / jnp.where(t > 0.0, t, 1.0), 0.0)
    corr[QUESTIONS] = jnp.zeros_like(corr[QUESTIONS])

    for slot in range(slots):
        o = owner_ref[slot]
        e = score[slot]
        g = e * (product[slot] - corr[o])
        both = jnp.concatenate([e, g], axis=0).astype(bf16)
        acc_v[o] = acc_v[o] + jnp.dot(both[:TGT], vblk[slot], preferred_element_type=f32)
        acc_k[o] = acc_k[o] + jnp.dot(both, kblk[slot], preferred_element_type=f32)

    part = lax.broadcasted_iota(jnp.int32, (TGT, keys), 1) % PL
    for q in range(QUESTIONS):
        at = slice(q * TGT, (q + 1) * TGT)
        out_ref[at, 0:cols] = acc_v[q].astype(bf16)
        out_ref[at, cols : 2 * cols] = acc_k[q, TGT:, :].astype(bf16)
        out_ref[at, 2 * cols : 3 * cols] = acc_k[q, :TGT, :].astype(bf16)
        extra = jnp.zeros((TGT, keys), f32)
        pieces_of = split_parts(top[q]) + split_parts(total[q]) + split_parts(corr[q])
        for n, piece in enumerate(pieces_of):
            extra = jnp.where(part == n, piece, extra)
        out_ref[at, 3 * cols :] = extra.astype(bf16)


def final_kernel(block_ref, r_ref, c_ref, out_ref):
    cols = c_ref.shape[1]
    heads = cols // HDIM
    keys = heads * PL
    rows = ROWS_EACH
    devices = r_ref.shape[0] // rows
    place = block_ref[block_ref.shape[0] - 1]
    pair = c_ref[pl.ds(pl.multiple_of((place >> 1) * 2 * rows, 2 * rows), 2 * rows), :].astype(f32)
    cotangent = jnp.where((place & 1) == 1, pair[rows:], pair[:rows])
    lane = lax.broadcasted_iota(jnp.int32, (keys, 3 * cols), 0)
    spot = lax.broadcasted_iota(jnp.int32, (keys, 3 * cols), 1)
    pick = (lane // PL == (spot % cols) // HDIM) & ((lane % PL) // PARTS == spot // cols)
    pick = pick.astype(f32).astype(bf16)
    wide = jnp.dot(r_ref[:, 3 * cols :], pick, preferred_element_type=f32).reshape(devices, rows, 3 * cols)
    top = wide[:, :, 0:cols]
    weight = jnp.exp(top - jnp.max(top, axis=0, keepdims=True))
    total = jnp.sum(weight * wide[:, :, cols : 2 * cols], axis=0)

    def read(n):
        return r_ref[:, n * cols : (n + 1) * cols].astype(f32).reshape(devices, rows, cols)

    summed = jnp.sum(weight * read(0), axis=0)
    attended = (summed / total).astype(bf16).astype(f32)
    corr = per_head(cotangent * attended, HDIM, jnp.sum, 0.0)
    shift = wide[:, :, 2 * cols :] - corr[None]
    grad = jnp.sum(weight * (read(1) + shift * read(2)), axis=0) / total
    both = jnp.concatenate([attended, grad], axis=1)
    two = jnp.concatenate([both, both], axis=0).astype(bf16)
    for n in range(devices // 2):
        out_ref[2 * rows * n : 2 * rows * (n + 1), :] = two


def swap(block):
    return lax.ppermute(block, "rep", [(0, 1), (1, 0)])


def block_numbers():
    n = lax.axis_size("pb")
    pb, rep = lax.axis_index("pb"), lax.axis_index("rep")
    step = 1 - 2 * rep
    own = [(pb + shift) % n for shift in (0, n - step, n + step, 2)]
    other = [(pb + shift) % n for shift in (0, n + step, n - step, 2)]
    numbers = [number for pair in zip(own, other) for number in (pair[0] * 2 + rep, pair[1] * 2 + 1 - rep)]
    return jnp.stack(numbers + [lax.axis_index("psg")]).astype(jnp.int32)


def along(block, way):
    n = lax.axis_size("pb")
    pairs = []
    for chip in range(n):
        pairs.append((chip * 2, (chip + way) % n * 2))
        pairs.append((chip * 2 + 1, (chip - way) % n * 2 + 1))
    return lax.ppermute(block, ("pb", "rep"), pairs)


def body(queries, prefixes, owner, key_weight, value_weight, cotangent):
    slots, vectors, features = prefixes.shape
    rows, cols = queries.shape
    heads = cols // HDIM
    keys = heads * PL
    devices = lax.axis_size("psg")
    assert rows == ROWS_EACH * devices

    passages = prefixes.reshape(slots * vectors, features)
    smem = pl.BlockSpec(memory_space=pltpu.SMEM)
    vmem = pl.BlockSpec(memory_space=pltpu.VMEM)
    small = pltpu.CompilerParams(vmem_limit_bytes=16 * 1024 * 1024)
    count = slots * vectors
    sums = jax.ShapeDtypeStruct((count, 2 * cols), f32)
    rest_rows = jax.ShapeDtypeStruct((key_weight.shape[0] - features, cols), bf16)
    block = block_numbers()

    ahead = along(passages, 1)
    keys_sum, rest_key = pl.pallas_call(
        own_kernel,
        out_shape=(jax.ShapeDtypeStruct((count, cols), f32), rest_rows),
        in_specs=[smem] + [vmem] * 2,
        out_specs=(vmem, vmem),
        compiler_params=small,
        name="own_keys",
    )(block, passages, key_weight)
    held, keys_sum, rest_key = lax.optimization_barrier((passages, keys_sum, rest_key))
    behind, other = along(held, -1), swap(held)
    far = along(ahead, 1)
    ahead_other = swap(ahead)
    early = [other, ahead]
    projected, rest_value = pl.pallas_call(
        early_kernel,
        out_shape=(sums, rest_rows),
        in_specs=[smem] + [vmem] * (4 + len(early)),
        out_specs=(vmem, vmem),
        compiler_params=small,
        name="early_blocks",
    )(block, keys_sum, rest_key, held, value_weight, *early)
    far, ahead_other, projected, rest_value = lax.optimization_barrier((far, ahead_other, projected, rest_value))
    late = [ahead_other, behind, swap(behind), far]
    far = swap(far)
    projected = pl.pallas_call(
        lambda *refs: late_kernel(len(early) * features, *refs),
        out_shape=sums,
        in_specs=[vmem] * (3 + len(late)),
        out_specs=vmem,
        compiler_params=small,
        name="late_blocks",
    )(projected, rest_key, rest_value, *late)
    payload = pl.pallas_call(
        local_kernel,
        out_shape=jax.ShapeDtypeStruct((rows, 3 * cols + keys), bf16),
        in_specs=[smem] + [vmem] * 6,
        out_specs=vmem,
        scratch_shapes=[
            pltpu.VMEM((slots, keys, cols), bf16),
            pltpu.VMEM((slots, keys, cols), bf16),
            pltpu.VMEM((slots, TGT, keys), f32),
            pltpu.VMEM((slots, TGT, keys), f32),
            pltpu.VMEM((QUESTIONS + 1, TGT, keys), f32),
            pltpu.VMEM((QUESTIONS + 1, TGT, keys), f32),
            pltpu.VMEM((QUESTIONS + 1, TGT, keys), f32),
            pltpu.VMEM((QUESTIONS + 1, TGT, keys), f32),
            pltpu.VMEM((QUESTIONS + 1, TGT, cols), f32),
            pltpu.VMEM((QUESTIONS + 1, 2 * TGT, cols), f32),
        ],
        compiler_params=pltpu.CompilerParams(vmem_limit_bytes=24 * 1024 * 1024),
        name="local_sums",
    )(owner, projected, far, rest_key, rest_value, queries, cotangent)

    received = lax.all_to_all(payload, "psg", 0, 0, tiled=True)
    finished = pl.pallas_call(
        final_kernel,
        out_shape=jax.ShapeDtypeStruct((rows, 2 * cols), bf16),
        in_specs=[smem, vmem, vmem],
        out_specs=vmem,
        compiler_params=pltpu.CompilerParams(vmem_limit_bytes=24 * 1024 * 1024),
        name="final_sums",
    )(block, received, cotangent)
    outputs = lax.all_to_all(finished, "psg", 0, 0, tiled=True)
    return outputs[:, :cols], outputs[:, cols:]


def solution(mesh):
    placed = (
        P(None, ("pb", "rep")),
        P("psg", None, ("pb", "rep")),
        P("psg"),
        P(None, ("pb", "rep")),
        P(None, ("pb", "rep")),
        P(None, ("pb", "rep")),
    )
    return jax.shard_map(
        body,
        mesh=mesh,
        in_specs=placed,
        out_specs=(P(None, ("pb", "rep")), P(None, ("pb", "rep"))),
        check_vma=False,
    )
```

```python
import jax
import jax.numpy as jnp
import numpy as np
from jax import lax
from jax.experimental import pallas as pl
from jax.experimental.pallas import tpu as pltpu
from jax.sharding import PartitionSpec as P

HDIM = 64
TGT = 32
PL = 32
QUESTIONS = 16
PARTS = 3
SIDE = 8
ROWS_EACH = 8

masked_value = -1e30

f32 = jnp.float32
bf16 = jnp.bfloat16
NT = (((1,), (1,)), ((), ()))


def split_parts(x):
    first = x.astype(bf16)
    rest = x - first.astype(f32)
    second = rest.astype(bf16)
    third = (rest - second.astype(f32)).astype(bf16)
    return first.astype(f32), second.astype(f32), third.astype(f32)


def per_head(x, width, reduce, fill):
    lane_head = lax.broadcasted_iota(jnp.int32, x.shape, x.ndim - 1) // width
    out = jnp.zeros_like(x)
    for head in range(x.shape[-1] // width):
        one = reduce(jnp.where(lane_head == head, x, fill), axis=-1, keepdims=True)
        out = jnp.where(lane_head == head, one, out)
    return out


def block_rows(block_ref, n, wide):
    return pl.ds(pl.multiple_of(block_ref[n] * wide, wide), wide)


def reorder(block_ref, w_ref, rest_ref, wide):
    for n in range(1, w_ref.shape[0] // wide):
        rest_ref[(n - 1) * wide : n * wide, :] = w_ref[block_rows(block_ref, n, wide), :]


def own_kernel(block_ref, x_ref, wk_ref, keys_ref, rest_ref):
    wide = x_ref.shape[1]
    weight = wk_ref[block_rows(block_ref, 0, wide), :]
    keys_ref[...] = jnp.dot(x_ref[...], weight, preferred_element_type=f32)
    reorder(block_ref, wk_ref, rest_ref, wide)


def early_kernel(block_ref, keys_ref, rest_key_ref, x_ref, wv_ref, c_ref, *refs):
    x_refs, out_ref, rest_ref, own_ref = refs[:-3], refs[-3], refs[-2], refs[-1]
    place = block_ref[block_ref.shape[0] - 1]
    count = own_ref.shape[0]
    pair = c_ref[pl.ds(pl.multiple_of((place >> 1) * 2 * count, 2 * count), 2 * count), :].astype(f32)
    own_ref[...] = jnp.where((place & 1) == 1, pair[count:], pair[:count])
    wide = x_ref.shape[1]
    cols = wv_ref.shape[1]
    depth = len(x_refs) * wide
    reorder(block_ref, wv_ref, rest_ref, wide)
    chunk = 512
    for low in range(0, x_ref.shape[0], chunk):
        at = slice(low, low + chunk)
        rows = jnp.concatenate([x[at, :] for x in x_refs], axis=1)
        out_ref[at, :cols] = keys_ref[at, :] + jnp.dot(rows, rest_key_ref[:depth, :], preferred_element_type=f32)
        rows = jnp.concatenate([rows, x_ref[at, :]], axis=1)
        weight = jnp.concatenate([rest_ref[:depth, :], wv_ref[block_rows(block_ref, 0, wide), :]], axis=0)
        out_ref[at, cols:] = jnp.dot(rows, weight, preferred_element_type=f32)


def late_kernel(first, acc_ref, rest_key_ref, rest_value_ref, *refs):
    x_refs, out_ref = refs[:-1], refs[-1]
    at = slice(first, first + len(x_refs) * x_refs[0].shape[1])
    weight = jnp.concatenate([rest_key_ref[at, :], rest_value_ref[at, :]], axis=1)
    chunk = 512
    for low in range(0, acc_ref.shape[0], chunk):
        rows = jnp.concatenate([x[low : low + chunk, :] for x in x_refs], axis=1)
        out_ref[low : low + chunk, :] = acc_ref[low : low + chunk, :] + jnp.dot(
            rows, weight, preferred_element_type=f32
        )


def local_kernel(owner_ref, acc_ref, *refs):
    (far_ref, rest_key_ref, rest_value_ref, q_ref, c_ref, out_ref, kblk, vblk, score, product, top, total, dots, corr, acc_v, acc_k) = refs
    slots = owner_ref.shape[0]
    half = slots // 2
    cols = q_ref.shape[1]
    heads = cols // HDIM
    keys = heads * PL

    top[...] = jnp.full_like(top, masked_value)
    total[...] = jnp.zeros_like(total)
    dots[...] = jnp.zeros_like(dots)
    acc_v[...] = jnp.zeros_like(acc_v)
    acc_k[...] = jnp.zeros_like(acc_k)

    on_diagonal = (
        lax.broadcasted_iota(jnp.int32, (keys, cols), 0) // PL
        == lax.broadcasted_iota(jnp.int32, (keys, cols), 1) // HDIM
    ).astype(f32).astype(bf16)

    weight = jnp.concatenate([ref[-far_ref.shape[1] :, :] for ref in (rest_key_ref, rest_value_ref)], axis=1)
    for side in range(2):
        low = side * half * PL
        rows = far_ref[low : low + half * PL, :]
        projected = acc_ref[low : low + half * PL, :] + jnp.dot(rows, weight, preferred_element_type=f32)
        projected = projected.astype(bf16)
        for i in range(half):
            slot = side * half + i
            own = projected[i * PL : (i + 1) * PL]
            kb = jnp.concatenate([own[:, :cols]] * heads, axis=0) * on_diagonal
            vb = jnp.concatenate([own[:, cols:]] * heads, axis=0) * on_diagonal
            kblk[slot] = kb
            vblk[slot] = vb
            o = owner_ref[slot]
            at = pl.ds(pl.multiple_of(jnp.minimum(o, QUESTIONS - 1) * TGT, TGT), TGT)
            s = lax.dot_general(q_ref[at, :], kb, NT, preferred_element_type=f32)
            score[slot] = s
            product[slot] = lax.dot_general(c_ref[at, :], vb, NT, preferred_element_type=f32)
            top[o] = jnp.maximum(top[o], s)

    for q in range(QUESTIONS):
        top[q] = per_head(top[q], PL, jnp.max, masked_value)

    for slot in range(slots):
        o = owner_ref[slot]
        e = jnp.exp(score[slot] - top[o])
        score[slot] = e
        total[o] = total[o] + e
        dots[o] = dots[o] + e * product[slot]

    for q in range(QUESTIONS):
        t = per_head(total[q], PL, jnp.sum, 0.0)
        d = per_head(dots[q], PL, jnp.sum, 0.0)
        total[q] = t
        corr[q] = jnp.where(t > 0.0, d / jnp.where(t > 0.0, t, 1.0), 0.0)
    corr[QUESTIONS] = jnp.zeros_like(corr[QUESTIONS])

    for slot in range(slots):
        o = owner_ref[slot]
        e = score[slot]
        g = e * (product[slot] - corr[o])
        both = jnp.concatenate([e, g], axis=0).astype(bf16)
        acc_v[o] = acc_v[o] + jnp.dot(both[:TGT], vblk[slot], preferred_element_type=f32)
        acc_k[o] = acc_k[o] + jnp.dot(both, kblk[slot], preferred_element_type=f32)

    for q in range(QUESTIONS):
        at = slice(q * TGT, (q + 1) * TGT)
        out_ref[at, 0:cols] = acc_v[q].astype(bf16)
        out_ref[at, cols : 2 * cols] = acc_k[q, TGT:, :].astype(bf16)
        out_ref[at, 2 * cols : 3 * cols] = acc_k[q, :TGT, :].astype(bf16)
        out_ref[at, 3 * cols :] = pack((top[q], total[q], corr[q]))


def spread(extra, cols):
    keys = extra.shape[1]
    heads = keys // PL
    lane = lax.broadcasted_iota(jnp.int32, (keys, 3 * cols), 0)
    spot = lax.broadcasted_iota(jnp.int32, (keys, 3 * cols), 1)
    pick = (lane // PL == (spot % cols) // (cols // heads)) & ((lane % PL) // PARTS == spot // cols)
    wide = jnp.dot(extra, pick.astype(f32).astype(bf16), preferred_element_type=f32)
    return [wide[:, n * cols : (n + 1) * cols] for n in range(3)]


def pack(values):
    part = lax.broadcasted_iota(jnp.int32, values[0].shape, 1) % PL
    out = jnp.zeros_like(values[0])
    for n, piece in enumerate([piece for value in values for piece in split_parts(value)]):
        out = jnp.where(part == n, piece, out)
    return out.astype(bf16)


def merge(extra, cols, rows):
    top, total, corr = [x.reshape(-1, rows, cols) for x in spread(extra, cols)]
    high = jnp.max(top, axis=0)
    scale = jnp.exp(top - high[None])
    sums = jnp.sum(scale * total, axis=0)
    dots = jnp.sum(scale * total * corr, axis=0)
    mean = jnp.where(sums > 0.0, dots / jnp.where(sums > 0.0, sums, 1.0), 0.0)
    return scale, corr, high, sums, mean


def merge_kernel(r_ref, out_ref):
    rows = out_ref.shape[0]
    keys = r_ref.shape[1] % 256
    cols = (r_ref.shape[1] - keys) // 3
    extra = r_ref[:, 3 * cols :]

    def read(n):
        return r_ref[:, n * cols : (n + 1) * cols].astype(f32).reshape(-1, rows, cols)

    scale, corr, _, _, mean = merge(extra, cols, rows)
    out_ref[:, 0:cols] = jnp.sum(scale * read(0), axis=0).astype(bf16)
    low = scale * read(2)
    grad = jnp.sum(scale * read(1) + (corr - mean[None]) * low, axis=0)
    out_ref[:, cols : 2 * cols] = grad.astype(bf16)
    out_ref[:, 2 * cols : 3 * cols] = jnp.sum(low, axis=0).astype(bf16)
    out_ref[:, 3 * cols :] = pack(merge(extra, keys, rows)[2:])


def final_kernel(r_ref, c_ref, out_ref):
    rows, cols = c_ref.shape
    scale, own, _, total, _ = merge(r_ref[:, 3 * cols :], cols, rows)

    def read(n):
        return r_ref[:, n * cols : (n + 1) * cols].astype(f32).reshape(-1, rows, cols)

    summed = jnp.sum(scale * read(0), axis=0)
    attended = (summed / total).astype(bf16).astype(f32)
    corr = per_head(c_ref[...] * attended, HDIM, jnp.sum, 0.0)
    grad = jnp.sum(scale * (read(1) + (own - corr[None]) * read(2)), axis=0) / total
    both = jnp.concatenate([attended, grad], axis=1)
    two = jnp.concatenate([both, both], axis=0).astype(bf16)
    for n in range(out_ref.shape[0] // (2 * rows)):
        out_ref[2 * rows * n : 2 * rows * (n + 1), :] = two


def swap(block):
    return lax.ppermute(block, "rep", [(0, 1), (1, 0)])


def block_numbers():
    n = lax.axis_size("pb")
    pb, rep = lax.axis_index("pb"), lax.axis_index("rep")
    step = 1 - 2 * rep
    own = [(pb + shift) % n for shift in (0, n - step, n + step, 2)]
    other = [(pb + shift) % n for shift in (0, n + step, n - step, 2)]
    numbers = [number for pair in zip(own, other) for number in (pair[0] * 2 + rep, pair[1] * 2 + 1 - rep)]
    place = lax.axis_index("psg")
    first, second = place // SIDE, place % SIDE
    row_block = jnp.where(rep == 0, second, first) * SIDE + jnp.where(rep == 0, first, second)
    return jnp.stack(numbers + [row_block]).astype(jnp.int32)


def along(block, way):
    n = lax.axis_size("pb")
    pairs = []
    for chip in range(n):
        pairs.append((chip * 2, (chip + way) % n * 2))
        pairs.append((chip * 2 + 1, (chip - way) % n * 2 + 1))
    return lax.ppermute(block, ("pb", "rep"), pairs)


AXES = ("psg", "pb", "rep")


def line_groups(mesh_shape, turn):
    side = SIDE
    assert side * side == mesh_shape[0]
    ids = np.arange(np.prod(mesh_shape)).reshape((side, side) + tuple(mesh_shape[1:]))
    groups = []
    for core in range(mesh_shape[2]):
        along = (core + turn + 1) % 2
        lines = np.moveaxis(ids[:, :, :, core], along, -1)
        groups += lines.reshape(-1, side).tolist()
    return groups


def plane_groups(mesh_shape):
    ids = np.arange(np.prod(mesh_shape)).reshape((SIDE, SIDE) + tuple(mesh_shape[1:]))
    groups = []
    for core in range(mesh_shape[2]):
        plane = ids[:, :, :, core]
        plane = np.moveaxis(plane, 2, 0) if core else np.transpose(plane, (2, 1, 0))
        groups += plane.reshape(mesh_shape[1], -1).tolist()
    return groups


def exchange(x, groups):
    return lax.all_to_all(x, AXES, 0, 0, axis_index_groups=groups, tiled=True)


def body(queries, prefixes, owner, key_weight, value_weight, cotangent):
    slots, vectors, features = prefixes.shape
    rows, cols = queries.shape
    heads = cols // HDIM
    keys = heads * PL
    devices = lax.axis_size("psg")
    assert rows == ROWS_EACH * devices

    passages = prefixes.reshape(slots * vectors, features)
    smem = pl.BlockSpec(memory_space=pltpu.SMEM)
    vmem = pl.BlockSpec(memory_space=pltpu.VMEM)
    small = pltpu.CompilerParams(vmem_limit_bytes=16 * 1024 * 1024)
    count = slots * vectors
    sums = jax.ShapeDtypeStruct((count, 2 * cols), f32)
    rest_rows = jax.ShapeDtypeStruct((key_weight.shape[0] - features, cols), bf16)
    block = block_numbers()

    ahead = along(passages, 1)
    keys_sum, rest_key = pl.pallas_call(
        own_kernel,
        out_shape=(jax.ShapeDtypeStruct((count, cols), f32), rest_rows),
        in_specs=[smem] + [vmem] * 2,
        out_specs=(vmem, vmem),
        compiler_params=small,
        name="own_keys",
    )(block, passages, key_weight)
    held, keys_sum, rest_key = lax.optimization_barrier((passages, keys_sum, rest_key))
    behind, other = along(held, -1), swap(held)
    far = along(ahead, 1)
    ahead_other = swap(ahead)
    early = [other, ahead]
    projected, rest_value, own_cotangent = pl.pallas_call(
        early_kernel,
        out_shape=(sums, rest_rows, jax.ShapeDtypeStruct((ROWS_EACH, cols), f32)),
        in_specs=[smem] + [vmem] * (5 + len(early)),
        out_specs=(vmem, vmem, vmem),
        compiler_params=small,
        name="early_blocks",
    )(block, keys_sum, rest_key, held, value_weight, cotangent, *early)
    far, ahead_other, projected, rest_value = lax.optimization_barrier((far, ahead_other, projected, rest_value))
    late = [ahead_other, behind, swap(behind), far]
    far = swap(far)
    projected = pl.pallas_call(
        lambda *refs: late_kernel(len(early) * features, *refs),
        out_shape=sums,
        in_specs=[vmem] * (3 + len(late)),
        out_specs=vmem,
        compiler_params=small,
        name="late_blocks",
    )(projected, rest_key, rest_value, *late)
    payload = pl.pallas_call(
        local_kernel,
        out_shape=jax.ShapeDtypeStruct((rows, 3 * cols + keys), bf16),
        in_specs=[smem] + [vmem] * 6,
        out_specs=vmem,
        scratch_shapes=[
            pltpu.VMEM((slots, keys, cols), bf16),
            pltpu.VMEM((slots, keys, cols), bf16),
            pltpu.VMEM((slots, TGT, keys), f32),
            pltpu.VMEM((slots, TGT, keys), f32),
            pltpu.VMEM((QUESTIONS + 1, TGT, keys), f32),
            pltpu.VMEM((QUESTIONS + 1, TGT, keys), f32),
            pltpu.VMEM((QUESTIONS + 1, TGT, keys), f32),
            pltpu.VMEM((QUESTIONS + 1, TGT, keys), f32),
            pltpu.VMEM((QUESTIONS + 1, TGT, cols), f32),
            pltpu.VMEM((QUESTIONS + 1, 2 * TGT, cols), f32),
        ],
        compiler_params=pltpu.CompilerParams(vmem_limit_bytes=24 * 1024 * 1024),
        name="local_sums",
    )(owner, projected, far, rest_key, rest_value, queries, cotangent)

    shape = tuple(lax.axis_size(name) for name in AXES)
    first_lines, second_lines = line_groups(shape, 0), line_groups(shape, 1)
    merged = pl.pallas_call(
        merge_kernel,
        out_shape=jax.ShapeDtypeStruct((rows // SIDE, payload.shape[1]), bf16),
        in_specs=[vmem],
        out_specs=vmem,
        compiler_params=pltpu.CompilerParams(vmem_limit_bytes=24 * 1024 * 1024),
        name="line_sums",
    )(exchange(payload, first_lines))
    received = exchange(merged, second_lines)
    finished = pl.pallas_call(
        final_kernel,
        out_shape=jax.ShapeDtypeStruct((rows, 2 * cols), bf16),
        in_specs=[vmem, vmem],
        out_specs=vmem,
        compiler_params=pltpu.CompilerParams(vmem_limit_bytes=24 * 1024 * 1024),
        name="final_sums",
    )(received, own_cotangent)
    outputs = exchange(finished, plane_groups(shape))
    return outputs[:, :cols], outputs[:, cols:]


def solution(mesh):
    placed = (
        P(None, ("pb", "rep")),
        P("psg", None, ("pb", "rep")),
        P("psg"),
        P(None, ("pb", "rep")),
        P(None, ("pb", "rep")),
        P(None, ("pb", "rep")),
    )
    return jax.shard_map(
        body,
        mesh=mesh,
        in_specs=placed,
        out_specs=(P(None, ("pb", "rep")), P(None, ("pb", "rep"))),
        check_vma=False,
    )
```

```python
import jax
import jax.numpy as jnp
import numpy as np
from jax import lax
from jax.experimental import pallas as pl
from jax.experimental.pallas import tpu as pltpu
from jax.sharding import PartitionSpec as P

HDIM = 64
TGT = 32
PL = 32
QUESTIONS = 16
PARTS = 3
SIDE = 8
LANES = 8
PACKED = 16
CHUNK = 400
ROWS_EACH = 8

masked_value = -1e30

f32 = jnp.float32
bf16 = jnp.bfloat16
NT = (((1,), (1,)), ((), ()))


def split_parts(x, count=PARTS):
    parts = []
    for _ in range(count):
        parts.append(x.astype(bf16).astype(f32))
        x = x - parts[-1]
    return parts


def two_parts(x):
    first, second = split_parts(x, 2)
    return first + second


def per_head(x, width, reduce, fill):
    lane_head = lax.broadcasted_iota(jnp.int32, x.shape, x.ndim - 1) // width
    out = jnp.zeros_like(x)
    for head in range(x.shape[-1] // width):
        one = reduce(jnp.where(lane_head == head, x, fill), axis=-1, keepdims=True)
        out = jnp.where(lane_head == head, one, out)
    return out


def block_rows(block_ref, n, wide):
    return pl.ds(pl.multiple_of(block_ref[n] * wide, wide), wide)


def reorder(block_ref, w_ref, rest_ref, wide):
    for n in range(1, w_ref.shape[0] // wide):
        rest_ref[(n - 1) * wide : n * wide, :] = w_ref[block_rows(block_ref, n, wide), :]


def own_kernel(block_ref, x_ref, wk_ref, keys_ref, rest_ref):
    wide = x_ref.shape[1]
    weight = wk_ref[block_rows(block_ref, 0, wide), :]
    keys_ref[...] = jnp.dot(x_ref[...], weight, preferred_element_type=f32)
    reorder(block_ref, wk_ref, rest_ref, wide)


def early_kernel(block_ref, keys_ref, rest_key_ref, x_ref, wv_ref, c_ref, *refs):
    x_refs, out_ref, rest_ref, own_ref = refs[:-3], refs[-3], refs[-2], refs[-1]
    place = block_ref[block_ref.shape[0] - 1]
    count = own_ref.shape[0]
    pair = c_ref[pl.ds(pl.multiple_of((place >> 1) * 2 * count, 2 * count), 2 * count), :].astype(f32)
    own_ref[...] = jnp.where((place & 1) == 1, pair[count:], pair[:count])
    wide = x_ref.shape[1]
    cols = wv_ref.shape[1]
    depth = len(x_refs) * wide
    reorder(block_ref, wv_ref, rest_ref, wide)
    chunk = 512
    for low in range(0, x_ref.shape[0], chunk):
        at = slice(low, low + chunk)
        rows = jnp.concatenate([x[at, :] for x in x_refs], axis=1)
        out_ref[at, :cols] = keys_ref[at, :] + jnp.dot(rows, rest_key_ref[:depth, :], preferred_element_type=f32)
        rows = jnp.concatenate([rows, x_ref[at, :]], axis=1)
        weight = jnp.concatenate([rest_ref[:depth, :], wv_ref[block_rows(block_ref, 0, wide), :]], axis=0)
        out_ref[at, cols:] = jnp.dot(rows, weight, preferred_element_type=f32)


def late_kernel(first, acc_ref, rest_key_ref, rest_value_ref, *refs):
    x_refs, out_ref = refs[:-1], refs[-1]
    at = slice(first, first + len(x_refs) * x_refs[0].shape[1])
    weight = jnp.concatenate([rest_key_ref[at, :], rest_value_ref[at, :]], axis=1)
    chunk = 512
    for low in range(0, acc_ref.shape[0], chunk):
        rows = jnp.concatenate([x[low : low + chunk, :] for x in x_refs], axis=1)
        out_ref[low : low + chunk, :] = acc_ref[low : low + chunk, :] + jnp.dot(
            rows, weight, preferred_element_type=f32
        )


def local_kernel(owner_ref, acc_ref, *refs):
    (far_ref, rest_key_ref, rest_value_ref, q_ref, c_ref, out_ref, kblk, vblk, score, product, top, total, dots, corr, acc_v, acc_k) = refs
    slots = owner_ref.shape[0]
    half = slots // 2
    cols = q_ref.shape[1]
    heads = cols // HDIM
    keys = heads * PL

    top[...] = jnp.full_like(top, masked_value)
    total[...] = jnp.zeros_like(total)
    dots[...] = jnp.zeros_like(dots)
    acc_v[...] = jnp.zeros_like(acc_v)
    acc_k[...] = jnp.zeros_like(acc_k)

    on_diagonal = (
        lax.broadcasted_iota(jnp.int32, (keys, cols), 0) // PL
        == lax.broadcasted_iota(jnp.int32, (keys, cols), 1) // HDIM
    ).astype(f32).astype(bf16)

    weight = jnp.concatenate([ref[-far_ref.shape[1] :, :] for ref in (rest_key_ref, rest_value_ref)], axis=1)
    for side in range(2):
        low = side * half * PL
        rows = far_ref[low : low + half * PL, :]
        projected = acc_ref[low : low + half * PL, :] + jnp.dot(rows, weight, preferred_element_type=f32)
        projected = projected.astype(bf16)
        for i in range(half):
            slot = side * half + i
            own = projected[i * PL : (i + 1) * PL]
            kb = jnp.concatenate([own[:, :cols]] * heads, axis=0) * on_diagonal
            vb = jnp.concatenate([own[:, cols:]] * heads, axis=0) * on_diagonal
            kblk[slot] = kb
            vblk[slot] = vb
            o = owner_ref[slot]
            at = pl.ds(pl.multiple_of(jnp.minimum(o, QUESTIONS - 1) * TGT, TGT), TGT)
            s = lax.dot_general(q_ref[at, :], kb, NT, preferred_element_type=f32)
            score[slot] = s
            product[slot] = lax.dot_general(c_ref[at, :], vb, NT, preferred_element_type=f32)
            top[o] = jnp.maximum(top[o], s)

    for q in range(QUESTIONS):
        top[q] = per_head(top[q], PL, jnp.max, masked_value)

    for slot in range(slots):
        o = owner_ref[slot]
        e = jnp.exp(score[slot] - top[o])
        score[slot] = e
        total[o] = total[o] + e
        dots[o] = dots[o] + e * product[slot]

    for q in range(QUESTIONS):
        t = per_head(total[q], PL, jnp.sum, 0.0)
        d = per_head(dots[q], PL, jnp.sum, 0.0)
        total[q] = t
        corr[q] = two_parts(jnp.where(t > 0.0, d / jnp.where(t > 0.0, t, 1.0), 0.0))
    corr[QUESTIONS] = jnp.zeros_like(corr[QUESTIONS])

    for slot in range(slots):
        o = owner_ref[slot]
        e = score[slot]
        g = e * (product[slot] - corr[o])
        both = jnp.concatenate([e, g], axis=0).astype(bf16)
        acc_v[o] = acc_v[o] + jnp.dot(both[:TGT], vblk[slot], preferred_element_type=f32)
        acc_k[o] = acc_k[o] + jnp.dot(both, kblk[slot], preferred_element_type=f32)

    segment = lax.broadcasted_iota(jnp.int32, (PACKED, keys), 1) % PL
    for block in range(QUESTIONS // 2):
        extras = []
        for side in range(2):
            q = 2 * block + side
            sums = jnp.concatenate([acc_v[q], acc_k[q, TGT:, :], acc_k[q, :TGT, :]], axis=1).astype(bf16)
            for n in range(sums.shape[1] // keys):
                low = block * CHUNK + (2 * n + side) * TGT
                out_ref[low : low + TGT, :] = sums[:, n * keys : (n + 1) * keys]
            extras.append(pack(top[q], total[q], corr[q]))
        quarters = [extra[low : low + PACKED] for extra in extras for low in range(0, TGT, PACKED)]
        packed = quarters[0]
        for n in range(1, len(quarters)):
            packed = jnp.where(segment // LANES == n, pltpu.roll(quarters[n], n * LANES, 1), packed)
        out_ref[(block + 1) * CHUNK - PACKED : (block + 1) * CHUNK, :] = packed.astype(bf16)


def spread(extra, cols):
    keys = extra.shape[1]
    heads = keys // PL
    lane = lax.broadcasted_iota(jnp.int32, (keys, 3 * cols), 0)
    spot = lax.broadcasted_iota(jnp.int32, (keys, 3 * cols), 1)
    pick = (lane // PL == (spot % cols) // (cols // heads)) & ((lane % PL) // PARTS == spot // cols)
    pick = pick & (lane % PL < LANES)
    wide = jnp.dot(extra, pick.astype(f32).astype(bf16), preferred_element_type=f32)
    return [wide[:, n * cols : (n + 1) * cols] for n in range(3)]


def pack(top, total, corr):
    part = lax.broadcasted_iota(jnp.int32, top.shape, 1) % PL
    out = jnp.zeros_like(top)
    for n, piece in enumerate(split_parts(top) + split_parts(total) + split_parts(corr, 2)):
        out = jnp.where(part == n, piece, out)
    return out


def merge(extra, cols, rows):
    top, total, corr = [x.reshape(-1, rows, cols) for x in spread(extra, cols)]
    high = jnp.max(top, axis=0)
    scale = jnp.exp(top - high[None])
    sums = jnp.sum(scale * total, axis=0)
    dots = jnp.sum(scale * total * corr, axis=0)
    mean = two_parts(jnp.where(sums > 0.0, dots / jnp.where(sums > 0.0, sums, 1.0), 0.0))
    return scale, corr, high, sums, mean


def merge_kernel(r_ref, out_ref):
    rows = out_ref.shape[0]
    keys = r_ref.shape[1]
    cols = (out_ref.shape[1] - keys) // 3
    starts = range(0, r_ref.shape[0], CHUNK)
    extras = []
    for start in starts:
        packed = r_ref[start + CHUNK - PACKED : start + CHUNK, :]
        extras.append(packed)
        for n in range(1, rows // PACKED):
            extras.append(pltpu.roll(packed.astype(f32), keys - n * LANES, 1).astype(bf16))
    extra = jnp.concatenate(extras, axis=0)

    def read(n):
        each = []
        for start in starts:
            lows = [start + (n * cols // keys + part) * rows for part in range(cols // keys)]
            each.append(jnp.concatenate([r_ref[low : low + rows, :].astype(f32) for low in lows], axis=1))
        return jnp.stack(each)

    scale, corr, _, _, mean = merge(extra, cols, rows)
    out_ref[:, 0:cols] = jnp.sum(scale * read(0), axis=0).astype(bf16)
    low = scale * read(2)
    grad = jnp.sum(scale * read(1) + (corr - mean[None]) * low, axis=0)
    out_ref[:, cols : 2 * cols] = grad.astype(bf16)
    out_ref[:, 2 * cols : 3 * cols] = jnp.sum(low, axis=0).astype(bf16)
    out_ref[:, 3 * cols :] = pack(*merge(extra, keys, rows)[2:]).astype(bf16)


def final_kernel(r_ref, c_ref, out_ref):
    rows, cols = c_ref.shape
    scale, own, _, total, _ = merge(r_ref[:, 3 * cols :], cols, rows)

    def read(n):
        return r_ref[:, n * cols : (n + 1) * cols].astype(f32).reshape(-1, rows, cols)

    summed = jnp.sum(scale * read(0), axis=0)
    attended = (summed / total).astype(bf16).astype(f32)
    corr = per_head(c_ref[...] * attended, HDIM, jnp.sum, 0.0)
    grad = jnp.sum(scale * (read(1) + (own - corr[None]) * read(2)), axis=0) / total
    both = jnp.concatenate([attended, grad], axis=1)
    two = jnp.concatenate([both, both], axis=0).astype(bf16)
    for n in range(out_ref.shape[0] // (2 * rows)):
        out_ref[2 * rows * n : 2 * rows * (n + 1), :] = two


def swap(block):
    return lax.ppermute(block, "rep", [(0, 1), (1, 0)])


def block_numbers():
    n = lax.axis_size("pb")
    pb, rep = lax.axis_index("pb"), lax.axis_index("rep")
    step = 1 - 2 * rep
    own = [(pb + shift) % n for shift in (0, n - step, n + step, 2)]
    other = [(pb + shift) % n for shift in (0, n + step, n - step, 2)]
    numbers = [number for pair in zip(own, other) for number in (pair[0] * 2 + rep, pair[1] * 2 + 1 - rep)]
    place = lax.axis_index("psg")
    first, second = place // SIDE, place % SIDE
    row_block = jnp.where(rep == 0, second, first) * SIDE + jnp.where(rep == 0, first, second)
    return jnp.stack(numbers + [row_block]).astype(jnp.int32)


def along(block, way):
    n = lax.axis_size("pb")
    pairs = []
    for chip in range(n):
        pairs.append((chip * 2, (chip + way) % n * 2))
        pairs.append((chip * 2 + 1, (chip - way) % n * 2 + 1))
    return lax.ppermute(block, ("pb", "rep"), pairs)


AXES = ("psg", "pb", "rep")


def line_groups(mesh_shape, turn):
    side = SIDE
    assert side * side == mesh_shape[0]
    ids = np.arange(np.prod(mesh_shape)).reshape((side, side) + tuple(mesh_shape[1:]))
    groups = []
    for core in range(mesh_shape[2]):
        along = (core + turn + 1) % 2
        lines = np.moveaxis(ids[:, :, :, core], along, -1)
        groups += lines.reshape(-1, side).tolist()
    return groups


def plane_groups(mesh_shape):
    ids = np.arange(np.prod(mesh_shape)).reshape((SIDE, SIDE) + tuple(mesh_shape[1:]))
    groups = []
    for core in range(mesh_shape[2]):
        plane = ids[:, :, :, core]
        plane = np.moveaxis(plane, 2, 0) if core else np.transpose(plane, (2, 1, 0))
        groups += plane.reshape(mesh_shape[1], -1).tolist()
    return groups


def exchange(x, groups):
    return lax.all_to_all(x, AXES, 0, 0, axis_index_groups=groups, tiled=True)


def body(queries, prefixes, owner, key_weight, value_weight, cotangent):
    slots, vectors, features = prefixes.shape
    rows, cols = queries.shape
    heads = cols // HDIM
    keys = heads * PL
    devices = lax.axis_size("psg")
    assert rows == ROWS_EACH * devices

    passages = prefixes.reshape(slots * vectors, features)
    smem = pl.BlockSpec(memory_space=pltpu.SMEM)
    vmem = pl.BlockSpec(memory_space=pltpu.VMEM)
    small = pltpu.CompilerParams(vmem_limit_bytes=16 * 1024 * 1024)
    count = slots * vectors
    sums = jax.ShapeDtypeStruct((count, 2 * cols), f32)
    rest_rows = jax.ShapeDtypeStruct((key_weight.shape[0] - features, cols), bf16)
    block = block_numbers()

    ahead = along(passages, 1)
    keys_sum, rest_key = pl.pallas_call(
        own_kernel,
        out_shape=(jax.ShapeDtypeStruct((count, cols), f32), rest_rows),
        in_specs=[smem] + [vmem] * 2,
        out_specs=(vmem, vmem),
        compiler_params=small,
        name="own_keys",
    )(block, passages, key_weight)
    held, keys_sum, rest_key = lax.optimization_barrier((passages, keys_sum, rest_key))
    behind, other = along(held, -1), swap(held)
    far = along(ahead, 1)
    ahead_other = swap(ahead)
    early = [other, ahead]
    projected, rest_value, own_cotangent = pl.pallas_call(
        early_kernel,
        out_shape=(sums, rest_rows, jax.ShapeDtypeStruct((ROWS_EACH, cols), f32)),
        in_specs=[smem] + [vmem] * (5 + len(early)),
        out_specs=(vmem, vmem, vmem),
        compiler_params=small,
        name="early_blocks",
    )(block, keys_sum, rest_key, held, value_weight, cotangent, *early)
    far, ahead_other, projected, rest_value = lax.optimization_barrier((far, ahead_other, projected, rest_value))
    late = [ahead_other, behind, swap(behind), far]
    far = swap(far)
    projected = pl.pallas_call(
        lambda *refs: late_kernel(len(early) * features, *refs),
        out_shape=sums,
        in_specs=[vmem] * (3 + len(late)),
        out_specs=vmem,
        compiler_params=small,
        name="late_blocks",
    )(projected, rest_key, rest_value, *late)
    payload = pl.pallas_call(
        local_kernel,
        out_shape=jax.ShapeDtypeStruct((SIDE * CHUNK, keys), bf16),
        in_specs=[smem] + [vmem] * 6,
        out_specs=vmem,
        scratch_shapes=[
            pltpu.VMEM((slots, keys, cols), bf16),
            pltpu.VMEM((slots, keys, cols), bf16),
            pltpu.VMEM((slots, TGT, keys), f32),
            pltpu.VMEM((slots, TGT, keys), f32),
            pltpu.VMEM((QUESTIONS + 1, TGT, keys), f32),
            pltpu.VMEM((QUESTIONS + 1, TGT, keys), f32),
            pltpu.VMEM((QUESTIONS + 1, TGT, keys), f32),
            pltpu.VMEM((QUESTIONS + 1, TGT, keys), f32),
            pltpu.VMEM((QUESTIONS + 1, TGT, cols), f32),
            pltpu.VMEM((QUESTIONS + 1, 2 * TGT, cols), f32),
        ],
        compiler_params=pltpu.CompilerParams(vmem_limit_bytes=24 * 1024 * 1024),
        name="local_sums",
    )(owner, projected, far, rest_key, rest_value, queries, cotangent)

    shape = tuple(lax.axis_size(name) for name in AXES)
    first_lines, second_lines = line_groups(shape, 0), line_groups(shape, 1)
    merged = pl.pallas_call(
        merge_kernel,
        out_shape=jax.ShapeDtypeStruct((rows // SIDE, 3 * cols + keys), bf16),
        in_specs=[vmem],
        out_specs=vmem,
        compiler_params=pltpu.CompilerParams(vmem_limit_bytes=24 * 1024 * 1024),
        name="line_sums",
    )(exchange(payload, first_lines))
    received = exchange(merged, second_lines)
    finished = pl.pallas_call(
        final_kernel,
        out_shape=jax.ShapeDtypeStruct((rows, 2 * cols), bf16),
        in_specs=[vmem, vmem],
        out_specs=vmem,
        compiler_params=pltpu.CompilerParams(vmem_limit_bytes=24 * 1024 * 1024),
        name="final_sums",
    )(received, own_cotangent)
    outputs = exchange(finished, plane_groups(shape))
    return outputs[:, :cols], outputs[:, cols:]


def solution(mesh):
    placed = (
        P(None, ("pb", "rep")),
        P("psg", None, ("pb", "rep")),
        P("psg"),
        P(None, ("pb", "rep")),
        P(None, ("pb", "rep")),
        P(None, ("pb", "rep")),
    )
    return jax.shard_map(
        body,
        mesh=mesh,
        in_specs=placed,
        out_specs=(P(None, ("pb", "rep")), P(None, ("pb", "rep"))),
        check_vma=False,
    )
```

```python
import jax
import jax.numpy as jnp
import numpy as np
from jax import lax
from jax.experimental import pallas as pl
from jax.experimental.pallas import tpu as pltpu
from jax.sharding import PartitionSpec as P

HDIM = 64
TGT = 32
PL = 32
QUESTIONS = 16
PARTS = 3
SIDE = 8
LANES = 8
PACKED = 16
CHUNK = 400
ROWS_EACH = 8

masked_value = -1e30

f32 = jnp.float32
bf16 = jnp.bfloat16
NT = (((1,), (1,)), ((), ()))


def split_parts(x, count=PARTS):
    parts = []
    for _ in range(count):
        parts.append(x.astype(bf16).astype(f32))
        x = x - parts[-1]
    return parts


def two_parts(x):
    first, second = split_parts(x, 2)
    return first + second


def per_head(x, width, reduce, fill):
    lane_head = lax.broadcasted_iota(jnp.int32, x.shape, x.ndim - 1) // width
    out = jnp.zeros_like(x)
    for head in range(x.shape[-1] // width):
        one = reduce(jnp.where(lane_head == head, x, fill), axis=-1, keepdims=True)
        out = jnp.where(lane_head == head, one, out)
    return out


def block_rows(block_ref, n, wide):
    return pl.ds(pl.multiple_of(block_ref[n] * wide, wide), wide)


def reorder(block_ref, w_ref, rest_ref, wide):
    for n in range(1, w_ref.shape[0] // wide):
        rest_ref[(n - 1) * wide : n * wide, :] = w_ref[block_rows(block_ref, n, wide), :]


def own_kernel(block_ref, x_ref, wk_ref, keys_ref, rest_ref):
    wide = x_ref.shape[1]
    weight = wk_ref[block_rows(block_ref, 0, wide), :]
    keys_ref[...] = jnp.dot(x_ref[...], weight, preferred_element_type=f32)
    reorder(block_ref, wk_ref, rest_ref, wide)


def early_kernel(block_ref, keys_ref, rest_key_ref, x_ref, wv_ref, c_ref, *refs):
    x_refs, out_ref, rest_ref, own_ref = refs[:-3], refs[-3], refs[-2], refs[-1]
    place = block_ref[block_ref.shape[0] - 1]
    count = own_ref.shape[0]
    pair = c_ref[pl.ds(pl.multiple_of((place >> 1) * 2 * count, 2 * count), 2 * count), :].astype(f32)
    own_ref[...] = jnp.where((place & 1) == 1, pair[count:], pair[:count])
    wide = x_ref.shape[1]
    cols = wv_ref.shape[1]
    depth = len(x_refs) * wide
    reorder(block_ref, wv_ref, rest_ref, wide)
    chunk = 512
    for low in range(0, x_ref.shape[0], chunk):
        at = slice(low, low + chunk)
        rows = jnp.concatenate([x[at, :] for x in x_refs], axis=1)
        out_ref[at, :cols] = keys_ref[at, :] + jnp.dot(rows, rest_key_ref[:depth, :], preferred_element_type=f32)
        rows = jnp.concatenate([rows, x_ref[at, :]], axis=1)
        weight = jnp.concatenate([rest_ref[:depth, :], wv_ref[block_rows(block_ref, 0, wide), :]], axis=0)
        out_ref[at, cols:] = jnp.dot(rows, weight, preferred_element_type=f32)


def late_kernel(first, acc_ref, rest_key_ref, rest_value_ref, *refs):
    x_refs, out_ref = refs[:-1], refs[-1]
    at = slice(first, first + len(x_refs) * x_refs[0].shape[1])
    weight = jnp.concatenate([rest_key_ref[at, :], rest_value_ref[at, :]], axis=1)
    chunk = 512
    for low in range(0, acc_ref.shape[0], chunk):
        rows = jnp.concatenate([x[low : low + chunk, :] for x in x_refs], axis=1)
        out_ref[low : low + chunk, :] = acc_ref[low : low + chunk, :] + jnp.dot(
            rows, weight, preferred_element_type=f32
        )


def local_kernel(owner_ref, acc_ref, *refs):
    (far_ref, rest_key_ref, rest_value_ref, q_ref, c_ref, out_ref, kblk, vblk, score, product, top, total, dots, corr, acc_v, acc_k) = refs
    slots = owner_ref.shape[0]
    cols = q_ref.shape[1]
    heads = cols // HDIM
    keys = heads * PL

    top[...] = jnp.full_like(top, masked_value)
    total[...] = jnp.zeros_like(total)
    dots[...] = jnp.zeros_like(dots)
    acc_v[...] = jnp.zeros_like(acc_v)
    acc_k[...] = jnp.zeros_like(acc_k)

    on_diagonal = (
        lax.broadcasted_iota(jnp.int32, (keys, cols), 0) // PL
        == lax.broadcasted_iota(jnp.int32, (keys, cols), 1) // HDIM
    ).astype(f32).astype(bf16)

    weight = jnp.concatenate([ref[-far_ref.shape[1] :, :] for ref in (rest_key_ref, rest_value_ref)], axis=1)
    rows = far_ref[...]
    projected = acc_ref[...] + jnp.dot(rows, weight, preferred_element_type=f32)
    projected = projected.astype(bf16)
    for slot in range(slots):
        own = projected[slot * PL : (slot + 1) * PL]
        kb = jnp.concatenate([own[:, :cols]] * heads, axis=0) * on_diagonal
        vb = jnp.concatenate([own[:, cols:]] * heads, axis=0) * on_diagonal
        kblk[slot] = kb
        vblk[slot] = vb
    for slot in range(0, slots, 2):
        owners = [owner_ref[slot + n] for n in range(2)]
        ats = [pl.ds(pl.multiple_of(jnp.minimum(o, QUESTIONS - 1) * TGT, TGT), TGT) for o in owners]

        def both_ways(rows_ref, block_ref):
            rows = jnp.concatenate([rows_ref[at, :] for at in ats], axis=0)
            blocks = jnp.concatenate([block_ref[slot], block_ref[slot + 1]], axis=0)
            return lax.dot_general(rows, blocks, NT, preferred_element_type=f32)

        s = both_ways(q_ref, kblk)
        p = both_ways(c_ref, vblk)
        for n, o in enumerate(owners):
            part = s[n * TGT : (n + 1) * TGT, n * keys : (n + 1) * keys]
            score[slot + n] = part
            product[slot + n] = p[n * TGT : (n + 1) * TGT, n * keys : (n + 1) * keys]
            top[o] = jnp.maximum(top[o], part)

    for q in range(QUESTIONS):
        top[q] = per_head(top[q], PL, jnp.max, masked_value)

    for slot in range(slots):
        o = owner_ref[slot]
        e = jnp.exp(score[slot] - top[o])
        score[slot] = e
        total[o] = total[o] + e
        dots[o] = dots[o] + e * product[slot]

    for q in range(QUESTIONS):
        t = per_head(total[q], PL, jnp.sum, 0.0)
        d = per_head(dots[q], PL, jnp.sum, 0.0)
        total[q] = t
        corr[q] = two_parts(jnp.where(t > 0.0, d / jnp.where(t > 0.0, t, 1.0), 0.0))
    corr[QUESTIONS] = jnp.zeros_like(corr[QUESTIONS])

    for slot in range(slots):
        o = owner_ref[slot]
        e = score[slot]
        g = e * (product[slot] - corr[o])
        both = jnp.concatenate([e, g], axis=0).astype(bf16)
        acc_v[o] = acc_v[o] + jnp.dot(both[:TGT], vblk[slot], preferred_element_type=f32)
        acc_k[o] = acc_k[o] + jnp.dot(both, kblk[slot], preferred_element_type=f32)

    segment = lax.broadcasted_iota(jnp.int32, (PACKED, keys), 1) % PL
    for block in range(QUESTIONS // 2):
        extras = []
        for side in range(2):
            q = 2 * block + side
            sums = jnp.concatenate([acc_v[q], acc_k[q, TGT:, :], acc_k[q, :TGT, :]], axis=1).astype(bf16)
            for n in range(sums.shape[1] // keys):
                low = block * CHUNK + (2 * n + side) * TGT
                out_ref[low : low + TGT, :] = sums[:, n * keys : (n + 1) * keys]
            extras.append(pack(top[q], total[q], corr[q]))
        quarters = [extra[low : low + PACKED] for extra in extras for low in range(0, TGT, PACKED)]
        packed = quarters[0]
        for n in range(1, len(quarters)):
            packed = jnp.where(segment // LANES == n, pltpu.roll(quarters[n], n * LANES, 1), packed)
        out_ref[(block + 1) * CHUNK - PACKED : (block + 1) * CHUNK, :] = packed.astype(bf16)


def spread(extra, cols):
    keys = extra.shape[1]
    heads = keys // PL
    lane = lax.broadcasted_iota(jnp.int32, (keys, 3 * cols), 0)
    spot = lax.broadcasted_iota(jnp.int32, (keys, 3 * cols), 1)
    pick = (lane // PL == (spot % cols) // (cols // heads)) & ((lane % PL) // PARTS == spot // cols)
    pick = pick & (lane % PL < LANES)
    wide = jnp.dot(extra, pick.astype(f32).astype(bf16), preferred_element_type=f32)
    return [wide[:, n * cols : (n + 1) * cols] for n in range(3)]


def pack(top, total, corr):
    part = lax.broadcasted_iota(jnp.int32, top.shape, 1) % PL
    out = jnp.zeros_like(top)
    for n, piece in enumerate(split_parts(top) + split_parts(total) + split_parts(corr, 2)):
        out = jnp.where(part == n, piece, out)
    return out


def merge(extra, cols, rows):
    top, total, corr = [x.reshape(-1, rows, cols) for x in spread(extra, cols)]
    high = jnp.max(top, axis=0)
    scale = jnp.exp(top - high[None])
    sums = jnp.sum(scale * total, axis=0)
    dots = jnp.sum(scale * total * corr, axis=0)
    mean = two_parts(jnp.where(sums > 0.0, dots / jnp.where(sums > 0.0, sums, 1.0), 0.0))
    return scale, corr, high, sums, mean


def merge_kernel(r_ref, out_ref):
    rows = out_ref.shape[0]
    keys = r_ref.shape[1]
    cols = (out_ref.shape[1] - keys) // 3
    starts = range(0, r_ref.shape[0], CHUNK)
    extras = []
    for start in starts:
        packed = r_ref[start + CHUNK - PACKED : start + CHUNK, :]
        extras.append(packed)
        for n in range(1, rows // PACKED):
            extras.append(pltpu.roll(packed.astype(f32), keys - n * LANES, 1).astype(bf16))
    extra = jnp.concatenate(extras, axis=0)

    def read(n):
        each = []
        for start in starts:
            lows = [start + (n * cols // keys + part) * rows for part in range(cols // keys)]
            each.append(jnp.concatenate([r_ref[low : low + rows, :].astype(f32) for low in lows], axis=1))
        return jnp.stack(each)

    scale, corr, _, _, mean = merge(extra, cols, rows)
    out_ref[:, 0:cols] = jnp.sum(scale * read(0), axis=0).astype(bf16)
    low = scale * read(2)
    grad = jnp.sum(scale * read(1) + (corr - mean[None]) * low, axis=0)
    out_ref[:, cols : 2 * cols] = grad.astype(bf16)
    out_ref[:, 2 * cols : 3 * cols] = jnp.sum(low, axis=0).astype(bf16)
    out_ref[:, 3 * cols :] = pack(*merge(extra, keys, rows)[2:]).astype(bf16)


def final_kernel(r_ref, c_ref, out_ref):
    rows, cols = c_ref.shape
    scale, own, _, total, _ = merge(r_ref[:, 3 * cols :], cols, rows)

    def read(n):
        return r_ref[:, n * cols : (n + 1) * cols].astype(f32).reshape(-1, rows, cols)

    summed = jnp.sum(scale * read(0), axis=0)
    attended = (summed / total).astype(bf16).astype(f32)
    corr = per_head(c_ref[...] * attended, HDIM, jnp.sum, 0.0)
    grad = jnp.sum(scale * (read(1) + (own - corr[None]) * read(2)), axis=0) / total
    both = jnp.concatenate([attended, grad], axis=1)
    two = jnp.concatenate([both, both], axis=0).astype(bf16)
    for n in range(out_ref.shape[0] // (2 * rows)):
        out_ref[2 * rows * n : 2 * rows * (n + 1), :] = two


def swap(block):
    return lax.ppermute(block, "rep", [(0, 1), (1, 0)])


def block_numbers():
    n = lax.axis_size("pb")
    pb, rep = lax.axis_index("pb"), lax.axis_index("rep")
    step = 1 - 2 * rep
    own = [(pb + shift) % n for shift in (0, n - step, n + step, 2)]
    other = [(pb + shift) % n for shift in (0, n + step, n - step, 2)]
    numbers = [number for pair in zip(own, other) for number in (pair[0] * 2 + rep, pair[1] * 2 + 1 - rep)]
    place = lax.axis_index("psg")
    first, second = place // SIDE, place % SIDE
    row_block = jnp.where(rep == 0, second, first) * SIDE + jnp.where(rep == 0, first, second)
    return jnp.stack(numbers + [row_block]).astype(jnp.int32)


def along(block, way):
    n = lax.axis_size("pb")
    pairs = []
    for chip in range(n):
        pairs.append((chip * 2, (chip + way) % n * 2))
        pairs.append((chip * 2 + 1, (chip - way) % n * 2 + 1))
    return lax.ppermute(block, ("pb", "rep"), pairs)


AXES = ("psg", "pb", "rep")


def line_groups(mesh_shape, turn):
    side = SIDE
    assert side * side == mesh_shape[0]
    ids = np.arange(np.prod(mesh_shape)).reshape((side, side) + tuple(mesh_shape[1:]))
    groups = []
    for core in range(mesh_shape[2]):
        along = (core + turn + 1) % 2
        lines = np.moveaxis(ids[:, :, :, core], along, -1)
        groups += lines.reshape(-1, side).tolist()
    return groups


def plane_groups(mesh_shape):
    ids = np.arange(np.prod(mesh_shape)).reshape((SIDE, SIDE) + tuple(mesh_shape[1:]))
    groups = []
    for core in range(mesh_shape[2]):
        plane = ids[:, :, :, core]
        plane = np.moveaxis(plane, 2, 0) if core else np.transpose(plane, (2, 1, 0))
        groups += plane.reshape(mesh_shape[1], -1).tolist()
    return groups


def exchange(x, groups):
    return lax.all_to_all(x, AXES, 0, 0, axis_index_groups=groups, tiled=True)


def body(queries, prefixes, owner, key_weight, value_weight, cotangent):
    slots, vectors, features = prefixes.shape
    rows, cols = queries.shape
    heads = cols // HDIM
    keys = heads * PL
    devices = lax.axis_size("psg")
    assert rows == ROWS_EACH * devices

    passages = prefixes.reshape(slots * vectors, features)
    smem = pl.BlockSpec(memory_space=pltpu.SMEM)
    vmem = pl.BlockSpec(memory_space=pltpu.VMEM)
    small = pltpu.CompilerParams(vmem_limit_bytes=16 * 1024 * 1024)
    count = slots * vectors
    sums = jax.ShapeDtypeStruct((count, 2 * cols), f32)
    rest_rows = jax.ShapeDtypeStruct((key_weight.shape[0] - features, cols), bf16)
    block = block_numbers()

    ahead = along(passages, 1)
    keys_sum, rest_key = pl.pallas_call(
        own_kernel,
        out_shape=(jax.ShapeDtypeStruct((count, cols), f32), rest_rows),
        in_specs=[smem] + [vmem] * 2,
        out_specs=(vmem, vmem),
        compiler_params=small,
        name="own_keys",
    )(block, passages, key_weight)
    held, keys_sum, rest_key = lax.optimization_barrier((passages, keys_sum, rest_key))
    behind, other = along(held, -1), swap(held)
    far = along(ahead, 1)
    ahead_other = swap(ahead)
    early = [other, ahead]
    projected, rest_value, own_cotangent = pl.pallas_call(
        early_kernel,
        out_shape=(sums, rest_rows, jax.ShapeDtypeStruct((ROWS_EACH, cols), f32)),
        in_specs=[smem] + [vmem] * (5 + len(early)),
        out_specs=(vmem, vmem, vmem),
        compiler_params=small,
        name="early_blocks",
    )(block, keys_sum, rest_key, held, value_weight, cotangent, *early)
    far, ahead_other, projected, rest_value = lax.optimization_barrier((far, ahead_other, projected, rest_value))
    late = [ahead_other, behind, swap(behind), far]
    far = swap(far)
    projected = pl.pallas_call(
        lambda *refs: late_kernel(len(early) * features, *refs),
        out_shape=sums,
        in_specs=[vmem] * (3 + len(late)),
        out_specs=vmem,
        compiler_params=small,
        name="late_blocks",
    )(projected, rest_key, rest_value, *late)
    payload = pl.pallas_call(
        local_kernel,
        out_shape=jax.ShapeDtypeStruct((SIDE * CHUNK, keys), bf16),
        in_specs=[smem] + [vmem] * 6,
        out_specs=vmem,
        scratch_shapes=[
            pltpu.VMEM((slots, keys, cols), bf16),
            pltpu.VMEM((slots, keys, cols), bf16),
            pltpu.VMEM((slots, TGT, keys), f32),
            pltpu.VMEM((slots, TGT, keys), f32),
            pltpu.VMEM((QUESTIONS + 1, TGT, keys), f32),
            pltpu.VMEM((QUESTIONS + 1, TGT, keys), f32),
            pltpu.VMEM((QUESTIONS + 1, TGT, keys), f32),
            pltpu.VMEM((QUESTIONS + 1, TGT, keys), f32),
            pltpu.VMEM((QUESTIONS + 1, TGT, cols), f32),
            pltpu.VMEM((QUESTIONS + 1, 2 * TGT, cols), f32),
        ],
        compiler_params=pltpu.CompilerParams(vmem_limit_bytes=24 * 1024 * 1024),
        name="local_sums",
    )(owner, projected, far, rest_key, rest_value, queries, cotangent)

    shape = tuple(lax.axis_size(name) for name in AXES)
    first_lines, second_lines = line_groups(shape, 0), line_groups(shape, 1)
    merged = pl.pallas_call(
        merge_kernel,
        out_shape=jax.ShapeDtypeStruct((rows // SIDE, 3 * cols + keys), bf16),
        in_specs=[vmem],
        out_specs=vmem,
        compiler_params=pltpu.CompilerParams(vmem_limit_bytes=24 * 1024 * 1024),
        name="line_sums",
    )(exchange(payload, first_lines))
    received = exchange(merged, second_lines)
    finished = pl.pallas_call(
        final_kernel,
        out_shape=jax.ShapeDtypeStruct((rows, 2 * cols), bf16),
        in_specs=[vmem, vmem],
        out_specs=vmem,
        compiler_params=pltpu.CompilerParams(vmem_limit_bytes=24 * 1024 * 1024),
        name="final_sums",
    )(received, own_cotangent)
    outputs = exchange(finished, plane_groups(shape))
    return outputs[:, :cols], outputs[:, cols:]


def solution(mesh):
    placed = (
        P(None, ("pb", "rep")),
        P("psg", None, ("pb", "rep")),
        P("psg"),
        P(None, ("pb", "rep")),
        P(None, ("pb", "rep")),
        P(None, ("pb", "rep")),
    )
    return jax.shard_map(
        body,
        mesh=mesh,
        in_specs=placed,
        out_specs=(P(None, ("pb", "rep")), P(None, ("pb", "rep"))),
        check_vma=False,
    )
```

```python
import jax
import jax.numpy as jnp
import numpy as np
from jax import lax
from jax.experimental import pallas as pl
from jax.experimental.pallas import tpu as pltpu
from jax.sharding import PartitionSpec as P

HDIM = 64
TGT = 32
PL = 32
QUESTIONS = 16
PARTS = 3
SIDE = 8
LANES = 8
PACKED = 16
CHUNK = 400
ROWS_EACH = 8

masked_value = -1e30

f32 = jnp.float32
bf16 = jnp.bfloat16
NT = (((1,), (1,)), ((), ()))


def split_parts(x, count=PARTS):
    parts = []
    for _ in range(count):
        parts.append(x.astype(bf16).astype(f32))
        x = x - parts[-1]
    return parts


def two_parts(x):
    first, second = split_parts(x, 2)
    return first + second


def per_head(x, width, reduce, fill):
    lane_head = lax.broadcasted_iota(jnp.int32, x.shape, x.ndim - 1) // width
    out = jnp.zeros_like(x)
    for head in range(x.shape[-1] // width):
        one = reduce(jnp.where(lane_head == head, x, fill), axis=-1, keepdims=True)
        out = jnp.where(lane_head == head, one, out)
    return out


def block_rows(block_ref, n, wide):
    return pl.ds(pl.multiple_of(block_ref[n] * wide, wide), wide)


def reorder(block_ref, w_ref, rest_ref, wide):
    for n in range(1, w_ref.shape[0] // wide):
        rest_ref[(n - 1) * wide : n * wide, :] = w_ref[block_rows(block_ref, n, wide), :]


def own_kernel(block_ref, x_ref, wk_ref, keys_ref, rest_ref):
    wide = x_ref.shape[1]
    weight = wk_ref[block_rows(block_ref, 0, wide), :]
    keys_ref[...] = jnp.dot(x_ref[...], weight, preferred_element_type=f32)
    reorder(block_ref, wk_ref, rest_ref, wide)


def early_kernel(block_ref, keys_ref, rest_key_ref, x_ref, wv_ref, c_ref, *refs):
    x_refs, out_ref, rest_ref, own_ref = refs[:-3], refs[-3], refs[-2], refs[-1]
    place = block_ref[block_ref.shape[0] - 1]
    count = own_ref.shape[0]
    pair = c_ref[pl.ds(pl.multiple_of((place >> 1) * 2 * count, 2 * count), 2 * count), :].astype(f32)
    own_ref[...] = jnp.where((place & 1) == 1, pair[count:], pair[:count])
    wide = x_ref.shape[1]
    cols = wv_ref.shape[1]
    depth = len(x_refs) * wide
    reorder(block_ref, wv_ref, rest_ref, wide)
    chunk = 512
    for low in range(0, x_ref.shape[0], chunk):
        at = slice(low, low + chunk)
        rows = jnp.concatenate([x[at, :] for x in x_refs], axis=1)
        out_ref[at, :cols] = keys_ref[at, :] + jnp.dot(rows, rest_key_ref[:depth, :], preferred_element_type=f32)
        rows = jnp.concatenate([rows, x_ref[at, :]], axis=1)
        weight = jnp.concatenate([rest_ref[:depth, :], wv_ref[block_rows(block_ref, 0, wide), :]], axis=0)
        out_ref[at, cols:] = jnp.dot(rows, weight, preferred_element_type=f32)


def late_kernel(first, acc_ref, rest_key_ref, rest_value_ref, *refs):
    x_refs, out_ref = refs[:-1], refs[-1]
    at = slice(first, first + len(x_refs) * x_refs[0].shape[1])
    weight = jnp.concatenate([rest_key_ref[at, :], rest_value_ref[at, :]], axis=1)
    chunk = 512
    for low in range(0, acc_ref.shape[0], chunk):
        rows = jnp.concatenate([x[low : low + chunk, :] for x in x_refs], axis=1)
        out_ref[low : low + chunk, :] = acc_ref[low : low + chunk, :] + jnp.dot(
            rows, weight, preferred_element_type=f32
        )


def local_kernel(owner_ref, acc_ref, *refs):
    (far_ref, rest_key_ref, rest_value_ref, q_ref, c_ref, out_ref, kblk, vblk, score, product, top, total, dots, corr, acc_v, acc_k) = refs
    slots = owner_ref.shape[0]
    cols = q_ref.shape[1]
    heads = cols // HDIM
    keys = heads * PL

    top[...] = jnp.full_like(top, masked_value)
    total[...] = jnp.zeros_like(total)
    dots[...] = jnp.zeros_like(dots)
    acc_v[...] = jnp.zeros_like(acc_v)
    acc_k[...] = jnp.zeros_like(acc_k)

    on_diagonal = (
        lax.broadcasted_iota(jnp.int32, (keys, cols), 0) // PL
        == lax.broadcasted_iota(jnp.int32, (keys, cols), 1) // HDIM
    ).astype(f32).astype(bf16)

    weight = jnp.concatenate([ref[-far_ref.shape[1] :, :] for ref in (rest_key_ref, rest_value_ref)], axis=1)
    rows = far_ref[...]
    projected = acc_ref[...] + jnp.dot(rows, weight, preferred_element_type=f32)
    projected = projected.astype(bf16)
    for slot in range(slots):
        own = projected[slot * PL : (slot + 1) * PL]
        kb = jnp.concatenate([own[:, :cols]] * heads, axis=0) * on_diagonal
        vb = jnp.concatenate([own[:, cols:]] * heads, axis=0) * on_diagonal
        kblk[slot] = kb
        vblk[slot] = vb
    for slot in range(0, slots, 2):
        owners = [owner_ref[slot + n] for n in range(2)]
        ats = [pl.ds(pl.multiple_of(jnp.minimum(o, QUESTIONS - 1) * TGT, TGT), TGT) for o in owners]

        def both_ways(rows_ref, block_ref):
            rows = jnp.concatenate([rows_ref[at, :] for at in ats], axis=0)
            blocks = jnp.concatenate([block_ref[slot], block_ref[slot + 1]], axis=0)
            return lax.dot_general(rows, blocks, NT, preferred_element_type=f32)

        s = both_ways(q_ref, kblk)
        p = both_ways(c_ref, vblk)
        for n, o in enumerate(owners):
            part = s[n * TGT : (n + 1) * TGT, n * keys : (n + 1) * keys]
            score[slot + n] = part
            product[slot + n] = p[n * TGT : (n + 1) * TGT, n * keys : (n + 1) * keys]
            top[o] = jnp.maximum(top[o], part)

    for q in range(QUESTIONS):
        top[q] = per_head(top[q], PL, jnp.max, masked_value)

    for slot in range(slots):
        o = owner_ref[slot]
        e = jnp.exp(score[slot] - top[o])
        score[slot] = e
        total[o] = total[o] + e
        dots[o] = dots[o] + e * product[slot]

    same_head = (
        lax.broadcasted_iota(jnp.int32, (PARTS * keys, keys), 0) % keys // PL
        == lax.broadcasted_iota(jnp.int32, (PARTS * keys, keys), 1) // PL
    ).astype(f32).astype(bf16)

    def head_sums(ref):
        parts = jnp.concatenate(split_parts(ref[:QUESTIONS].reshape(QUESTIONS * TGT, keys)), axis=1)
        return jnp.dot(parts.astype(bf16), same_head, preferred_element_type=f32).reshape(QUESTIONS, TGT, keys)

    t = head_sums(total)
    d = head_sums(dots)
    total[:QUESTIONS] = t
    corr[:QUESTIONS] = two_parts(jnp.where(t > 0.0, d / jnp.where(t > 0.0, t, 1.0), 0.0))
    corr[QUESTIONS] = jnp.zeros_like(corr[QUESTIONS])

    for slot in range(slots):
        o = owner_ref[slot]
        e = score[slot]
        g = e * (product[slot] - corr[o])
        both = jnp.concatenate([e, g], axis=0).astype(bf16)
        acc_v[o] = acc_v[o] + jnp.dot(both[:TGT], vblk[slot], preferred_element_type=f32)
        acc_k[o] = acc_k[o] + jnp.dot(both, kblk[slot], preferred_element_type=f32)

    segment = lax.broadcasted_iota(jnp.int32, (PACKED, keys), 1) % PL
    for block in range(QUESTIONS // 2):
        extras = []
        for side in range(2):
            q = 2 * block + side
            sums = jnp.concatenate([acc_v[q], acc_k[q, TGT:, :], acc_k[q, :TGT, :]], axis=1).astype(bf16)
            for n in range(sums.shape[1] // keys):
                low = block * CHUNK + (2 * n + side) * TGT
                out_ref[low : low + TGT, :] = sums[:, n * keys : (n + 1) * keys]
            extras.append(pack(top[q], total[q], corr[q]))
        quarters = [extra[low : low + PACKED] for extra in extras for low in range(0, TGT, PACKED)]
        packed = quarters[0]
        for n in range(1, len(quarters)):
            packed = jnp.where(segment // LANES == n, pltpu.roll(quarters[n], n * LANES, 1), packed)
        out_ref[(block + 1) * CHUNK - PACKED : (block + 1) * CHUNK, :] = packed.astype(bf16)


def spread(extra, cols):
    keys = extra.shape[1]
    heads = keys // PL
    lane = lax.broadcasted_iota(jnp.int32, (keys, 3 * cols), 0)
    spot = lax.broadcasted_iota(jnp.int32, (keys, 3 * cols), 1)
    pick = (lane // PL == (spot % cols) // (cols // heads)) & ((lane % PL) // PARTS == spot // cols)
    pick = pick & (lane % PL < LANES)
    wide = jnp.dot(extra, pick.astype(f32).astype(bf16), preferred_element_type=f32)
    return [wide[:, n * cols : (n + 1) * cols] for n in range(3)]


def pack(top, total, corr):
    part = lax.broadcasted_iota(jnp.int32, top.shape, 1) % PL
    out = jnp.zeros_like(top)
    for n, piece in enumerate(split_parts(top) + split_parts(total) + split_parts(corr, 2)):
        out = jnp.where(part == n, piece, out)
    return out


def merge(extra, cols, rows):
    top, total, corr = [x.reshape(-1, rows, cols) for x in spread(extra, cols)]
    high = jnp.max(top, axis=0)
    scale = jnp.exp(top - high[None])
    sums = jnp.sum(scale * total, axis=0)
    dots = jnp.sum(scale * total * corr, axis=0)
    mean = two_parts(jnp.where(sums > 0.0, dots / jnp.where(sums > 0.0, sums, 1.0), 0.0))
    return scale, corr, high, sums, mean


def merge_kernel(r_ref, out_ref):
    rows = out_ref.shape[0]
    keys = r_ref.shape[1]
    cols = (out_ref.shape[1] - keys) // 3
    starts = range(0, r_ref.shape[0], CHUNK)
    extras = []
    for start in starts:
        packed = r_ref[start + CHUNK - PACKED : start + CHUNK, :]
        extras.append(packed)
        for n in range(1, rows // PACKED):
            extras.append(pltpu.roll(packed.astype(f32), keys - n * LANES, 1).astype(bf16))
    extra = jnp.concatenate(extras, axis=0)

    def read(n):
        each = []
        for start in starts:
            lows = [start + (n * cols // keys + part) * rows for part in range(cols // keys)]
            each.append(jnp.concatenate([r_ref[low : low + rows, :].astype(f32) for low in lows], axis=1))
        return jnp.stack(each)

    scale, corr, _, _, mean = merge(extra, cols, rows)
    out_ref[:, 0:cols] = jnp.sum(scale * read(0), axis=0).astype(bf16)
    low = scale * read(2)
    grad = jnp.sum(scale * read(1) + (corr - mean[None]) * low, axis=0)
    out_ref[:, cols : 2 * cols] = grad.astype(bf16)
    out_ref[:, 2 * cols : 3 * cols] = jnp.sum(low, axis=0).astype(bf16)
    out_ref[:, 3 * cols :] = pack(*merge(extra, keys, rows)[2:]).astype(bf16)


def final_kernel(r_ref, c_ref, out_ref):
    rows, cols = c_ref.shape
    scale, own, _, total, _ = merge(r_ref[:, 3 * cols :], cols, rows)

    def read(n):
        return r_ref[:, n * cols : (n + 1) * cols].astype(f32).reshape(-1, rows, cols)

    summed = jnp.sum(scale * read(0), axis=0)
    attended = (summed / total).astype(bf16).astype(f32)
    corr = per_head(c_ref[...] * attended, HDIM, jnp.sum, 0.0)
    grad = jnp.sum(scale * (read(1) + (own - corr[None]) * read(2)), axis=0) / total
    both = jnp.concatenate([attended, grad], axis=1)
    two = jnp.concatenate([both, both], axis=0).astype(bf16)
    for n in range(out_ref.shape[0] // (2 * rows)):
        out_ref[2 * rows * n : 2 * rows * (n + 1), :] = two


def swap(block):
    return lax.ppermute(block, "rep", [(0, 1), (1, 0)])


def block_numbers():
    n = lax.axis_size("pb")
    pb, rep = lax.axis_index("pb"), lax.axis_index("rep")
    step = 1 - 2 * rep
    own = [(pb + shift) % n for shift in (0, n - step, n + step, 2)]
    other = [(pb + shift) % n for shift in (0, n + step, n - step, 2)]
    numbers = [number for pair in zip(own, other) for number in (pair[0] * 2 + rep, pair[1] * 2 + 1 - rep)]
    place = lax.axis_index("psg")
    first, second = place // SIDE, place % SIDE
    row_block = jnp.where(rep == 0, second, first) * SIDE + jnp.where(rep == 0, first, second)
    return jnp.stack(numbers + [row_block]).astype(jnp.int32)


def along(block, way):
    n = lax.axis_size("pb")
    pairs = []
    for chip in range(n):
        pairs.append((chip * 2, (chip + way) % n * 2))
        pairs.append((chip * 2 + 1, (chip - way) % n * 2 + 1))
    return lax.ppermute(block, ("pb", "rep"), pairs)


AXES = ("psg", "pb", "rep")


def line_groups(mesh_shape, turn):
    side = SIDE
    assert side * side == mesh_shape[0]
    ids = np.arange(np.prod(mesh_shape)).reshape((side, side) + tuple(mesh_shape[1:]))
    groups = []
    for core in range(mesh_shape[2]):
        along = (core + turn + 1) % 2
        lines = np.moveaxis(ids[:, :, :, core], along, -1)
        groups += lines.reshape(-1, side).tolist()
    return groups


def plane_groups(mesh_shape):
    ids = np.arange(np.prod(mesh_shape)).reshape((SIDE, SIDE) + tuple(mesh_shape[1:]))
    groups = []
    for core in range(mesh_shape[2]):
        plane = ids[:, :, :, core]
        plane = np.moveaxis(plane, 2, 0) if core else np.transpose(plane, (2, 1, 0))
        groups += plane.reshape(mesh_shape[1], -1).tolist()
    return groups


def exchange(x, groups):
    return lax.all_to_all(x, AXES, 0, 0, axis_index_groups=groups, tiled=True)


def body(queries, prefixes, owner, key_weight, value_weight, cotangent):
    slots, vectors, features = prefixes.shape
    rows, cols = queries.shape
    heads = cols // HDIM
    keys = heads * PL
    devices = lax.axis_size("psg")
    assert rows == ROWS_EACH * devices

    passages = prefixes.reshape(slots * vectors, features)
    smem = pl.BlockSpec(memory_space=pltpu.SMEM)
    vmem = pl.BlockSpec(memory_space=pltpu.VMEM)
    small = pltpu.CompilerParams(vmem_limit_bytes=16 * 1024 * 1024)
    count = slots * vectors
    sums = jax.ShapeDtypeStruct((count, 2 * cols), f32)
    rest_rows = jax.ShapeDtypeStruct((key_weight.shape[0] - features, cols), bf16)
    block = block_numbers()

    ahead = along(passages, 1)
    keys_sum, rest_key = pl.pallas_call(
        own_kernel,
        out_shape=(jax.ShapeDtypeStruct((count, cols), f32), rest_rows),
        in_specs=[smem] + [vmem] * 2,
        out_specs=(vmem, vmem),
        compiler_params=small,
        name="own_keys",
    )(block, passages, key_weight)
    held, keys_sum, rest_key = lax.optimization_barrier((passages, keys_sum, rest_key))
    behind, other = along(held, -1), swap(held)
    far = along(ahead, 1)
    ahead_other = swap(ahead)
    early = [other, ahead]
    projected, rest_value, own_cotangent = pl.pallas_call(
        early_kernel,
        out_shape=(sums, rest_rows, jax.ShapeDtypeStruct((ROWS_EACH, cols), f32)),
        in_specs=[smem] + [vmem] * (5 + len(early)),
        out_specs=(vmem, vmem, vmem),
        compiler_params=small,
        name="early_blocks",
    )(block, keys_sum, rest_key, held, value_weight, cotangent, *early)
    far, ahead_other, projected, rest_value = lax.optimization_barrier((far, ahead_other, projected, rest_value))
    late = [ahead_other, behind, swap(behind), far]
    far = swap(far)
    projected = pl.pallas_call(
        lambda *refs: late_kernel(len(early) * features, *refs),
        out_shape=sums,
        in_specs=[vmem] * (3 + len(late)),
        out_specs=vmem,
        compiler_params=small,
        name="late_blocks",
    )(projected, rest_key, rest_value, *late)
    payload = pl.pallas_call(
        local_kernel,
        out_shape=jax.ShapeDtypeStruct((SIDE * CHUNK, keys), bf16),
        in_specs=[smem] + [vmem] * 6,
        out_specs=vmem,
        scratch_shapes=[
            pltpu.VMEM((slots, keys, cols), bf16),
            pltpu.VMEM((slots, keys, cols), bf16),
            pltpu.VMEM((slots, TGT, keys), f32),
            pltpu.VMEM((slots, TGT, keys), f32),
            pltpu.VMEM((QUESTIONS + 1, TGT, keys), f32),
            pltpu.VMEM((QUESTIONS + 1, TGT, keys), f32),
            pltpu.VMEM((QUESTIONS + 1, TGT, keys), f32),
            pltpu.VMEM((QUESTIONS + 1, TGT, keys), f32),
            pltpu.VMEM((QUESTIONS + 1, TGT, cols), f32),
            pltpu.VMEM((QUESTIONS + 1, 2 * TGT, cols), f32),
        ],
        compiler_params=pltpu.CompilerParams(vmem_limit_bytes=24 * 1024 * 1024),
        name="local_sums",
    )(owner, projected, far, rest_key, rest_value, queries, cotangent)

    shape = tuple(lax.axis_size(name) for name in AXES)
    first_lines, second_lines = line_groups(shape, 0), line_groups(shape, 1)
    merged = pl.pallas_call(
        merge_kernel,
        out_shape=jax.ShapeDtypeStruct((rows // SIDE, 3 * cols + keys), bf16),
        in_specs=[vmem],
        out_specs=vmem,
        compiler_params=pltpu.CompilerParams(vmem_limit_bytes=24 * 1024 * 1024),
        name="line_sums",
    )(exchange(payload, first_lines))
    received = exchange(merged, second_lines)
    finished = pl.pallas_call(
        final_kernel,
        out_shape=jax.ShapeDtypeStruct((rows, 2 * cols), bf16),
        in_specs=[vmem, vmem],
        out_specs=vmem,
        compiler_params=pltpu.CompilerParams(vmem_limit_bytes=24 * 1024 * 1024),
        name="final_sums",
    )(received, own_cotangent)
    outputs = exchange(finished, plane_groups(shape))
    return outputs[:, :cols], outputs[:, cols:]


def solution(mesh):
    placed = (
        P(None, ("pb", "rep")),
        P("psg", None, ("pb", "rep")),
        P("psg"),
        P(None, ("pb", "rep")),
        P(None, ("pb", "rep")),
        P(None, ("pb", "rep")),
    )
    return jax.shard_map(
        body,
        mesh=mesh,
        in_specs=placed,
        out_specs=(P(None, ("pb", "rep")), P(None, ("pb", "rep"))),
        check_vma=False,
    )
```
